512 devices in a mesh: gx: 16 (over y, z_hi, core), gy: 8 (over z_lo), vert: 4 (over x).
Axes of the slice: x: 4, y: 4, z: 16 (z_hi: 2, z_lo: 8; z = z_hi * 8 + z_lo), core: 2. Of those that a mesh axis runs over, the one named last changes fastest.
Arguments:
- distribution: float32 [64, 16, 13824], P('gx', 'gy', 'vert'), may hold values from 0.1 to 1
- cell_types: int32 [64, 16], P('gx', 'gy'), may hold values from 0 to 2, as said below
- wall_state: float32 [13824], P('vert'), may hold values from 0.1 to 1
- inflow_state: float32 [13824], P('vert'), may hold values from 0.05 to 1.2
- upwind_side: int32 [2, 13824], P(None, 'vert'), may hold values from 0 to 1
- gain_left: float32 [4, 24, 24, 24], replicated, may hold values from -2 to 2
- gain_right: float32 [4, 24, 24, 24], replicated, may hold values from -2 to 2
- loss_table: float32 [24, 24, 24], replicated, may hold values from 0.5 to 1.5
Outputs:
- advanced: float32 [64, 16, 13824], P('gx', 'gy', 'vert')
The draws below stay inside these ranges and needn't reach their ends.
Inputs may be any that keep to these rules, and one draw needn't show every extreme that they name: `cell_types`: row y = 0 is wall; along every streamwise position x the cells from some wall-normal index up to y = 15 are wall (between 1 and 5 rows, varying with x); the gas cells at x = 0 are inflow; all other cells are gas.
All inputs are finite; a program needn't handle non-finite values.
Results may differ from the reference program's by a relative error of at most 0.0001.
Values sent between devices are 32-bit elements; how exact they have to be, the bound alone decides.
A program may use at most 64 MiB of HBM per device.

```python
import math
import jax
import jax.numpy as jnp
from jax import lax

V = 24
RANK = 4
NX = 64
NY = 16
NV = 13824


def draw_cell_types(key, part):
    key = jax.random.fold_in(key, 7)
    deepest = max(2, NY // 3)
    depth = jax.random.randint(key, (NX, 1), 1, deepest + 1)
    wall_index = jnp.arange(NY, dtype=jnp.int32)[None, :]
    stream_index = jnp.arange(NX, dtype=jnp.int32)[:, None]
    walls = (wall_index == 0) | (wall_index >= NY - depth)
    inflow = (stream_index == 0) & jnp.logical_not(walls)
    return jnp.where(walls, 1, jnp.where(inflow, 2, 0)).astype(jnp.int32)


def touch_ends(drawn, key, least, top_value):
    place = [jax.random.randint(jax.random.fold_in(key, axis), (), 0, length) for axis, length in enumerate(drawn.shape)]
    main_axis = drawn.shape.index(max(drawn.shape))
    neighbour = place[:main_axis] + [(place[main_axis] + 1) % drawn.shape[main_axis]] + place[main_axis + 1:]
    return drawn.at[tuple(place)].set(least).at[tuple(neighbour)].set(top_value)


def block_levels(rng, extent, shards, low, top_value):
    factor_of = 1.0
    for position, blocks in shards:
        draws = jax.random.uniform(jax.random.fold_in(jax.random.fold_in(rng, 6), position), (blocks,), jnp.float32, low / len(shards), top_value / len(shards))
        factor_of = factor_of * jnp.repeat(jnp.exp(draws), extent[position] // blocks).reshape((-1,) + (1,) * (len(extent) - 1 - position))
    return factor_of


def setup_inputs(seed: int = 0) -> dict:
    keys = jax.random.split(jax.random.key(seed), 9)
    distribution = jnp.clip(jnp.exp(math.log(1.0) - 2.3025851 * jax.random.uniform(keys[0], (NX, NY, NV), jnp.float32) ** block_levels(keys[0], (NX, NY, NV), ((0, 16), (1, 8), (2, 4)), -0.2, 0.2)), 0.1, 1.0)
    cell_types = draw_cell_types(jax.random.fold_in(keys[8], 71), 0)
    wall_state = jnp.clip(jnp.exp(math.log(1.0) - 2.3025851 * jax.random.uniform(keys[2], (NV,), jnp.float32) ** block_levels(keys[2], (NV,), ((0, 4),), -0.2, 0.2)), 0.1, 1.0)
    inflow_state = jnp.clip(jnp.exp(math.log(1.2) - 3.1780539 * jax.random.uniform(keys[3], (NV,), jnp.float32) ** block_levels(keys[3], (NV,), ((0, 4),), -0.2, 0.2)), 0.05, 1.2)
    upwind_side = touch_ends(jax.random.randint(keys[4], (2, NV), 0, 2), jax.random.fold_in(keys[4], 1), 0, 1).astype(jnp.int32)
    gain_left = jnp.clip(jax.random.uniform(keys[5], (RANK, V, V, V), jnp.float32, -2.0, 2.0), -2.0, 2.0)
    gain_right = jnp.clip(jax.random.uniform(keys[6], (RANK, V, V, V), jnp.float32, -2.0, 2.0), -2.0, 2.0)
    loss_table = jnp.clip(jax.random.uniform(keys[7], (V, V, V), jnp.float32, 0.5, 1.5), 0.5, 1.5)
    return {"distribution": distribution, "cell_types": cell_types, "wall_state": wall_state, "inflow_state": inflow_state, "upwind_side": upwind_side, "gain_left": gain_left, "gain_right": gain_right, "loss_table": loss_table}


collision_step = 0.25
courant = 0.45


def collide(cell_block, gain_left, gain_right, loss_table):
    spectrum = jnp.fft.fftn(cell_block, axes=(1, 2, 3))

    def filtered(multiplier):
        return jnp.real(jnp.fft.ifftn(multiplier[None] * spectrum, axes=(1, 2, 3)))

    gain_sum = filtered(gain_left[0]) * filtered(gain_right[0])
    for rank_index in range(1, RANK):
        gain_sum = gain_sum + filtered(gain_left[rank_index]) * filtered(gain_right[rank_index])
    loss_rate = filtered(loss_table)
    return cell_block + collision_step * (gain_sum - cell_block * loss_rate)


def reference(distribution, cell_types, wall_state, inflow_state, upwind_side, gain_left, gain_right, loss_table):
    kind_column = cell_types[:, :, None]
    boundary_state = jnp.where(kind_column == 1, wall_state[None, None, :],
                               jnp.where(kind_column == 2, inflow_state[None, None, :], distribution))

    def per_row(row_cells):
        return collide(row_cells.reshape(NY, V, V, V), gain_left, gain_right, loss_table).reshape(NY, V ** 3)

    collided = lax.map(per_row, boundary_state)
    padded = jnp.pad(collided, ((1, 1), (1, 1), (0, 0)))
    centre = padded[1:-1, 1:-1]
    velocity_index = jnp.arange(V ** 3, dtype=jnp.int32)
    plane_index = velocity_index // (V * V)
    column_index = (velocity_index // V) % V
    courant_x = courant * jnp.abs(2 * plane_index - (V - 1)).astype(jnp.float32) / (V - 1)
    courant_y = courant * jnp.abs(2 * column_index - (V - 1)).astype(jnp.float32) / (V - 1)
    upstream_x = jnp.where(upwind_side[0] == 1, padded[:-2, 1:-1], padded[2:, 1:-1])
    upstream_y = jnp.where(upwind_side[1] == 1, padded[1:-1, :-2], padded[1:-1, 2:])
    return centre - courant_x * (centre - upstream_x) - courant_y * (centre - upstream_y)
```

```python
import functools

import jax
import jax.numpy as jnp
import ml_dtypes
import numpy as np
from jax import lax
from jax.experimental import pallas as pl
from jax.experimental.pallas import tpu as pltpu
from jax.sharding import PartitionSpec as P

MESH = pl.DeviceIdType.MESH
F32 = jnp.float32
BF16 = jnp.bfloat16

V = 24
PLANE = V * V
HALF = V // 2
RANK = 4
TABLES = 2 * RANK + 1
GROUPS = 4
NX, NY = 4, 2
SLAB = PLANE * V // GROUPS
LANES = 128
ROWS = SLAB // LANES
BLOCK = 56
EDGE = 32
PAIRS = 3
CHUNKS = 2 * PLANE // LANES
W = 256
PACK = 5
GROUPED = 5 * LANES
SIGNS = ((1, 1), (1, -1), (-1, 1), (-1, -1))
COLLISION_STEP = 0.25
COURANT = 0.45


def split_constant(a):
    hi = a.astype(ml_dtypes.bfloat16)
    lo = (a - hi.astype(np.float64)).astype(ml_dtypes.bfloat16)
    return hi, lo


def chunked(a):
    pad = -a.shape[-1] % LANES
    a = np.pad(a, [(0, 0)] * (a.ndim - 1) + [(0, pad)])
    a = a.reshape(*a.shape[:-1], -1, LANES)
    return np.ascontiguousarray(np.moveaxis(a, -2, -3))


def stacked(a):
    hi, lo = split_constant(a)
    return chunked(np.concatenate([hi, hi, lo], axis=1))


@functools.cache
def constants():
    step = 2.0 * np.pi / V
    inner = [(a, b) for a in range(1, HALF) for b in range(1, HALF)]
    outer = [(a, b) for a in range(HALF + 1) for b in range(HALF + 1) if a % HALF == 0 or b % HALF == 0]
    points = np.array(inner + outer)
    count = len(points)
    qy, qz = points[:, 0], points[:, 1]
    natural = np.arange(PLANE)
    ny, nz = natural // V, natural % V
    trig = (np.cos, np.sin)
    classes = ((0, 0), (0, 1), (1, 0), (1, 1))

    def grid(rows_y, rows_z, cy, cz):
        by = trig[cy](step * (rows_y[:, None] * qy[None, :] % V))
        bz = trig[cz](step * (rows_z[:, None] * qz[None, :] % V))
        return by * bz

    plane_forward = np.zeros((PLANE, 4 * W))
    plane_inverse = np.zeros((4, W, W))
    weight = np.where(qy % HALF == 0, 0.5, 1.0) * np.where(qz % HALF == 0, 0.5, 1.0) / PLANE
    for c, (cy, cz) in enumerate(classes):
        plane_forward[:, c * W : c * W + count] = grid(ny, nz, cy, cz)
        plane_inverse[c, :count, :count] = weight[:, None] * grid(qy, qz, cy, cz)

    place = np.zeros((GROUPED, 4 * W))
    unplace = np.zeros((4 * W, PLANE))
    seen = set()
    for s, (sy, sz) in enumerate(SIGNS):
        for q in range(count):
            y, z = sy * qy[q] % V, sz * qz[q] % V
            place[(y // PACK) * LANES + (y % PACK) * V + z, s * W + q] = 1.0
            if (y, z) not in seen:
                seen.add((y, z))
                unplace[s * W + q, y * V + z] = 1.0

    row_of = np.zeros((2, V), dtype=int)
    for jx in range(V):
        pair, odd = jx // 2, jx % 2
        u, q = pair // PAIRS, pair % PAIRS
        for cell in range(2):
            row_of[cell, jx] = odd * V + 2 * PAIRS * u + PAIRS * cell + q
    k = np.arange(V)
    theta = step * (k[:, None] * k[None, :] % V)
    cos, sin = np.cos(theta), np.sin(theta)
    x_forward = np.zeros((2 * V, 2 * V))
    x_forward[:V, row_of[0]] = cos
    x_forward[:V, row_of[1]] = sin
    x_forward[V:, row_of[0]] = -sin
    x_forward[V:, row_of[1]] = cos
    real = np.concatenate([cos, -sin], axis=1)
    imag = np.concatenate([sin, cos], axis=1)
    x_inverse = []
    for first, second in ((real, imag), (-imag, real), (-imag, real), (-real, -imag)):
        m = np.zeros((2 * V, 2 * V))
        m[row_of[0]] = first
        m[row_of[1]] = second
        x_inverse.append(stacked(m / (2 * V)))

    reverse = np.zeros((32, 2 * V))
    for r in range(V):
        reverse[r, (V - r) % V] = 1.0
        reverse[r, V + (V - r) % V] = 1.0

    velocity = np.arange(PLANE * V)
    courant_x = COURANT * np.abs(2 * (velocity // PLANE) - (V - 1)).astype(np.float32) / (V - 1)
    courant_y = COURANT * np.abs(2 * (velocity // V % V) - (V - 1)).astype(np.float32) / (V - 1)
    courants = np.zeros((GROUPS, 2, EDGE, LANES), np.float32)
    courants[:, 0, :ROWS] = courant_x.reshape(GROUPS, ROWS, LANES)
    courants[:, 1, :ROWS] = courant_y.reshape(GROUPS, ROWS, LANES)

    return {
        "x_forward": stacked(x_forward),
        "x_inverse": np.stack(x_inverse),
        "plane_forward": chunked(np.stack(split_constant(plane_forward))),
        "plane_inverse": chunked(np.stack(split_constant(plane_inverse))),
        "place": chunked(place.astype(ml_dtypes.bfloat16)),
        "unplace": chunked(unplace.astype(ml_dtypes.bfloat16)),
        "reverse": reverse.astype(ml_dtypes.bfloat16),
        "courants": courants,
    }


NAMES = ("x_forward", "x_inverse", "plane_forward", "plane_inverse", "place", "unplace", "reverse", "courants")


def halves(a):
    hi = a.astype(BF16)
    lo = (a - hi.astype(F32)).astype(BF16)
    return hi, lo


def wide(ref, start, count, width=None):
    a = jnp.concatenate([ref[start + i] for i in range(count)], axis=1)
    return a if width is None else a[:, :width]


def dot(a, b):
    return jnp.dot(a, b, preferred_element_type=F32)


def quadrants(a, b, c, d):
    p, m = a + b, a - b
    q, r = c + d, c - d
    return p + q, m + r, p - q, m - r


def kernel(
    sizes,
    dist_hbm, kinds_ref, wall_hbm, inflow_hbm, side_hbm, left_hbm, right_hbm, loss_hbm,
    xf_hbm, xi_hbm, pf_hbm, pi_hbm, place_hbm, unplace_hbm, reverse_hbm, courants_hbm,
    out_ref,
    dist, dense, wall, inflow, side, raw, xf, xi, pf, pi, place, unplace, reverse, courants,
    sides, packed, quads, table, send, recv, field, shaped_hi, shaped_lo, planes, collided, back, own, from_y, from_x,
    local_sem, send1, recv1, send_own, recv_own, send_y, recv_y, send_x, recv_x,
):
    n_gx, n_gy = sizes
    gx, gy, me = lax.axis_index("gx"), lax.axis_index("gy"), lax.axis_index("vert")
    my_y, my_h = lax.rem(me, 2), me // 2
    step_y, step_x = 2 * my_y - 1, 2 * my_h - 1
    to_y, to_x = gy + step_y, gx + step_x
    has_y = jnp.logical_and(to_y >= 0, to_y < n_gy)
    has_x = jnp.logical_and(to_x >= 0, to_x < n_gx)

    at_gain = RANK * V * PLANE // V
    pulls = [
        (dist_hbm, dist), (wall_hbm, wall), (inflow_hbm, inflow),
        (left_hbm, raw.at[pl.ds(0, at_gain)]), (right_hbm, raw.at[pl.ds(at_gain, at_gain)]),
        (loss_hbm, raw.at[pl.ds(2 * at_gain, PLANE)]), (place_hbm, place), (reverse_hbm, reverse),
        (xf_hbm, xf), (pf_hbm, pf), (xi_hbm, xi), (pi_hbm, pi), (unplace_hbm, unplace), (side_hbm, side),
        (courants_hbm.at[me], courants),
    ]
    pulls = [pltpu.make_async_copy(a, b, local_sem.at[i]) for i, (a, b) in enumerate(pulls)]
    for pull in pulls:
        pull.start()

    for edge, buffers in ((0, from_x), (n_gx - 1, from_x)):
        @pl.when(gx == edge)
        def _(edge=edge):
            from_x[0 if edge == 0 else 1] = jnp.zeros((2, EDGE, LANES), F32)

    for edge in (0, n_gy - 1):
        @pl.when(gy == edge)
        def _(edge=edge):
            from_y[0 if edge == 0 else 1] = jnp.zeros((2, BLOCK, LANES), F32)

    barrier = pltpu.get_barrier_semaphore()

    def greet(x, y, v):
        pl.semaphore_signal(barrier, inc=1, device_id=(x, y, v), device_id_type=MESH)

    for d in range(1, GROUPS):
        greet(gx, gy, lax.rem(me + d, GROUPS))
    for step in (-1, 1):
        @pl.when(jnp.logical_and(gy + step >= 0, gy + step < n_gy))
        def _(step=step):
            for h in range(2):
                greet(gx, gy + step, 2 * h + (1 if step < 0 else 0))

        @pl.when(jnp.logical_and(gx + step >= 0, gx + step < n_gx))
        def _(step=step):
            for y in range(2):
                greet(gx + step, gy, y + (2 if step < 0 else 0))

    for i in range(3):
        pulls[i].wait()
    for x in range(NX):
        for r in range(ROWS):
            at = (x * ROWS + r) * NY
            dense[at : at + NY, :] = dist[x, :, r * LANES : (r + 1) * LANES]
    for v in range(GROUPS):
        y, h = v % 2, v // 2
        send[v, pl.ds(48, 8)] = jnp.zeros((8, LANES), F32)
        for cell in range(2):
            x = 3 * h + (1 - 2 * h) * cell
            kind = jnp.full((ROWS, LANES), kinds_ref[y, x], jnp.int32)
            own_state = dense[pl.ds(x * 2 * ROWS + y, ROWS, stride=2), :]
            state = jnp.where(kind == 1, wall[...], jnp.where(kind == 2, inflow[...], own_state))
            send[v, pl.ds(cell * ROWS, ROWS)] = state
    recv[me] = send[me]

    pl.semaphore_wait(
        barrier, GROUPS - 1 + GROUPS * has_y.astype(jnp.int32) + GROUPS * has_x.astype(jnp.int32)
    )
    first = []
    for d in range(1, GROUPS):
        to = lax.rem(me + d, GROUPS)
        first.append(
            pltpu.make_async_remote_copy(
                src_ref=send.at[to], dst_ref=recv.at[me], send_sem=send1.at[d], recv_sem=recv1.at[d],
                device_id=(gx, gy, to), device_id_type=MESH,
            )
        )
        first[-1].start()

    for i in range(3, 8):
        pulls[i].wait()
    packed[...] = jnp.zeros_like(packed)
    for ky in range(V):
        at = (ky // PACK) * LANES + (ky % PACK) * V
        packed[:, at : at + V] = raw[pl.ds(ky, TABLES * V, stride=V), :]
    hi, lo = halves(packed[...])
    both = jnp.concatenate([hi, lo], axis=0)
    for s in range(4):
        q = dot(both, wide(place, 2 * s, 2))
        quads[s] = q[: TABLES * V] + q[TABLES * V :]

    def symmetrise(t, _):
        at = pl.ds(pl.multiple_of(t * V, 8), V)
        for s in range(4):
            hi, lo = halves(quads[3 - s, at])
            mirrored = dot(reverse[...], jnp.concatenate([hi, lo], axis=0))[:V]
            table[s, at] = quads[s, at] + mirrored
        return 0

    lax.fori_loop(0, TABLES, symmetrise, 0)

    pulls[13].wait()
    for r in range(ROWS):
        for k in range(2):
            sides[k, r : r + 1, :] = side[k : k + 1, r * LANES : (r + 1) * LANES]

    for i in range(8, 13):
        pulls[i].wait()
    for d in range(1, GROUPS):
        first[d - 1].wait_recv()
    for u in range(GROUPS):
        for c in range(CHUNKS):
            field[6 * u : 6 * u + 6, c * LANES : (c + 1) * LANES] = recv[u, pl.ds(c, 6, stride=CHUNKS), :]
    cells = jnp.concatenate([field[:, :PLANE], field[:, PLANE:]], axis=0)
    hi, lo = halves(cells)
    along_x = dot(wide(xf, 0, 2, 6 * V), jnp.concatenate([hi, lo, hi], axis=0))
    hi, lo = halves(along_x)
    both = jnp.concatenate([hi, lo], axis=0)
    parts = []
    for c in range(4):
        top = dot(both, wide(pf.at[0], 2 * c, 2))
        parts.append(top[: 2 * V] + top[2 * V :] + dot(hi, wide(pf.at[1], 2 * c, 2)))
    cc, cs, sc, ss = parts
    cos_cos, sin_sin = cc, -ss
    swapped = lambda a: jnp.concatenate([a[V:], -a[:V]], axis=0)
    spectrum = quadrants(cos_cos, swapped(cs), swapped(sc), sin_sin)

    for t in range(TABLES):
        at = slice(t * V, (t + 1) * V)
        a = []
        for s in range(4):
            m = table[s, at]
            a.append(jnp.concatenate([spectrum[s][:V] * m, spectrum[s][V:] * m], axis=0))
        for c, b in enumerate(quadrants_to_classes(*a)):
            hi, lo = halves(b)
            z = dot(wide(xi.at[c], 0, 2, 6 * V), jnp.concatenate([hi, lo, hi], axis=0))
            hi, lo = halves(z)
            shaped_hi[c, t * 2 * V : (t + 1) * 2 * V] = hi
            shaped_lo[c, t * 2 * V : (t + 1) * 2 * V] = lo
    for c in range(4):
        top, low = wide(pi.at[0, c], 0, 2), wide(pi.at[1, c], 0, 2)
        planes[c] = dot(shaped_hi[c], top) + dot(shaped_lo[c], top) + dot(shaped_hi[c], low)

    def fields(t):
        at = slice(t * 2 * V, (t + 1) * 2 * V)
        return quadrants(*(planes[c, at] for c in range(4)))

    gain = [0.0] * 4
    for r in range(RANK):
        gain = [g + a * b for g, a, b in zip(gain, fields(r), fields(RANK + r))]
    rates = jnp.concatenate(
        [jnp.concatenate(list(gain), axis=1), jnp.concatenate(list(fields(2 * RANK)), axis=1)], axis=0
    )
    hi, lo = halves(rates)
    rates = dot(jnp.concatenate([hi, lo], axis=0), wide(unplace, 0, 5, PLANE))
    rates = rates[: 4 * V] + rates[4 * V :]
    result = cells + COLLISION_STEP * (rates[: 2 * V] - cells * rates[2 * V :])
    collided[:, :PLANE] = result[:V]
    collided[:, PLANE:] = result[V:]
    for u in range(GROUPS):
        back[u, pl.ds(48, 8)] = jnp.zeros((8, LANES), F32)
        for c in range(CHUNKS):
            back[u, pl.ds(c, 6, stride=CHUNKS), :] = collided[6 * u : 6 * u + 6, c * LANES : (c + 1) * LANES]

    def push_x(u):
        return pltpu.make_async_remote_copy(
            src_ref=back.at[u, pl.ds(0, EDGE)], dst_ref=from_x.at[1 - my_h, my_y],
            send_sem=send_x.at[u], recv_sem=recv_x.at[1 - my_h, my_y],
            device_id=(to_x, gy, u), device_id_type=MESH,
        )

    def push_y(u):
        return pltpu.make_async_remote_copy(
            src_ref=back.at[u], dst_ref=from_y.at[1 - my_y, my_h],
            send_sem=send_y.at[u], recv_sem=recv_y.at[1 - my_y, my_h],
            device_id=(gx, to_y, u), device_id_type=MESH,
        )

    def push_own(d):
        to = lax.rem(me + d, GROUPS)
        return pltpu.make_async_remote_copy(
            src_ref=back.at[to], dst_ref=own.at[me], send_sem=send_own.at[d], recv_sem=recv_own.at[d],
            device_id=(gx, gy, to), device_id_type=MESH,
        )

    @pl.when(has_x)
    def _():
        for u in range(GROUPS):
            push_x(u).start()

    @pl.when(has_y)
    def _():
        for u in range(GROUPS):
            push_y(u).start()

    for d in range(1, GROUPS):
        push_own(d).start()
    own[me] = back[me]

    pulls[14].wait()
    for d in range(1, GROUPS):
        push_own(d).wait_recv()
    for step in (-1, 1):
        k = 0 if step < 0 else 1

        @pl.when(jnp.logical_and(gy + step >= 0, gy + step < n_gy))
        def _(k=k):
            for h in range(2):
                pltpu.make_async_remote_copy(
                    src_ref=back.at[0], dst_ref=from_y.at[k, h], send_sem=send_y.at[0], recv_sem=recv_y.at[k, h],
                    device_id=(gx, to_y, me), device_id_type=MESH,
                ).wait_recv()

        @pl.when(jnp.logical_and(gx + step >= 0, gx + step < n_gx))
        def _(k=k):
            for y in range(2):
                pltpu.make_async_remote_copy(
                    src_ref=back.at[0, pl.ds(0, EDGE)], dst_ref=from_x.at[k, y], send_sem=send_x.at[0],
                    recv_sem=recv_x.at[k, y], device_id=(to_x, gy, me), device_id_type=MESH,
                ).wait_recv()

    def at_cell(ref, x):
        cell = (0, 1, 1, 0)[x]
        return ref[pl.ds(cell * ROWS, ROWS), :]

    courant_x, courant_y = courants[0, pl.ds(0, ROWS)], courants[1, pl.ds(0, ROWS)]
    higher_x, higher_y = sides[0] == 1, sides[1] == 1
    centre = {(x, y): at_cell(own.at[y + 2 * (x // 2)], x) for x in range(NX) for y in range(NY)}
    for x in range(NX):
        for y in range(NY):
            here = centre[x, y]
            below_x = centre[x - 1, y] if x > 0 else from_x[0, y, pl.ds(0, ROWS)]
            above_x = centre[x + 1, y] if x < NX - 1 else from_x[1, y, pl.ds(0, ROWS)]
            below_y = centre[x, 0] if y > 0 else at_cell(from_y.at[0, x // 2], x)
            above_y = centre[x, 1] if y < 1 else at_cell(from_y.at[1, x // 2], x)
            up_x = jnp.where(higher_x, below_x, above_x)
            up_y = jnp.where(higher_y, below_y, above_y)
            dense[pl.ds(x * 2 * ROWS + y, ROWS, stride=2), :] = (
                here - courant_x * (here - up_x) - courant_y * (here - up_y)
            )
        for r in range(ROWS):
            at = (x * ROWS + r) * NY
            out_ref[x, :, r * LANES : (r + 1) * LANES] = dense[at : at + NY, :]

    for d in range(1, GROUPS):
        first[d - 1].wait_send()
        push_own(d).wait_send()

    @pl.when(has_y)
    def _():
        for u in range(GROUPS):
            push_y(u).wait_send()

    @pl.when(has_x)
    def _():
        for u in range(GROUPS):
            push_x(u).wait_send()


def quadrants_to_classes(pp, pm, mp, mm):
    a, b = pp + pm, pp - pm
    c, d = mp + mm, mp - mm
    return a + c, b + d, a - c, b - d


def on_device(sizes, distribution, cell_types, wall_state, inflow_state, upwind_side, gain_left, gain_right, loss_table):
    tables = constants()
    tables = [jnp.asarray(tables[name]) for name in NAMES]
    operands = [
        distribution,
        cell_types.T,
        wall_state.reshape(ROWS, LANES),
        inflow_state.reshape(ROWS, LANES),
        upwind_side,
        gain_left.reshape(RANK * PLANE, V),
        gain_right.reshape(RANK * PLANE, V),
        loss_table.reshape(PLANE, V),
        *tables,
    ]
    spaces = [pl.BlockSpec(memory_space=pl.ANY)] * len(operands)
    spaces[1] = pl.BlockSpec(memory_space=pltpu.SMEM)
    dma = pltpu.SemaphoreType.DMA
    held = [
        pltpu.VMEM((NX, NY, SLAB), F32),
        pltpu.VMEM((NX * NY * ROWS, LANES), F32),
        pltpu.VMEM((ROWS, LANES), F32),
        pltpu.VMEM((ROWS, LANES), F32),
        pltpu.VMEM((2, SLAB), jnp.int32),
        pltpu.VMEM((TABLES * PLANE, V), F32),
        *(pltpu.VMEM(t.shape, t.dtype) for t in tables[:-1]),
        pltpu.VMEM(tables[-1].shape[1:], F32),
        pltpu.VMEM((2, ROWS, LANES), jnp.int32),
        pltpu.VMEM((TABLES * V, GROUPED), F32),
        pltpu.VMEM((4, TABLES * V, W), F32),
        pltpu.VMEM((4, TABLES * V, W), F32),
        pltpu.VMEM((GROUPS, BLOCK, LANES), F32),
        pltpu.VMEM((GROUPS, BLOCK, LANES), F32),
        pltpu.VMEM((V, 2 * PLANE), F32),
        pltpu.VMEM((4, TABLES * 2 * V, W), BF16),
        pltpu.VMEM((4, TABLES * 2 * V, W), BF16),
        pltpu.VMEM((4, TABLES * 2 * V, W), F32),
        pltpu.VMEM((V, 2 * PLANE), F32),
        pltpu.VMEM((GROUPS, BLOCK, LANES), F32),
        pltpu.VMEM((GROUPS, BLOCK, LANES), F32),
        pltpu.VMEM((2, 2, BLOCK, LANES), F32),
        pltpu.VMEM((2, 2, EDGE, LANES), F32),
        dma((15,)),
        dma((GROUPS,)), dma((GROUPS,)),
        dma((GROUPS,)), dma((GROUPS,)),
        dma((GROUPS,)), dma((2, 2)),
        dma((GROUPS,)), dma((2, 2)),
    ]
    return pl.pallas_call(
        functools.partial(kernel, sizes),
        out_shape=jax.ShapeDtypeStruct((NX, NY, SLAB), F32),
        in_specs=spaces,
        out_specs=pl.BlockSpec(memory_space=pltpu.VMEM),
        scratch_shapes=held,
        compiler_params=pltpu.CompilerParams(
            collective_id=0, has_side_effects=True, vmem_limit_bytes=60 * 1024 * 1024
        ),
        cost_estimate=pl.CostEstimate(flops=3_000_000_000, bytes_accessed=10_000_000, transcendentals=0),
        name="step",
    )(*operands)


def solution(mesh):
    placed = (
        P("gx", "gy", "vert"),
        P("gx", "gy"),
        P("vert"),
        P("vert"),
        P(None, "vert"),
        P(),
        P(),
        P(),
    )
    sizes = (mesh.shape["gx"], mesh.shape["gy"])
    return jax.shard_map(
        functools.partial(on_device, sizes),
        mesh=mesh,
        in_specs=placed,
        out_specs=P("gx", "gy", "vert"),
        check_vma=False,
    )
```

```python
import functools

import jax
import jax.numpy as jnp
import ml_dtypes
import numpy as np
from jax import lax
from jax.experimental import pallas as pl
from jax.experimental.pallas import tpu as pltpu
from jax.sharding import PartitionSpec as P

MESH = pl.DeviceIdType.MESH
F32 = jnp.float32
BF16 = jnp.bfloat16

V = 24
PLANE = V * V
HALF = V // 2
RANK = 4
TABLES = 2 * RANK + 1
GROUPS = 4
NX, NY = 4, 2
SLAB = PLANE * V // GROUPS
LANES = 128
ROWS = SLAB // LANES
BLOCK = 56
EDGE = 32
PAIRS = 3
CHUNKS = 2 * PLANE // LANES
W = 256
PACK = 5
GROUPED = 5 * LANES
SIGNS = ((1, 1), (1, -1), (-1, 1), (-1, -1))
COLLISION_STEP = 0.25
COURANT = 0.45


def split_constant(a):
    hi = a.astype(ml_dtypes.bfloat16)
    lo = (a - hi.astype(np.float64)).astype(ml_dtypes.bfloat16)
    return hi, lo


def chunked(a):
    pad = -a.shape[-1] % LANES
    a = np.pad(a, [(0, 0)] * (a.ndim - 1) + [(0, pad)])
    a = a.reshape(*a.shape[:-1], -1, LANES)
    return np.ascontiguousarray(np.moveaxis(a, -2, -3))


def stacked(a):
    hi, lo = split_constant(a)
    return chunked(np.concatenate([hi, hi, lo], axis=1))


@functools.cache
def constants():
    step = 2.0 * np.pi / V
    inner = [(a, b) for a in range(1, HALF) for b in range(1, HALF)]
    outer = [(a, b) for a in range(HALF + 1) for b in range(HALF + 1) if a % HALF == 0 or b % HALF == 0]
    points = np.array(inner + outer)
    count = len(points)
    qy, qz = points[:, 0], points[:, 1]
    natural = np.arange(PLANE)
    ny, nz = natural // V, natural % V
    trig = (np.cos, np.sin)
    classes = ((0, 0), (0, 1), (1, 0), (1, 1))

    def grid(rows_y, rows_z, cy, cz):
        by = trig[cy](step * (rows_y[:, None] * qy[None, :] % V))
        bz = trig[cz](step * (rows_z[:, None] * qz[None, :] % V))
        return by * bz

    plane_forward = np.zeros((PLANE, 4 * W))
    plane_inverse = np.zeros((4, W, W))
    weight = np.where(qy % HALF == 0, 0.5, 1.0) * np.where(qz % HALF == 0, 0.5, 1.0) / PLANE
    for c, (cy, cz) in enumerate(classes):
        plane_forward[:, c * W : c * W + count] = grid(ny, nz, cy, cz)
        plane_inverse[c, :count, :count] = weight[:, None] * grid(qy, qz, cy, cz)

    place = np.zeros((GROUPED, 4 * W))
    unplace = np.zeros((4 * W, PLANE))
    seen = set()
    for s, (sy, sz) in enumerate(SIGNS):
        for q in range(count):
            y, z = sy * qy[q] % V, sz * qz[q] % V
            place[(y // PACK) * LANES + (y % PACK) * V + z, s * W + q] = 1.0
            if (y, z) not in seen:
                seen.add((y, z))
                unplace[s * W + q, y * V + z] = 1.0

    row_of = np.zeros((2, V), dtype=int)
    for jx in range(V):
        pair, odd = jx // 2, jx % 2
        u, q = pair // PAIRS, pair % PAIRS
        for cell in range(2):
            row_of[cell, jx] = odd * V + 2 * PAIRS * u + PAIRS * cell + q
    k = np.arange(V)
    theta = step * (k[:, None] * k[None, :] % V)
    cos, sin = np.cos(theta), np.sin(theta)
    x_forward = np.zeros((2 * V, 2 * V))
    x_forward[:V, row_of[0]] = cos
    x_forward[:V, row_of[1]] = sin
    x_forward[V:, row_of[0]] = -sin
    x_forward[V:, row_of[1]] = cos
    real = np.concatenate([cos, -sin], axis=1)
    imag = np.concatenate([sin, cos], axis=1)
    x_inverse = []
    for first, second in ((real, imag), (-imag, real), (-imag, real), (-real, -imag)):
        m = np.zeros((2 * V, 2 * V))
        m[row_of[0]] = first
        m[row_of[1]] = second
        x_inverse.append(stacked(m / (2 * V)))

    reverse = np.zeros((32, 2 * V))
    for r in range(V):
        reverse[r, (V - r) % V] = 1.0
        reverse[r, V + (V - r) % V] = 1.0

    velocity = np.arange(PLANE * V)
    courant_x = COURANT * np.abs(2 * (velocity // PLANE) - (V - 1)).astype(np.float32) / (V - 1)
    courant_y = COURANT * np.abs(2 * (velocity // V % V) - (V - 1)).astype(np.float32) / (V - 1)
    courants = np.zeros((GROUPS, 2, EDGE, LANES), np.float32)
    courants[:, 0, :ROWS] = courant_x.reshape(GROUPS, ROWS, LANES)
    courants[:, 1, :ROWS] = courant_y.reshape(GROUPS, ROWS, LANES)

    return {
        "x_forward": stacked(x_forward),
        "x_inverse": np.stack(x_inverse),
        "plane_forward": chunked(np.stack(split_constant(plane_forward))),
        "plane_inverse": chunked(np.stack(split_constant(plane_inverse))),
        "place": chunked(place.astype(ml_dtypes.bfloat16)),
        "unplace": chunked(unplace.astype(ml_dtypes.bfloat16)),
        "reverse": reverse.astype(ml_dtypes.bfloat16),
        "courants": courants,
    }


NAMES = ("x_forward", "x_inverse", "plane_forward", "plane_inverse", "place", "unplace", "reverse", "courants")


def halves(a):
    hi = a.astype(BF16)
    lo = (a - hi.astype(F32)).astype(BF16)
    return hi, lo


def wide(ref, start, count, width=None):
    a = jnp.concatenate([ref[start + i] for i in range(count)], axis=1)
    return a if width is None else a[:, :width]


def dot(a, b):
    return jnp.dot(a, b, preferred_element_type=F32)


def quadrants(a, b, c, d):
    p, m = a + b, a - b
    q, r = c + d, c - d
    return p + q, m + r, p - q, m - r


def kernel(
    sizes,
    dist_hbm, kinds_ref, wall_hbm, inflow_hbm, side_hbm, left_hbm, right_hbm, loss_hbm,
    xf_hbm, xi_hbm, pf_hbm, pi_hbm, place_hbm, unplace_hbm, reverse_hbm, courants_hbm,
    out_ref,
    dist, dense, wall, inflow, side, raw, xf, xi, pf, pi, place, unplace, reverse, courants,
    sides, packed, quads, table, send, recv, field, shaped_hi, shaped_lo, planes, collided, back, own, from_y, from_x,
    local_sem, send1, recv1, send_own, recv_own, send_y, recv_y, send_x, recv_x, ready,
):
    n_gx, n_gy = sizes
    gx, gy, me = lax.axis_index("gx"), lax.axis_index("gy"), lax.axis_index("vert")
    my_y, my_h = lax.rem(me, 2), me // 2
    step_y, step_x = 2 * my_y - 1, 2 * my_h - 1
    to_y, to_x = gy + step_y, gx + step_x
    has_y = jnp.logical_and(to_y >= 0, to_y < n_gy)
    has_x = jnp.logical_and(to_x >= 0, to_x < n_gx)
    core = lax.rem(gx, 2)
    early = lax.rem(gx // 2, 2) == 0
    near_x, far_x = gx + 1 - 2 * core, gx - 1 + 2 * core
    has_far = jnp.logical_and(far_x >= 0, far_x < n_gx)
    sends_far = my_h == core
    early_far = jnp.logical_and(has_far, early)
    late_far = jnp.logical_and(has_far, jnp.logical_not(early))

    at_gain = RANK * V * PLANE // V
    pulls = [
        (dist_hbm, dist), (wall_hbm, wall), (inflow_hbm, inflow),
        (left_hbm, raw.at[pl.ds(0, at_gain)]), (right_hbm, raw.at[pl.ds(at_gain, at_gain)]),
        (loss_hbm, raw.at[pl.ds(2 * at_gain, PLANE)]), (place_hbm, place), (reverse_hbm, reverse),
        (xf_hbm, xf), (pf_hbm, pf), (xi_hbm, xi), (pi_hbm, pi), (unplace_hbm, unplace), (side_hbm, side),
        (courants_hbm.at[me], courants),
    ]
    pulls = [pltpu.make_async_copy(a, b, local_sem.at[i]) for i, (a, b) in enumerate(pulls)]
    for pull in pulls:
        pull.start()

    for k in range(2):
        @pl.when(gx == k * (n_gx - 1))
        def _(k=k):
            from_x[k] = jnp.zeros((2, EDGE, LANES), F32)

        @pl.when(gy == k * (n_gy - 1))
        def _(k=k):
            from_y[k] = jnp.zeros((2, BLOCK, LANES), F32)

    barrier = pltpu.get_barrier_semaphore()

    def greet(x, y, v):
        pl.semaphore_signal(barrier, inc=1, device_id=(x, y, v), device_id_type=MESH)

    for d in range(1, GROUPS):
        greet(gx, gy, lax.rem(me + d, GROUPS))
    for step in (-1, 1):
        @pl.when(jnp.logical_and(gy + step >= 0, gy + step < n_gy))
        def _(step=step):
            for h in range(2):
                greet(gx, gy + step, 2 * h + (1 if step < 0 else 0))

    for y in range(2):
        greet(near_x, gy, y + 2 * core)

    @pl.when(early_far)
    def _():
        for y in range(2):
            greet(far_x, gy, y + 2 * (1 - core))

        @pl.when(sends_far)
        def _():
            for y in range(2):
                greet(far_x, gy, y + 2 * core)

    for i in range(3):
        pulls[i].wait()
    for x in range(NX):
        for r in range(ROWS):
            at = (x * ROWS + r) * NY
            dense[at : at + NY, :] = dist[x, :, r * LANES : (r + 1) * LANES]
    for v in range(GROUPS):
        y, h = v % 2, v // 2
        send[v, pl.ds(48, 8)] = jnp.zeros((8, LANES), F32)
        for cell in range(2):
            x = 3 * h + (1 - 2 * h) * cell
            kind = jnp.full((ROWS, LANES), kinds_ref[y, x], jnp.int32)
            own_state = dense[pl.ds(x * 2 * ROWS + y, ROWS, stride=2), :]
            state = jnp.where(kind == 1, wall[...], jnp.where(kind == 2, inflow[...], own_state))
            send[v, pl.ds(cell * ROWS, ROWS)] = state
    recv[me] = send[me]

    awaited = GROUPS - 1 + jnp.where(has_y, GROUPS, 0) + jnp.where(sends_far, 0, GROUPS)
    pl.semaphore_wait(barrier, awaited + jnp.where(late_far, jnp.where(sends_far, GROUPS, 2), 0))
    first = []
    for d in range(1, GROUPS):
        to = lax.rem(me + d, GROUPS)
        first.append(
            pltpu.make_async_remote_copy(
                src_ref=send.at[to], dst_ref=recv.at[me], send_sem=send1.at[d], recv_sem=recv1.at[d],
                device_id=(gx, gy, to), device_id_type=MESH,
            )
        )
        first[-1].start()

    @pl.when(late_far)
    def _():
        for y in range(2):
            pl.semaphore_signal(
                ready, inc=1, device_id=(far_x, gy, y + 2 * (1 - core)), device_id_type=MESH
            )

    for i in range(3, 8):
        pulls[i].wait()
    packed[...] = jnp.zeros_like(packed)
    for ky in range(V):
        at = (ky // PACK) * LANES + (ky % PACK) * V
        packed[:, at : at + V] = raw[pl.ds(ky, TABLES * V, stride=V), :]
    hi, lo = halves(packed[...])
    both = jnp.concatenate([hi, lo], axis=0)
    for s in range(4):
        q = dot(both, wide(place, 2 * s, 2))
        quads[s] = q[: TABLES * V] + q[TABLES * V :]

    def symmetrise(t, _):
        at = pl.ds(pl.multiple_of(t * V, 8), V)
        for s in range(4):
            hi, lo = halves(quads[3 - s, at])
            mirrored = dot(reverse[...], jnp.concatenate([hi, lo], axis=0))[:V]
            table[s, at] = quads[s, at] + mirrored
        return 0

    lax.fori_loop(0, TABLES, symmetrise, 0)

    pulls[13].wait()
    for r in range(ROWS):
        for k in range(2):
            sides[k, r : r + 1, :] = side[k : k + 1, r * LANES : (r + 1) * LANES]

    for i in range(8, 13):
        pulls[i].wait()
    for d in range(1, GROUPS):
        first[d - 1].wait_recv()
    for u in range(GROUPS):
        for c in range(CHUNKS):
            field[6 * u : 6 * u + 6, c * LANES : (c + 1) * LANES] = recv[u, pl.ds(c, 6, stride=CHUNKS), :]
    cells = jnp.concatenate([field[:, :PLANE], field[:, PLANE:]], axis=0)
    hi, lo = halves(cells)
    along_x = dot(wide(xf, 0, 2, 6 * V), jnp.concatenate([hi, lo, hi], axis=0))
    hi, lo = halves(along_x)
    both = jnp.concatenate([hi, lo], axis=0)
    parts = []
    for c in range(4):
        top = dot(both, wide(pf.at[0], 2 * c, 2))
        parts.append(top[: 2 * V] + top[2 * V :] + dot(hi, wide(pf.at[1], 2 * c, 2)))
    cc, cs, sc, ss = parts
    cos_cos, sin_sin = cc, -ss
    swapped = lambda a: jnp.concatenate([a[V:], -a[:V]], axis=0)
    spectrum = quadrants(cos_cos, swapped(cs), swapped(sc), sin_sin)

    for t in range(TABLES):
        at = slice(t * V, (t + 1) * V)
        a = []
        for s in range(4):
            m = table[s, at]
            a.append(jnp.concatenate([spectrum[s][:V] * m, spectrum[s][V:] * m], axis=0))
        for c, b in enumerate(quadrants_to_classes(*a)):
            hi, lo = halves(b)
            z = dot(wide(xi.at[c], 0, 2, 6 * V), jnp.concatenate([hi, lo, hi], axis=0))
            hi, lo = halves(z)
            shaped_hi[c, t * 2 * V : (t + 1) * 2 * V] = hi
            shaped_lo[c, t * 2 * V : (t + 1) * 2 * V] = lo
    for c in range(4):
        top, low = wide(pi.at[0, c], 0, 2), wide(pi.at[1, c], 0, 2)
        planes[c] = dot(shaped_hi[c], top) + dot(shaped_lo[c], top) + dot(shaped_hi[c], low)

    def fields(t):
        at = slice(t * 2 * V, (t + 1) * 2 * V)
        return quadrants(*(planes[c, at] for c in range(4)))

    gain = [0.0] * 4
    for r in range(RANK):
        gain = [g + a * b for g, a, b in zip(gain, fields(r), fields(RANK + r))]
    rates = jnp.concatenate(
        [jnp.concatenate(list(gain), axis=1), jnp.concatenate(list(fields(2 * RANK)), axis=1)], axis=0
    )
    hi, lo = halves(rates)
    rates = dot(jnp.concatenate([hi, lo], axis=0), wide(unplace, 0, 5, PLANE))
    rates = rates[: 4 * V] + rates[4 * V :]
    result = cells + COLLISION_STEP * (rates[: 2 * V] - cells * rates[2 * V :])
    collided[:, :PLANE] = result[:V]
    collided[:, PLANE:] = result[V:]
    for u in range(GROUPS):
        back[u, pl.ds(48, 8)] = jnp.zeros((8, LANES), F32)
        for c in range(CHUNKS):
            back[u, pl.ds(c, 6, stride=CHUNKS), :] = collided[6 * u : 6 * u + 6, c * LANES : (c + 1) * LANES]

    def push_x(u):
        return pltpu.make_async_remote_copy(
            src_ref=back.at[u, pl.ds(0, EDGE)], dst_ref=from_x.at[1 - my_h, my_y],
            send_sem=send_x.at[u], recv_sem=recv_x.at[1 - my_h, my_y],
            device_id=(to_x, gy, u), device_id_type=MESH,
        )

    def push_y(u):
        return pltpu.make_async_remote_copy(
            src_ref=back.at[u], dst_ref=from_y.at[1 - my_y, my_h],
            send_sem=send_y.at[u], recv_sem=recv_y.at[1 - my_y, my_h],
            device_id=(gx, to_y, u), device_id_type=MESH,
        )

    def push_own(d):
        to = lax.rem(me + d, GROUPS)
        return pltpu.make_async_remote_copy(
            src_ref=back.at[to], dst_ref=own.at[me], send_sem=send_own.at[d], recv_sem=recv_own.at[d],
            device_id=(gx, gy, to), device_id_type=MESH,
        )

    @pl.when(jnp.logical_and(has_x, jnp.logical_not(jnp.logical_and(early, sends_far))))
    def _():
        for u in range(GROUPS):
            push_x(u).start()

    @pl.when(has_y)
    def _():
        for u in range(GROUPS):
            push_y(u).start()

    for d in range(1, GROUPS):
        push_own(d).start()
    own[me] = back[me]

    @pl.when(jnp.logical_and(early_far, sends_far))
    def _():
        pl.semaphore_wait(ready, GROUPS)
        for u in range(GROUPS):
            push_x(u).start()

    pulls[14].wait()
    for d in range(1, GROUPS):
        push_own(d).wait_recv()
    for step in (-1, 1):
        k = 0 if step < 0 else 1

        @pl.when(jnp.logical_and(gy + step >= 0, gy + step < n_gy))
        def _(k=k):
            for h in range(2):
                pltpu.make_async_remote_copy(
                    src_ref=back.at[0], dst_ref=from_y.at[k, h], send_sem=send_y.at[0], recv_sem=recv_y.at[k, h],
                    device_id=(gx, to_y, me), device_id_type=MESH,
                ).wait_recv()

        @pl.when(jnp.logical_and(gx + step >= 0, gx + step < n_gx))
        def _(k=k):
            for y in range(2):
                pltpu.make_async_remote_copy(
                    src_ref=back.at[0, pl.ds(0, EDGE)], dst_ref=from_x.at[k, y], send_sem=send_x.at[0],
                    recv_sem=recv_x.at[k, y], device_id=(to_x, gy, me), device_id_type=MESH,
                ).wait_recv()

    def at_cell(ref, x):
        cell = (0, 1, 1, 0)[x]
        return ref[pl.ds(cell * ROWS, ROWS), :]

    courant_x, courant_y = courants[0, pl.ds(0, ROWS)], courants[1, pl.ds(0, ROWS)]
    higher_x, higher_y = sides[0] == 1, sides[1] == 1
    centre = {(x, y): at_cell(own.at[y + 2 * (x // 2)], x) for x in range(NX) for y in range(NY)}
    for x in range(NX):
        for y in range(NY):
            here = centre[x, y]
            below_x = centre[x - 1, y] if x > 0 else from_x[0, y, pl.ds(0, ROWS)]
            above_x = centre[x + 1, y] if x < NX - 1 else from_x[1, y, pl.ds(0, ROWS)]
            below_y = centre[x, 0] if y > 0 else at_cell(from_y.at[0, x // 2], x)
            above_y = centre[x, 1] if y < 1 else at_cell(from_y.at[1, x // 2], x)
            up_x = jnp.where(higher_x, below_x, above_x)
            up_y = jnp.where(higher_y, below_y, above_y)
            dense[pl.ds(x * 2 * ROWS + y, ROWS, stride=2), :] = (
                here - courant_x * (here - up_x) - courant_y * (here - up_y)
            )
        for r in range(ROWS):
            at = (x * ROWS + r) * NY
            out_ref[x, :, r * LANES : (r + 1) * LANES] = dense[at : at + NY, :]

    for d in range(1, GROUPS):
        first[d - 1].wait_send()
        push_own(d).wait_send()

    @pl.when(has_y)
    def _():
        for u in range(GROUPS):
            push_y(u).wait_send()

    @pl.when(has_x)
    def _():
        for u in range(GROUPS):
            push_x(u).wait_send()


def quadrants_to_classes(pp, pm, mp, mm):
    a, b = pp + pm, pp - pm
    c, d = mp + mm, mp - mm
    return a + c, b + d, a - c, b - d


def on_device(sizes, distribution, cell_types, wall_state, inflow_state, upwind_side, gain_left, gain_right, loss_table):
    tables = constants()
    tables = [jnp.asarray(tables[name]) for name in NAMES]
    operands = [
        distribution,
        cell_types.T,
        wall_state.reshape(ROWS, LANES),
        inflow_state.reshape(ROWS, LANES),
        upwind_side,
        gain_left.reshape(RANK * PLANE, V),
        gain_right.reshape(RANK * PLANE, V),
        loss_table.reshape(PLANE, V),
        *tables,
    ]
    spaces = [pl.BlockSpec(memory_space=pl.ANY)] * len(operands)
    spaces[1] = pl.BlockSpec(memory_space=pltpu.SMEM)
    dma = pltpu.SemaphoreType.DMA
    held = [
        pltpu.VMEM((NX, NY, SLAB), F32),
        pltpu.VMEM((NX * NY * ROWS, LANES), F32),
        pltpu.VMEM((ROWS, LANES), F32),
        pltpu.VMEM((ROWS, LANES), F32),
        pltpu.VMEM((2, SLAB), jnp.int32),
        pltpu.VMEM((TABLES * PLANE, V), F32),
        *(pltpu.VMEM(t.shape, t.dtype) for t in tables[:-1]),
        pltpu.VMEM(tables[-1].shape[1:], F32),
        pltpu.VMEM((2, ROWS, LANES), jnp.int32),
        pltpu.VMEM((TABLES * V, GROUPED), F32),
        pltpu.VMEM((4, TABLES * V, W), F32),
        pltpu.VMEM((4, TABLES * V, W), F32),
        pltpu.VMEM((GROUPS, BLOCK, LANES), F32),
        pltpu.VMEM((GROUPS, BLOCK, LANES), F32),
        pltpu.VMEM((V, 2 * PLANE), F32),
        pltpu.VMEM((4, TABLES * 2 * V, W), BF16),
        pltpu.VMEM((4, TABLES * 2 * V, W), BF16),
        pltpu.VMEM((4, TABLES * 2 * V, W), F32),
        pltpu.VMEM((V, 2 * PLANE), F32),
        pltpu.VMEM((GROUPS, BLOCK, LANES), F32),
        pltpu.VMEM((GROUPS, BLOCK, LANES), F32),
        pltpu.VMEM((2, 2, BLOCK, LANES), F32),
        pltpu.VMEM((2, 2, EDGE, LANES), F32),
        dma((15,)),
        dma((GROUPS,)), dma((GROUPS,)),
        dma((GROUPS,)), dma((GROUPS,)),
        dma((GROUPS,)), dma((2, 2)),
        dma((GROUPS,)), dma((2, 2)),
        pltpu.SemaphoreType.REGULAR,
    ]
    return pl.pallas_call(
        functools.partial(kernel, sizes),
        out_shape=jax.ShapeDtypeStruct((NX, NY, SLAB), F32),
        in_specs=spaces,
        out_specs=pl.BlockSpec(memory_space=pltpu.VMEM),
        scratch_shapes=held,
        compiler_params=pltpu.CompilerParams(
            collective_id=0, has_side_effects=True, vmem_limit_bytes=60 * 1024 * 1024
        ),
        cost_estimate=pl.CostEstimate(flops=3_000_000_000, bytes_accessed=10_000_000, transcendentals=0),
        name="step",
    )(*operands)


def solution(mesh):
    placed = (
        P("gx", "gy", "vert"),
        P("gx", "gy"),
        P("vert"),
        P("vert"),
        P(None, "vert"),
        P(),
        P(),
        P(),
    )
    sizes = (mesh.shape["gx"], mesh.shape["gy"])
    return jax.shard_map(
        functools.partial(on_device, sizes),
        mesh=mesh,
        in_specs=placed,
        out_specs=P("gx", "gy", "vert"),
        check_vma=False,
    )
```

```python
import functools

import jax
import jax.numpy as jnp
import ml_dtypes
import numpy as np
from jax import lax
from jax.experimental import pallas as pl
from jax.experimental.pallas import tpu as pltpu
from jax.sharding import PartitionSpec as P

MESH = pl.DeviceIdType.MESH
F32 = jnp.float32
BF16 = jnp.bfloat16

V = 24
PLANE = V * V
HALF = V // 2
RANK = 4
TABLES = 2 * RANK + 1
GROUPS = 4
NX, NY = 4, 2
SLAB = PLANE * V // GROUPS
LANES = 128
ROWS = SLAB // LANES
BLOCK = 56
EDGE = 32
PAIRS = 3
SOME = 16
CHUNKS = 2 * PLANE // LANES
W = 256
PACK = 5
GROUPED = 5 * LANES
SIGNS = ((1, 1), (1, -1), (-1, 1), (-1, -1))
COLLISION_STEP = 0.25
COURANT = 0.45


def split_constant(a):
    hi = a.astype(ml_dtypes.bfloat16)
    lo = (a - hi.astype(np.float64)).astype(ml_dtypes.bfloat16)
    return hi, lo


def chunked(a):
    pad = -a.shape[-1] % LANES
    a = np.pad(a, [(0, 0)] * (a.ndim - 1) + [(0, pad)])
    a = a.reshape(*a.shape[:-1], -1, LANES)
    return np.ascontiguousarray(np.moveaxis(a, -2, -3))


def stacked(a):
    hi, lo = split_constant(a)
    return chunked(np.concatenate([hi, hi, lo], axis=1))


@functools.cache
def constants():
    step = 2.0 * np.pi / V
    inner = [(a, b) for a in range(1, HALF) for b in range(1, HALF)]
    outer = [(a, b) for a in range(HALF + 1) for b in range(HALF + 1) if a % HALF == 0 or b % HALF == 0]
    points = np.array(inner + outer)
    count = len(points)
    qy, qz = points[:, 0], points[:, 1]
    natural = np.arange(PLANE)
    ny, nz = natural // V, natural % V
    trig = (np.cos, np.sin)
    classes = ((0, 0), (0, 1), (1, 0), (1, 1))

    def grid(rows_y, rows_z, cy, cz):
        by = trig[cy](step * (rows_y[:, None] * qy[None, :] % V))
        bz = trig[cz](step * (rows_z[:, None] * qz[None, :] % V))
        return by * bz

    plane_forward = np.zeros((PLANE, 4 * W))
    plane_inverse = np.zeros((4, W, W))
    weight = np.where(qy % HALF == 0, 0.5, 1.0) * np.where(qz % HALF == 0, 0.5, 1.0) / PLANE
    for c, (cy, cz) in enumerate(classes):
        plane_forward[:, c * W : c * W + count] = grid(ny, nz, cy, cz)
        plane_inverse[c, :count, :count] = weight[:, None] * grid(qy, qz, cy, cz)

    place = np.zeros((GROUPED, 4 * W))
    unplace = np.zeros((4 * W, PLANE))
    seen = set()
    for s, (sy, sz) in enumerate(SIGNS):
        for q in range(count):
            y, z = sy * qy[q] % V, sz * qz[q] % V
            place[(y // PACK) * LANES + (y % PACK) * V + z, s * W + q] = 1.0
            if (y, z) not in seen:
                seen.add((y, z))
                unplace[s * W + q, y * V + z] = 1.0

    row_of = np.zeros((2, V), dtype=int)
    for jx in range(V):
        pair, odd = jx // 2, jx % 2
        u, q = pair // PAIRS, pair % PAIRS
        for cell in range(2):
            row_of[cell, jx] = odd * V + 2 * PAIRS * u + PAIRS * cell + q
    k = np.arange(V)
    theta = step * (k[:, None] * k[None, :] % V)
    cos, sin = np.cos(theta), np.sin(theta)
    x_forward = np.zeros((2 * V, 2 * V))
    x_forward[:V, row_of[0]] = cos
    x_forward[:V, row_of[1]] = sin
    x_forward[V:, row_of[0]] = -sin
    x_forward[V:, row_of[1]] = cos
    real = np.concatenate([cos, -sin], axis=1)
    imag = np.concatenate([sin, cos], axis=1)
    x_inverse, x_slab = [], [[] for _ in range(GROUPS)]
    for first, second in ((real, imag), (-imag, real), (-imag, real), (-real, -imag)):
        m = np.zeros((2 * V, 2 * V))
        m[row_of[0]] = first
        m[row_of[1]] = second
        m = m / (2 * V)
        x_inverse.append(stacked(m))
        for u in range(GROUPS):
            own = np.zeros((SOME, 2 * V))
            own[:6], own[6:12] = m[6 * u : 6 * u + 6], m[V + 6 * u : V + 6 * u + 6]
            x_slab[u].append(stacked(own))

    reverse = np.zeros((32, 2 * V))
    for r in range(V):
        reverse[r, (V - r) % V] = 1.0
        reverse[r, V + (V - r) % V] = 1.0

    velocity = np.arange(PLANE * V)
    courant_x = COURANT * np.abs(2 * (velocity // PLANE) - (V - 1)).astype(np.float32) / (V - 1)
    courant_y = COURANT * np.abs(2 * (velocity // V % V) - (V - 1)).astype(np.float32) / (V - 1)
    courants = np.zeros((GROUPS, 2, EDGE, LANES), np.float32)
    courants[:, 0, :ROWS] = courant_x.reshape(GROUPS, ROWS, LANES)
    courants[:, 1, :ROWS] = courant_y.reshape(GROUPS, ROWS, LANES)

    return {
        "x_forward": stacked(x_forward),
        "x_inverse": np.stack(x_inverse),
        "x_slab": np.stack([np.stack(a) for a in x_slab]),
        "plane_forward": chunked(np.stack(split_constant(plane_forward))),
        "plane_inverse": chunked(np.stack(split_constant(plane_inverse))),
        "place": chunked(place.astype(ml_dtypes.bfloat16)),
        "unplace": chunked(unplace.astype(ml_dtypes.bfloat16)),
        "reverse": reverse.astype(ml_dtypes.bfloat16),
        "courants": courants,
    }


NAMES = ("x_forward", "x_inverse", "plane_forward", "plane_inverse", "place", "unplace", "reverse", "x_slab", "courants")


def halves(a):
    hi = a.astype(BF16)
    lo = (a - hi.astype(F32)).astype(BF16)
    return hi, lo


def wide(ref, start, count, width=None):
    a = jnp.concatenate([ref[start + i] for i in range(count)], axis=1)
    return a if width is None else a[:, :width]


def dot(a, b):
    return jnp.dot(a, b, preferred_element_type=F32)


def quadrants(a, b, c, d):
    p, m = a + b, a - b
    q, r = c + d, c - d
    return p + q, m + r, p - q, m - r


def kernel(
    sizes,
    dist_hbm, kinds_ref, wall_hbm, inflow_hbm, side_hbm, left_hbm, right_hbm, loss_hbm,
    xf_hbm, xi_hbm, pf_hbm, pi_hbm, place_hbm, unplace_hbm, reverse_hbm, xs_hbm, courants_hbm,
    out_ref,
    dist, dense, wall, inflow, side, raw, xf, xi, pf, pi, place, unplace, reverse, xs, courants,
    sides, packed, quads, table, send, recv, field, shaped_hi, shaped_lo, planes, collided, back, own, from_y, from_x, edge, far_raw, far_done,
    local_sem, send1, recv1, send_own, recv_own, send_y, recv_y, send_x, recv_x, send_raw, recv_raw, ready,
):
    n_gx, n_gy = sizes
    gx, gy, me = lax.axis_index("gx"), lax.axis_index("gy"), lax.axis_index("vert")
    my_y, my_h = lax.rem(me, 2), me // 2
    step_y, step_x = 2 * my_y - 1, 2 * my_h - 1
    to_y, to_x = gy + step_y, gx + step_x
    has_y = jnp.logical_and(to_y >= 0, to_y < n_gy)
    core = lax.rem(gx, 2)
    early = lax.rem(gx // 2, 2) == 0
    near_x, far_x = gx + 1 - 2 * core, gx - 1 + 2 * core
    has_far = jnp.logical_and(far_x >= 0, far_x < n_gx)
    sends_far = my_h == core
    early_far = jnp.logical_and(has_far, early)
    late_far = jnp.logical_and(has_far, jnp.logical_not(early))

    at_gain = RANK * V * PLANE // V
    pulls = [
        (dist_hbm, dist), (wall_hbm, wall), (inflow_hbm, inflow),
        (left_hbm, raw.at[pl.ds(0, at_gain)]), (right_hbm, raw.at[pl.ds(at_gain, at_gain)]),
        (loss_hbm, raw.at[pl.ds(2 * at_gain, PLANE)]), (place_hbm, place), (reverse_hbm, reverse),
        (xf_hbm, xf), (pf_hbm, pf), (xi_hbm, xi), (pi_hbm, pi), (unplace_hbm, unplace), (side_hbm, side),
        (courants_hbm.at[me], courants), (xs_hbm.at[me], xs),
    ]
    pulls = [pltpu.make_async_copy(a, b, local_sem.at[i]) for i, (a, b) in enumerate(pulls)]
    for pull in pulls:
        pull.start()

    for k in range(2):
        @pl.when(gx == k * (n_gx - 1))
        def _(k=k):
            from_x[k] = jnp.zeros((2, EDGE, LANES), F32)

        @pl.when(gy == k * (n_gy - 1))
        def _(k=k):
            from_y[k] = jnp.zeros((2, BLOCK, LANES), F32)

    barrier = pltpu.get_barrier_semaphore()

    def greet(x, y, v):
        pl.semaphore_signal(barrier, inc=1, device_id=(x, y, v), device_id_type=MESH)

    for d in range(1, GROUPS):
        greet(gx, gy, lax.rem(me + d, GROUPS))
    for step in (-1, 1):
        @pl.when(jnp.logical_and(gy + step >= 0, gy + step < n_gy))
        def _(step=step):
            for h in range(2):
                greet(gx, gy + step, 2 * h + (1 if step < 0 else 0))

    for y in range(2):
        greet(near_x, gy, y + 2 * core)

    @pl.when(early_far)
    def _():
        for v in range(GROUPS):
            greet(far_x, gy, v)

    for i in range(3):
        pulls[i].wait()
    for x in range(NX):
        for r in range(ROWS):
            at = (x * ROWS + r) * NY
            dense[at : at + NY, :] = dist[x, :, r * LANES : (r + 1) * LANES]
    for v in range(GROUPS):
        y, h = v % 2, v // 2
        send[v, pl.ds(48, 8)] = jnp.zeros((8, LANES), F32)
        for cell in range(2):
            x = 3 * h + (1 - 2 * h) * cell
            kind = jnp.full((ROWS, LANES), kinds_ref[y, x], jnp.int32)
            own_state = dense[pl.ds(x * 2 * ROWS + y, ROWS, stride=2), :]
            state = jnp.where(kind == 1, wall[...], jnp.where(kind == 2, inflow[...], own_state))
            send[v, pl.ds(cell * ROWS, ROWS)] = state
    recv[me] = send[me]
    for y in range(NY):
        edge[pl.ds(y * ROWS, ROWS)] = send[2 * core + y, pl.ds(0, ROWS)]
    edge[pl.ds(2 * ROWS, BLOCK - 2 * ROWS)] = jnp.zeros((BLOCK - 2 * ROWS, LANES), F32)

    awaited = GROUPS - 1 + jnp.where(has_y, GROUPS, 0) + jnp.where(sends_far, 0, GROUPS)
    pl.semaphore_wait(barrier, awaited + jnp.where(late_far, GROUPS, 0))

    push_raw = pltpu.make_async_remote_copy(
        src_ref=edge, dst_ref=far_raw.at[me], send_sem=send_raw.at[0], recv_sem=recv_raw.at[me],
        device_id=(far_x, gy, me), device_id_type=MESH,
    )

    @pl.when(late_far)
    def _():
        push_raw.start()

    first = []
    for d in range(1, GROUPS):
        to = lax.rem(me + d, GROUPS)
        first.append(
            pltpu.make_async_remote_copy(
                src_ref=send.at[to], dst_ref=recv.at[me], send_sem=send1.at[d], recv_sem=recv1.at[d],
                device_id=(gx, gy, to), device_id_type=MESH,
            )
        )
        first[-1].start()

    @pl.when(late_far)
    def _():
        for y in range(2):
            pl.semaphore_signal(
                ready, inc=1, device_id=(far_x, gy, y + 2 * (1 - core)), device_id_type=MESH
            )

    for i in range(3, 8):
        pulls[i].wait()
    packed[...] = jnp.zeros_like(packed)
    for ky in range(V):
        at = (ky // PACK) * LANES + (ky % PACK) * V
        packed[:, at : at + V] = raw[pl.ds(ky, TABLES * V, stride=V), :]
    hi, lo = halves(packed[...])
    both = jnp.concatenate([hi, lo], axis=0)
    for s in range(4):
        q = dot(both, wide(place, 2 * s, 2))
        quads[s] = q[: TABLES * V] + q[TABLES * V :]

    def symmetrise(t, _):
        at = pl.ds(pl.multiple_of(t * V, 8), V)
        for s in range(4):
            hi, lo = halves(quads[3 - s, at])
            mirrored = dot(reverse[...], jnp.concatenate([hi, lo], axis=0))[:V]
            table[s, at] = quads[s, at] + mirrored
        return 0

    lax.fori_loop(0, TABLES, symmetrise, 0)

    pulls[13].wait()
    for r in range(ROWS):
        for k in range(2):
            sides[k, r : r + 1, :] = side[k : k + 1, r * LANES : (r + 1) * LANES]

    for i in range(8, 13):
        pulls[i].wait()
    for d in range(1, GROUPS):
        first[d - 1].wait_recv()

    def gather_cells(blocks):
        for u in range(GROUPS):
            for c in range(CHUNKS):
                field[6 * u : 6 * u + 6, c * LANES : (c + 1) * LANES] = blocks[u, pl.ds(c, 6, stride=CHUNKS), :]
        return jnp.concatenate([field[:, :PLANE], field[:, PLANE:]], axis=0)

    def forward(cells):
        hi, lo = halves(cells)
        along_x = dot(wide(xf, 0, 2, 6 * V), jnp.concatenate([hi, lo, hi], axis=0))
        hi, lo = halves(along_x)
        both = jnp.concatenate([hi, lo], axis=0)
        parts = []
        for c in range(4):
            top = dot(both, wide(pf.at[0], 2 * c, 2))
            parts.append(top[: 2 * V] + top[2 * V :] + dot(hi, wide(pf.at[1], 2 * c, 2)))
        cc, cs, sc, ss = parts
        swapped = lambda a: jnp.concatenate([a[V:], -a[:V]], axis=0)
        return quadrants(cc, swapped(cs), swapped(sc), -ss)

    def collide(cells, spectrum, along_x, rows):
        for t in range(TABLES):
            at = slice(t * V, (t + 1) * V)
            a = []
            for s in range(4):
                m = table[s, at]
                a.append(jnp.concatenate([spectrum[s][:V] * m, spectrum[s][V:] * m], axis=0))
            for c, b in enumerate(quadrants_to_classes(*a)):
                hi, lo = halves(b)
                z = dot(wide(along_x.at[c], 0, 2, 6 * V), jnp.concatenate([hi, lo, hi], axis=0))
                hi, lo = halves(z)
                shaped_hi[c, t * rows : (t + 1) * rows] = hi
                shaped_lo[c, t * rows : (t + 1) * rows] = lo
        used = slice(0, TABLES * rows)
        for c in range(4):
            top, low = wide(pi.at[0, c], 0, 2), wide(pi.at[1, c], 0, 2)
            hi, lo = shaped_hi[c, used], shaped_lo[c, used]
            planes[c, used] = dot(hi, top) + dot(lo, top) + dot(hi, low)

        def fields(t):
            return quadrants(*(planes[c, t * rows : (t + 1) * rows] for c in range(4)))

        gain = [0.0] * 4
        for r in range(RANK):
            gain = [g + a * b for g, a, b in zip(gain, fields(r), fields(RANK + r))]
        rates = jnp.concatenate(
            [jnp.concatenate(list(gain), axis=1), jnp.concatenate(list(fields(2 * RANK)), axis=1)], axis=0
        )
        hi, lo = halves(rates)
        rates = dot(jnp.concatenate([hi, lo], axis=0), wide(unplace, 0, 5, PLANE))
        rates = rates[: 2 * rows] + rates[2 * rows :]
        return cells + COLLISION_STEP * (rates[:rows] - cells * rates[rows:])

    cells = gather_cells(recv)
    result = collide(cells, forward(cells), xi, 2 * V)
    collided[:, :PLANE] = result[:V]
    collided[:, PLANE:] = result[V:]
    for u in range(GROUPS):
        back[u, pl.ds(48, 8)] = jnp.zeros((8, LANES), F32)
        for c in range(CHUNKS):
            back[u, pl.ds(c, 6, stride=CHUNKS), :] = collided[6 * u : 6 * u + 6, c * LANES : (c + 1) * LANES]

    def push_x(u):
        return pltpu.make_async_remote_copy(
            src_ref=back.at[u, pl.ds(0, EDGE)], dst_ref=from_x.at[1 - my_h, my_y],
            send_sem=send_x.at[u], recv_sem=recv_x.at[1 - my_h, my_y],
            device_id=(to_x, gy, u), device_id_type=MESH,
        )

    def push_y(u):
        return pltpu.make_async_remote_copy(
            src_ref=back.at[u], dst_ref=from_y.at[1 - my_y, my_h],
            send_sem=send_y.at[u], recv_sem=recv_y.at[1 - my_y, my_h],
            device_id=(gx, to_y, u), device_id_type=MESH,
        )

    def push_own(d):
        to = lax.rem(me + d, GROUPS)
        return pltpu.make_async_remote_copy(
            src_ref=back.at[to], dst_ref=own.at[me], send_sem=send_own.at[d], recv_sem=recv_own.at[d],
            device_id=(gx, gy, to), device_id_type=MESH,
        )

    @pl.when(jnp.logical_not(sends_far))
    def _():
        for u in range(GROUPS):
            push_x(u).start()

    @pl.when(has_y)
    def _():
        for u in range(GROUPS):
            push_y(u).start()

    for d in range(1, GROUPS):
        push_own(d).start()
    own[me] = back[me]

    @pl.when(jnp.logical_and(early_far, sends_far))
    def _():
        pl.semaphore_wait(ready, GROUPS)
        for u in range(GROUPS):
            push_x(u).start()

    pulls[14].wait()
    for d in range(1, GROUPS):
        push_own(d).wait_recv()
    for step in (-1, 1):
        k = 0 if step < 0 else 1

        @pl.when(jnp.logical_and(gy + step >= 0, gy + step < n_gy))
        def _(k=k):
            for h in range(2):
                pltpu.make_async_remote_copy(
                    src_ref=back.at[0], dst_ref=from_y.at[k, h], send_sem=send_y.at[0], recv_sem=recv_y.at[k, h],
                    device_id=(gx, to_y, me), device_id_type=MESH,
                ).wait_recv()

    def wait_x(k):
        for y in range(2):
            pltpu.make_async_remote_copy(
                src_ref=back.at[0, pl.ds(0, EDGE)], dst_ref=from_x.at[k, y], send_sem=send_x.at[0],
                recv_sem=recv_x.at[k, y], device_id=(near_x, gy, me), device_id_type=MESH,
            ).wait_recv()

    wait_x(1 - core)

    @pl.when(late_far)
    def _():
        wait_x(core)

    def share_raw(d):
        return pltpu.make_async_remote_copy(
            src_ref=far_raw.at[me], dst_ref=far_raw.at[me], send_sem=send_raw.at[d], recv_sem=recv_raw.at[me],
            device_id=(gx, gy, lax.rem(me + d, GROUPS)), device_id_type=MESH,
        )

    pulls[15].wait()

    @pl.when(early_far)
    def _():
        push_raw.wait_recv()
        for d in range(1, GROUPS):
            share_raw(d).start()
        for d in range(1, GROUPS):
            peer = lax.rem(me + d, GROUPS)
            pltpu.make_async_remote_copy(
                src_ref=edge, dst_ref=far_raw.at[peer], send_sem=send_raw.at[d], recv_sem=recv_raw.at[peer],
                device_id=(gx, gy, peer), device_id_type=MESH,
            ).wait_recv()
        spectrum = forward(gather_cells(far_raw))
        for c in range(CHUNKS):
            collided[:6, c * LANES : (c + 1) * LANES] = far_raw[me, pl.ds(c, 6, stride=CHUNKS), :]
        far = jnp.concatenate([collided[:6, :PLANE], collided[:6, PLANE:], jnp.zeros((SOME - 12, PLANE), F32)], axis=0)
        far = collide(far, spectrum, xs, SOME)
        collided[:6, :PLANE] = far[:6]
        collided[:6, PLANE:] = far[6:12]
        for c in range(CHUNKS):
            far_done[pl.ds(c, 6, stride=CHUNKS), :] = collided[:6, c * LANES : (c + 1) * LANES]
        for y in range(NY):
            from_x[core, y, pl.ds(0, ROWS)] = far_done[pl.ds(y * ROWS, ROWS)]

    def at_cell(ref, x):
        cell = (0, 1, 1, 0)[x]
        return ref[pl.ds(cell * ROWS, ROWS), :]

    courant_x, courant_y = courants[0, pl.ds(0, ROWS)], courants[1, pl.ds(0, ROWS)]
    higher_x, higher_y = sides[0] == 1, sides[1] == 1
    centre = {(x, y): at_cell(own.at[y + 2 * (x // 2)], x) for x in range(NX) for y in range(NY)}
    for x in range(NX):
        for y in range(NY):
            here = centre[x, y]
            below_x = centre[x - 1, y] if x > 0 else from_x[0, y, pl.ds(0, ROWS)]
            above_x = centre[x + 1, y] if x < NX - 1 else from_x[1, y, pl.ds(0, ROWS)]
            below_y = centre[x, 0] if y > 0 else at_cell(from_y.at[0, x // 2], x)
            above_y = centre[x, 1] if y < 1 else at_cell(from_y.at[1, x // 2], x)
            up_x = jnp.where(higher_x, below_x, above_x)
            up_y = jnp.where(higher_y, below_y, above_y)
            out_ref[pl.ds(x * 2 * ROWS + y, ROWS, stride=2), :] = (
                here - courant_x * (here - up_x) - courant_y * (here - up_y)
            )

    for d in range(1, GROUPS):
        first[d - 1].wait_send()
        push_own(d).wait_send()

    @pl.when(has_y)
    def _():
        for u in range(GROUPS):
            push_y(u).wait_send()

    @pl.when(jnp.logical_or(jnp.logical_not(sends_far), early_far))
    def _():
        for u in range(GROUPS):
            push_x(u).wait_send()

    @pl.when(late_far)
    def _():
        push_raw.wait_send()

    @pl.when(early_far)
    def _():
        for d in range(1, GROUPS):
            share_raw(d).wait_send()


def spread(dense, out_ref):
    for x in range(NX):
        for r in range(ROWS):
            at = (x * ROWS + r) * NY
            out_ref[x, :, r * LANES : (r + 1) * LANES] = dense[at : at + NY, :]


def quadrants_to_classes(pp, pm, mp, mm):
    a, b = pp + pm, pp - pm
    c, d = mp + mm, mp - mm
    return a + c, b + d, a - c, b - d


def on_device(sizes, distribution, cell_types, wall_state, inflow_state, upwind_side, gain_left, gain_right, loss_table):
    tables = constants()
    tables = [jnp.asarray(tables[name]) for name in NAMES]
    operands = [
        distribution,
        cell_types.T,
        wall_state.reshape(ROWS, LANES),
        inflow_state.reshape(ROWS, LANES),
        upwind_side,
        gain_left.reshape(RANK * PLANE, V),
        gain_right.reshape(RANK * PLANE, V),
        loss_table.reshape(PLANE, V),
        *tables,
    ]
    spaces = [pl.BlockSpec(memory_space=pl.ANY)] * len(operands)
    spaces[1] = pl.BlockSpec(memory_space=pltpu.SMEM)
    dma = pltpu.SemaphoreType.DMA
    held = [
        pltpu.VMEM((NX, NY, SLAB), F32),
        pltpu.VMEM((NX * NY * ROWS, LANES), F32),
        pltpu.VMEM((ROWS, LANES), F32),
        pltpu.VMEM((ROWS, LANES), F32),
        pltpu.VMEM((2, SLAB), jnp.int32),
        pltpu.VMEM((TABLES * PLANE, V), F32),
        *(pltpu.VMEM(t.shape, t.dtype) for t in tables[:-2]),
        *(pltpu.VMEM(t.shape[1:], t.dtype) for t in tables[-2:]),
        pltpu.VMEM((2, ROWS, LANES), jnp.int32),
        pltpu.VMEM((TABLES * V, GROUPED), F32),
        pltpu.VMEM((4, TABLES * V, W), F32),
        pltpu.VMEM((4, TABLES * V, W), F32),
        pltpu.VMEM((GROUPS, BLOCK, LANES), F32),
        pltpu.VMEM((GROUPS, BLOCK, LANES), F32),
        pltpu.VMEM((V, 2 * PLANE), F32),
        pltpu.VMEM((4, TABLES * 2 * V, W), BF16),
        pltpu.VMEM((4, TABLES * 2 * V, W), BF16),
        pltpu.VMEM((4, TABLES * 2 * V, W), F32),
        pltpu.VMEM((V, 2 * PLANE), F32),
        pltpu.VMEM((GROUPS, BLOCK, LANES), F32),
        pltpu.VMEM((GROUPS, BLOCK, LANES), F32),
        pltpu.VMEM((2, 2, BLOCK, LANES), F32),
        pltpu.VMEM((2, 2, EDGE, LANES), F32),
        pltpu.VMEM((BLOCK, LANES), F32),
        pltpu.VMEM((GROUPS, BLOCK, LANES), F32),
        pltpu.VMEM((BLOCK, LANES), F32),
        dma((16,)),
        dma((GROUPS,)), dma((GROUPS,)),
        dma((GROUPS,)), dma((GROUPS,)),
        dma((GROUPS,)), dma((2, 2)),
        dma((GROUPS,)), dma((2, 2)),
        dma((GROUPS,)), dma((GROUPS,)),
        pltpu.SemaphoreType.REGULAR,
    ]
    dense = pl.pallas_call(
        functools.partial(kernel, sizes),
        out_shape=pltpu.VMEM((NX * NY * ROWS, LANES), F32),
        in_specs=spaces,
        out_specs=pl.BlockSpec(memory_space=pltpu.VMEM),
        scratch_shapes=held,
        compiler_params=pltpu.CompilerParams(
            collective_id=0, has_side_effects=True, vmem_limit_bytes=60 * 1024 * 1024
        ),
        cost_estimate=pl.CostEstimate(flops=3_000_000_000, bytes_accessed=10_000_000, transcendentals=0),
        name="step",
    )(*operands)
    return pl.pallas_call(
        spread,
        out_shape=jax.ShapeDtypeStruct((NX, NY, SLAB), F32),
        in_specs=[pl.BlockSpec(memory_space=pltpu.VMEM)],
        out_specs=pl.BlockSpec(memory_space=pltpu.VMEM),
        name="spread",
    )(pltpu.with_memory_space_constraint(dense, pltpu.VMEM))


def solution(mesh):
    placed = (
        P("gx", "gy", "vert"),
        P("gx", "gy"),
        P("vert"),
        P("vert"),
        P(None, "vert"),
        P(),
        P(),
        P(),
    )
    sizes = (mesh.shape["gx"], mesh.shape["gy"])
    return jax.shard_map(
        functools.partial(on_device, sizes),
        mesh=mesh,
        in_specs=placed,
        out_specs=P("gx", "gy", "vert"),
        check_vma=False,
    )
```

```python
import functools

import jax
import jax.numpy as jnp
import ml_dtypes
import numpy as np
from jax import lax
from jax.experimental import pallas as pl
from jax.experimental.pallas import tpu as pltpu
from jax.sharding import PartitionSpec as P

MESH = pl.DeviceIdType.MESH
F32 = jnp.float32
BF16 = jnp.bfloat16

V = 24
PLANE = V * V
HALF = V // 2
RANK = 4
TABLES = 2 * RANK + 1
GROUPS = 4
NX, NY = 4, 2
SLAB = PLANE * V // GROUPS
LANES = 128
ROWS = SLAB // LANES
BLOCK = 56
EDGE = 32
PAIRS = 3
SOME = 16
CHUNKS = 2 * PLANE // LANES
W = 256
PACK = 5
GROUPED = 5 * LANES
SIGNS = ((1, 1), (1, -1), (-1, 1), (-1, -1))
COLLISION_STEP = 0.25
COURANT = 0.45


def split_constant(a):
    hi = a.astype(ml_dtypes.bfloat16)
    lo = (a - hi.astype(np.float64)).astype(ml_dtypes.bfloat16)
    return hi, lo


def chunked(a):
    pad = -a.shape[-1] % LANES
    a = np.pad(a, [(0, 0)] * (a.ndim - 1) + [(0, pad)])
    a = a.reshape(*a.shape[:-1], -1, LANES)
    return np.ascontiguousarray(np.moveaxis(a, -2, -3))


def stacked(a):
    hi, lo = split_constant(a)
    return chunked(np.concatenate([hi, hi, lo], axis=1))


@functools.cache
def constants():
    step = 2.0 * np.pi / V
    inner = [(a, b) for a in range(1, HALF) for b in range(1, HALF)]
    outer = [(a, b) for a in range(HALF + 1) for b in range(HALF + 1) if a % HALF == 0 or b % HALF == 0]
    points = np.array(inner + outer)
    count = len(points)
    qy, qz = points[:, 0], points[:, 1]
    natural = np.arange(PLANE)
    ny, nz = natural // V, natural % V
    trig = (np.cos, np.sin)
    classes = ((0, 0), (0, 1), (1, 0), (1, 1))

    def grid(rows_y, rows_z, cy, cz):
        by = trig[cy](step * (rows_y[:, None] * qy[None, :] % V))
        bz = trig[cz](step * (rows_z[:, None] * qz[None, :] % V))
        return by * bz

    plane_forward = np.zeros((PLANE, 4 * W))
    plane_inverse = np.zeros((4, W, W))
    weight = np.where(qy % HALF == 0, 0.5, 1.0) * np.where(qz % HALF == 0, 0.5, 1.0) / PLANE
    for c, (cy, cz) in enumerate(classes):
        plane_forward[:, c * W : c * W + count] = grid(ny, nz, cy, cz)
        plane_inverse[c, :count, :count] = weight[:, None] * grid(qy, qz, cy, cz)

    place = np.zeros((GROUPED, 4 * W))
    unplace = np.zeros((4 * W, PLANE))
    seen = set()
    for s, (sy, sz) in enumerate(SIGNS):
        for q in range(count):
            y, z = sy * qy[q] % V, sz * qz[q] % V
            place[(y // PACK) * LANES + (y % PACK) * V + z, s * W + q] = 1.0
            if (y, z) not in seen:
                seen.add((y, z))
                unplace[s * W + q, y * V + z] = 1.0

    row_of = np.zeros((2, V), dtype=int)
    for jx in range(V):
        pair, odd = jx // 2, jx % 2
        u, q = pair // PAIRS, pair % PAIRS
        for cell in range(2):
            row_of[cell, jx] = odd * V + 2 * PAIRS * u + PAIRS * cell + q
    k = np.arange(V)
    theta = step * (k[:, None] * k[None, :] % V)
    cos, sin = np.cos(theta), np.sin(theta)
    x_forward = np.zeros((2 * V, 2 * V))
    x_forward[:V, row_of[0]] = cos
    x_forward[:V, row_of[1]] = sin
    x_forward[V:, row_of[0]] = -sin
    x_forward[V:, row_of[1]] = cos
    real = np.concatenate([cos, -sin], axis=1)
    imag = np.concatenate([sin, cos], axis=1)
    x_inverse, x_slab = [], [[] for _ in range(GROUPS)]
    for first, second in ((real, imag), (-imag, real), (-imag, real), (-real, -imag)):
        m = np.zeros((2 * V, 2 * V))
        m[row_of[0]] = first
        m[row_of[1]] = second
        m = m / (2 * V)
        x_inverse.append(stacked(m))
        for u in range(GROUPS):
            own = np.zeros((SOME, 2 * V))
            own[:6], own[6:12] = m[6 * u : 6 * u + 6], m[V + 6 * u : V + 6 * u + 6]
            x_slab[u].append(stacked(own))

    reverse = np.zeros((32, 2 * V))
    for r in range(V):
        reverse[r, (V - r) % V] = 1.0
        reverse[r, V + (V - r) % V] = 1.0

    velocity = np.arange(PLANE * V)
    courant_x = COURANT * np.abs(2 * (velocity // PLANE) - (V - 1)).astype(np.float32) / (V - 1)
    courant_y = COURANT * np.abs(2 * (velocity // V % V) - (V - 1)).astype(np.float32) / (V - 1)
    courants = np.zeros((GROUPS, 2, EDGE, LANES), np.float32)
    courants[:, 0, :ROWS] = courant_x.reshape(GROUPS, ROWS, LANES)
    courants[:, 1, :ROWS] = courant_y.reshape(GROUPS, ROWS, LANES)

    return {
        "x_forward": stacked(x_forward),
        "x_inverse": np.stack(x_inverse),
        "x_slab": np.stack([np.stack(a) for a in x_slab]),
        "plane_forward": chunked(np.stack(split_constant(plane_forward))),
        "plane_inverse": chunked(np.stack(split_constant(plane_inverse))),
        "place": chunked(place.astype(ml_dtypes.bfloat16)),
        "unplace": chunked(unplace.astype(ml_dtypes.bfloat16)),
        "reverse": reverse.astype(ml_dtypes.bfloat16),
        "courants": courants,
    }


NAMES = ("x_forward", "x_inverse", "plane_forward", "plane_inverse", "place", "unplace", "reverse", "x_slab", "courants")


def halves(a):
    hi = a.astype(BF16)
    lo = (a - hi.astype(F32)).astype(BF16)
    return hi, lo


def wide(ref, start, count, width=None):
    a = jnp.concatenate([ref[start + i] for i in range(count)], axis=1)
    return a if width is None else a[:, :width]


def dot(a, b):
    return jnp.dot(a, b, preferred_element_type=F32)


def quadrants(a, b, c, d):
    p, m = a + b, a - b
    q, r = c + d, c - d
    return p + q, m + r, p - q, m - r


def kernel(
    sizes,
    dist_hbm, kinds_hbm, wall_hbm, inflow_hbm, side_hbm, left_hbm, right_hbm, loss_hbm,
    xf_hbm, xi_hbm, pf_hbm, pi_hbm, place_hbm, unplace_hbm, reverse_hbm, xs_hbm, courants_hbm,
    out_ref,
    dist, dense, kinds, wall, inflow, side, raw, xf, xi, pf, pi, place, unplace, reverse, xs, courants,
    sides, packed, quads, table, send, recv, field, shaped_hi, shaped_lo, planes, collided, back, own, from_y, from_x, edge, far_raw, far_done,
    local_sem, send1, recv1, send_own, recv_own, send_y, recv_y, send_x, recv_x, send_raw, recv_raw, ready,
):
    n_gx, n_gy = sizes
    gx, gy, me = lax.axis_index("gx"), lax.axis_index("gy"), lax.axis_index("vert")
    my_y, my_h = lax.rem(me, 2), me // 2
    step_y, step_x = 2 * my_y - 1, 2 * my_h - 1
    to_y, to_x = gy + step_y, gx + step_x
    has_y = jnp.logical_and(to_y >= 0, to_y < n_gy)
    core = lax.rem(gx, 2)
    early = lax.rem(gx // 2, 2) == 0
    near_x, far_x = gx + 1 - 2 * core, gx - 1 + 2 * core
    has_far = jnp.logical_and(far_x >= 0, far_x < n_gx)
    sends_far = my_h == core
    early_far = jnp.logical_and(has_far, early)
    late_far = jnp.logical_and(has_far, jnp.logical_not(early))

    barrier = pltpu.get_barrier_semaphore()

    def greet(x, y, v):
        pl.semaphore_signal(barrier, inc=1, device_id=(x, y, v), device_id_type=MESH)

    @pl.when(early_far)
    def _():
        for v in range(GROUPS):
            greet(far_x, gy, v)

    for d in range(1, GROUPS):
        greet(gx, gy, lax.rem(me + d, GROUPS))
    for step in (-1, 1):
        @pl.when(jnp.logical_and(gy + step >= 0, gy + step < n_gy))
        def _(step=step):
            for h in range(2):
                greet(gx, gy + step, 2 * h + (1 if step < 0 else 0))

    for y in range(2):
        greet(near_x, gy, y + 2 * core)

    at_gain = RANK * V * PLANE // V
    pulls = [
        (dist_hbm, dist), (wall_hbm, wall), (inflow_hbm, inflow),
        (left_hbm, raw.at[pl.ds(0, at_gain)]), (right_hbm, raw.at[pl.ds(at_gain, at_gain)]),
        (loss_hbm, raw.at[pl.ds(2 * at_gain, PLANE)]), (place_hbm, place), (reverse_hbm, reverse),
        (xf_hbm, xf), (pf_hbm, pf), (xi_hbm, xi), (pi_hbm, pi), (unplace_hbm, unplace), (side_hbm, side),
        (courants_hbm.at[me], courants), (xs_hbm.at[me], xs), (kinds_hbm, kinds),
    ]
    pulls = [pltpu.make_async_copy(a, b, local_sem.at[i]) for i, (a, b) in enumerate(pulls)]
    for i in (0, 16, 1, 2, *range(3, 16)):
        pulls[i].start()

    @pl.when(jnp.logical_not(late_far))
    def _():
        from_x[core] = jnp.zeros((2, EDGE, LANES), F32)

    for k in range(2):
        @pl.when(gy == k * (n_gy - 1))
        def _(k=k):
            from_y[k] = jnp.zeros((2, BLOCK, LANES), F32)

    for i in (0, 1, 2, 16):
        pulls[i].wait()
    for x in range(NX):
        for r in range(ROWS):
            at = (x * ROWS + r) * NY
            dense[at : at + NY, :] = dist[x, :, r * LANES : (r + 1) * LANES]
    for v in range(GROUPS):
        y, h = v % 2, v // 2
        send[v, pl.ds(48, 8)] = jnp.zeros((8, LANES), F32)
        for cell in range(2):
            x = 3 * h + (1 - 2 * h) * cell
            kind = jnp.broadcast_to(kinds[y : y + 1, x : x + 1], (ROWS, LANES))
            own_state = dense[pl.ds(x * 2 * ROWS + y, ROWS, stride=2), :]
            state = jnp.where(kind == 1, wall[...], jnp.where(kind == 2, inflow[...], own_state))
            send[v, pl.ds(cell * ROWS, ROWS)] = state
    recv[me] = send[me]
    for y in range(NY):
        edge[pl.ds(y * ROWS, ROWS)] = send[2 * core + y, pl.ds(0, ROWS)]
    edge[pl.ds(2 * ROWS, BLOCK - 2 * ROWS)] = jnp.zeros((BLOCK - 2 * ROWS, LANES), F32)

    awaited = GROUPS - 1 + jnp.where(has_y, GROUPS, 0) + jnp.where(sends_far, 0, GROUPS)
    pl.semaphore_wait(barrier, awaited + jnp.where(late_far, GROUPS, 0))

    every = gy == n_gy // 8
    some = jnp.logical_or(every, gy < n_gy // 8)

    def push_raw(d):
        return pltpu.make_async_remote_copy(
            src_ref=edge, dst_ref=far_raw.at[me], send_sem=send_raw.at[d], recv_sem=recv_raw.at[me],
            device_id=(far_x, gy, lax.rem(me + d, GROUPS)), device_id_type=MESH,
        )

    def at_offsets(near, across, act):
        @pl.when(near)
        def _():
            for d in (1, 3):
                act(d)

        @pl.when(across)
        def _():
            act(2)

    unshared = jnp.logical_not(every), jnp.logical_not(some)

    @pl.when(late_far)
    def _():
        push_raw(0).start()
        at_offsets(every, some, lambda d: push_raw(d).start())

    first = []
    for d in range(1, GROUPS):
        to = lax.rem(me + d, GROUPS)
        first.append(
            pltpu.make_async_remote_copy(
                src_ref=send.at[to], dst_ref=recv.at[me], send_sem=send1.at[d], recv_sem=recv1.at[d],
                device_id=(gx, gy, to), device_id_type=MESH,
            )
        )
        first[-1].start()

    @pl.when(late_far)
    def _():
        for y in range(2):
            pl.semaphore_signal(
                ready, inc=1, device_id=(far_x, gy, y + 2 * (1 - core)), device_id_type=MESH
            )

    for i in range(3, 8):
        pulls[i].wait()
    packed[...] = jnp.zeros_like(packed)
    for ky in range(V):
        at = (ky // PACK) * LANES + (ky % PACK) * V
        packed[:, at : at + V] = raw[pl.ds(ky, TABLES * V, stride=V), :]
    hi, lo = halves(packed[...])
    both = jnp.concatenate([hi, lo], axis=0)
    for s in range(4):
        q = dot(both, wide(place, 2 * s, 2))
        quads[s] = q[: TABLES * V] + q[TABLES * V :]

    def symmetrise(t, _):
        at = pl.ds(pl.multiple_of(t * V, 8), V)
        for s in range(4):
            hi, lo = halves(quads[3 - s, at])
            mirrored = dot(reverse[...], jnp.concatenate([hi, lo], axis=0))[:V]
            table[s, at] = quads[s, at] + mirrored
        return 0

    lax.fori_loop(0, TABLES, symmetrise, 0)

    pulls[13].wait()
    for r in range(ROWS):
        for k in range(2):
            sides[k, r : r + 1, :] = side[k : k + 1, r * LANES : (r + 1) * LANES]

    for i in range(8, 13):
        pulls[i].wait()
    for d in range(1, GROUPS):
        first[d - 1].wait_recv()

    def gather_cells(blocks):
        for u in range(GROUPS):
            for c in range(CHUNKS):
                field[6 * u : 6 * u + 6, c * LANES : (c + 1) * LANES] = blocks[u, pl.ds(c, 6, stride=CHUNKS), :]
        return jnp.concatenate([field[:, :PLANE], field[:, PLANE:]], axis=0)

    def forward(cells):
        hi, lo = halves(cells)
        along_x = dot(wide(xf, 0, 2, 6 * V), jnp.concatenate([hi, lo, hi], axis=0))
        hi, lo = halves(along_x)
        both = jnp.concatenate([hi, lo], axis=0)
        parts = []
        for c in range(4):
            top = dot(both, wide(pf.at[0], 2 * c, 2))
            parts.append(top[: 2 * V] + top[2 * V :] + dot(hi, wide(pf.at[1], 2 * c, 2)))
        cc, cs, sc, ss = parts
        swapped = lambda a: jnp.concatenate([a[V:], -a[:V]], axis=0)
        return quadrants(cc, swapped(cs), swapped(sc), -ss)

    def collide(cells, spectrum, along_x, rows):
        for t in range(TABLES):
            at = slice(t * V, (t + 1) * V)
            a = []
            for s in range(4):
                m = table[s, at]
                a.append(jnp.concatenate([spectrum[s][:V] * m, spectrum[s][V:] * m], axis=0))
            for c, b in enumerate(quadrants_to_classes(*a)):
                hi, lo = halves(b)
                z = dot(wide(along_x.at[c], 0, 2, 6 * V), jnp.concatenate([hi, lo, hi], axis=0))
                hi, lo = halves(z)
                shaped_hi[c, t * rows : (t + 1) * rows] = hi
                shaped_lo[c, t * rows : (t + 1) * rows] = lo
        used = slice(0, TABLES * rows)
        for c in range(4):
            top, low = wide(pi.at[0, c], 0, 2), wide(pi.at[1, c], 0, 2)
            hi, lo = shaped_hi[c, used], shaped_lo[c, used]
            planes[c, used] = dot(hi, top) + dot(lo, top) + dot(hi, low)

        def fields(t):
            return quadrants(*(planes[c, t * rows : (t + 1) * rows] for c in range(4)))

        gain = [0.0] * 4
        for r in range(RANK):
            gain = [g + a * b for g, a, b in zip(gain, fields(r), fields(RANK + r))]
        rates = jnp.concatenate(
            [jnp.concatenate(list(gain), axis=1), jnp.concatenate(list(fields(2 * RANK)), axis=1)], axis=0
        )
        hi, lo = halves(rates)
        rates = dot(jnp.concatenate([hi, lo], axis=0), wide(unplace, 0, 5, PLANE))
        rates = rates[: 2 * rows] + rates[2 * rows :]
        return cells + COLLISION_STEP * (rates[:rows] - cells * rates[rows:])

    cells = gather_cells(recv)
    result = collide(cells, forward(cells), xi, 2 * V)
    collided[:, :PLANE] = result[:V]
    collided[:, PLANE:] = result[V:]
    for u in range(GROUPS):
        back[u, pl.ds(48, 8)] = jnp.zeros((8, LANES), F32)
        for c in range(CHUNKS):
            back[u, pl.ds(c, 6, stride=CHUNKS), :] = collided[6 * u : 6 * u + 6, c * LANES : (c + 1) * LANES]

    def push_x(u):
        return pltpu.make_async_remote_copy(
            src_ref=back.at[u, pl.ds(0, EDGE)], dst_ref=from_x.at[1 - my_h, my_y],
            send_sem=send_x.at[u], recv_sem=recv_x.at[1 - my_h, my_y],
            device_id=(to_x, gy, u), device_id_type=MESH,
        )

    def push_y(u):
        return pltpu.make_async_remote_copy(
            src_ref=back.at[u], dst_ref=from_y.at[1 - my_y, my_h],
            send_sem=send_y.at[u], recv_sem=recv_y.at[1 - my_y, my_h],
            device_id=(gx, to_y, u), device_id_type=MESH,
        )

    def push_own(d):
        to = lax.rem(me + d, GROUPS)
        return pltpu.make_async_remote_copy(
            src_ref=back.at[to], dst_ref=own.at[me], send_sem=send_own.at[d], recv_sem=recv_own.at[d],
            device_id=(gx, gy, to), device_id_type=MESH,
        )

    @pl.when(jnp.logical_not(sends_far))
    def _():
        for u in range(GROUPS):
            push_x(u).start()

    @pl.when(has_y)
    def _():
        for u in range(GROUPS):
            push_y(u).start()

    for d in range(1, GROUPS):
        push_own(d).start()
    own[me] = back[me]

    def push_far():
        pl.semaphore_wait(ready, GROUPS)
        for u in range(GROUPS):
            push_x(u).start()

    @pl.when(jnp.logical_and(early_far, sends_far))
    def _():
        push_far()

    def share_raw(d):
        return pltpu.make_async_remote_copy(
            src_ref=far_raw.at[me], dst_ref=far_raw.at[me], send_sem=send_raw.at[d], recv_sem=recv_raw.at[me],
            device_id=(gx, gy, lax.rem(me + d, GROUPS)), device_id_type=MESH,
        )

    @pl.when(early_far)
    def _():
        push_raw(0).wait_recv()
        at_offsets(*unshared, lambda d: share_raw(d).start())

    pulls[14].wait()
    for d in range(1, GROUPS):
        push_own(d).wait_recv()
    for step in (-1, 1):
        k = 0 if step < 0 else 1

        @pl.when(jnp.logical_and(gy + step >= 0, gy + step < n_gy))
        def _(k=k):
            for h in range(2):
                pltpu.make_async_remote_copy(
                    src_ref=back.at[0], dst_ref=from_y.at[k, h], send_sem=send_y.at[0], recv_sem=recv_y.at[k, h],
                    device_id=(gx, to_y, me), device_id_type=MESH,
                ).wait_recv()

    def wait_x(k):
        for y in range(2):
            pltpu.make_async_remote_copy(
                src_ref=back.at[0, pl.ds(0, EDGE)], dst_ref=from_x.at[k, y], send_sem=send_x.at[0],
                recv_sem=recv_x.at[k, y], device_id=(near_x, gy, me), device_id_type=MESH,
            ).wait_recv()

    wait_x(1 - core)

    @pl.when(late_far)
    def _():
        wait_x(core)

    def at_cell(ref, x):
        cell = (0, 1, 1, 0)[x]
        return ref[pl.ds(cell * ROWS, ROWS), :]

    courant_x, courant_y = courants[0, pl.ds(0, ROWS)], courants[1, pl.ds(0, ROWS)]
    higher_x, higher_y = sides[0] == 1, sides[1] == 1
    centre = {(x, y): at_cell(own.at[y + 2 * (x // 2)], x) for x in range(NX) for y in range(NY)}
    for x in range(NX):
        for y in range(NY):
            here = centre[x, y]
            below_x = centre[x - 1, y] if x > 0 else from_x[0, y, pl.ds(0, ROWS)]
            above_x = centre[x + 1, y] if x < NX - 1 else from_x[1, y, pl.ds(0, ROWS)]
            below_y = centre[x, 0] if y > 0 else at_cell(from_y.at[0, x // 2], x)
            above_y = centre[x, 1] if y < 1 else at_cell(from_y.at[1, x // 2], x)
            up_x = jnp.where(higher_x, below_x, above_x)
            up_y = jnp.where(higher_y, below_y, above_y)
            out_ref[pl.ds(x * 2 * ROWS + y, ROWS, stride=2), :] = (
                here - courant_x * (here - up_x) - courant_y * (here - up_y)
            )

    pulls[15].wait()

    @pl.when(early_far)
    def _():
        for d in range(1, GROUPS):
            peer = lax.rem(me + d, GROUPS)
            pltpu.make_async_remote_copy(
                src_ref=edge, dst_ref=far_raw.at[peer], send_sem=send_raw.at[d], recv_sem=recv_raw.at[peer],
                device_id=(gx, gy, peer), device_id_type=MESH,
            ).wait_recv()
        spectrum = forward(gather_cells(far_raw))
        for c in range(CHUNKS):
            collided[:6, c * LANES : (c + 1) * LANES] = far_raw[me, pl.ds(c, 6, stride=CHUNKS), :]
        far = jnp.concatenate([collided[:6, :PLANE], collided[:6, PLANE:], jnp.zeros((SOME - 12, PLANE), F32)], axis=0)
        far = collide(far, spectrum, xs, SOME)
        collided[:6, :PLANE] = far[:6]
        collided[:6, PLANE:] = far[6:12]
        for c in range(CHUNKS):
            far_done[pl.ds(c, 6, stride=CHUNKS), :] = collided[:6, c * LANES : (c + 1) * LANES]
        x = (NX - 1) * core
        for y in range(NY):
            at = pl.ds(x * NY * ROWS + y, ROWS, stride=NY)
            inward = courant_x * far_done[pl.ds(y * ROWS, ROWS)]
            out_ref[at, :] = out_ref[at, :] + jnp.where(sides[0] == 1 - core, inward, 0.0)

    for d in range(1, GROUPS):
        first[d - 1].wait_send()
        push_own(d).wait_send()

    @pl.when(has_y)
    def _():
        for u in range(GROUPS):
            push_y(u).wait_send()

    @pl.when(jnp.logical_or(jnp.logical_not(sends_far), early_far))
    def _():
        for u in range(GROUPS):
            push_x(u).wait_send()

    @pl.when(late_far)
    def _():
        push_raw(0).wait_send()
        at_offsets(every, some, lambda d: push_raw(d).wait_send())

    @pl.when(early_far)
    def _():
        at_offsets(*unshared, lambda d: share_raw(d).wait_send())


def spread(dense, out_ref):
    for x in range(NX):
        for r in range(ROWS):
            at = (x * ROWS + r) * NY
            out_ref[x, :, r * LANES : (r + 1) * LANES] = dense[at : at + NY, :]


def quadrants_to_classes(pp, pm, mp, mm):
    a, b = pp + pm, pp - pm
    c, d = mp + mm, mp - mm
    return a + c, b + d, a - c, b - d


def on_device(sizes, distribution, cell_types, wall_state, inflow_state, upwind_side, gain_left, gain_right, loss_table):
    tables = constants()
    tables = [jnp.asarray(tables[name]) for name in NAMES]
    operands = [
        distribution,
        cell_types.T,
        wall_state.reshape(ROWS, LANES),
        inflow_state.reshape(ROWS, LANES),
        upwind_side,
        gain_left.reshape(RANK * PLANE, V),
        gain_right.reshape(RANK * PLANE, V),
        loss_table.reshape(PLANE, V),
        *tables,
    ]
    spaces = [pl.BlockSpec(memory_space=pl.ANY)] * len(operands)
    dma = pltpu.SemaphoreType.DMA
    held = [
        pltpu.VMEM((NX, NY, SLAB), F32),
        pltpu.VMEM((NX * NY * ROWS, LANES), F32),
        pltpu.VMEM((NY, NX), jnp.int32),
        pltpu.VMEM((ROWS, LANES), F32),
        pltpu.VMEM((ROWS, LANES), F32),
        pltpu.VMEM((2, SLAB), jnp.int32),
        pltpu.VMEM((TABLES * PLANE, V), F32),
        *(pltpu.VMEM(t.shape, t.dtype) for t in tables[:-2]),
        *(pltpu.VMEM(t.shape[1:], t.dtype) for t in tables[-2:]),
        pltpu.VMEM((2, ROWS, LANES), jnp.int32),
        pltpu.VMEM((TABLES * V, GROUPED), F32),
        pltpu.VMEM((4, TABLES * V, W), F32),
        pltpu.VMEM((4, TABLES * V, W), F32),
        pltpu.VMEM((GROUPS, BLOCK, LANES), F32),
        pltpu.VMEM((GROUPS, BLOCK, LANES), F32),
        pltpu.VMEM((V, 2 * PLANE), F32),
        pltpu.VMEM((4, TABLES * 2 * V, W), BF16),
        pltpu.VMEM((4, TABLES * 2 * V, W), BF16),
        pltpu.VMEM((4, TABLES * 2 * V, W), F32),
        pltpu.VMEM((V, 2 * PLANE), F32),
        pltpu.VMEM((GROUPS, BLOCK, LANES), F32),
        pltpu.VMEM((GROUPS, BLOCK, LANES), F32),
        pltpu.VMEM((2, 2, BLOCK, LANES), F32),
        pltpu.VMEM((2, 2, EDGE, LANES), F32),
        pltpu.VMEM((BLOCK, LANES), F32),
        pltpu.VMEM((GROUPS, BLOCK, LANES), F32),
        pltpu.VMEM((BLOCK, LANES), F32),
        dma((17,)),
        dma((GROUPS,)), dma((GROUPS,)),
        dma((GROUPS,)), dma((GROUPS,)),
        dma((GROUPS,)), dma((2, 2)),
        dma((GROUPS,)), dma((2, 2)),
        dma((GROUPS,)), dma((GROUPS,)),
        pltpu.SemaphoreType.REGULAR,
    ]
    dense = pl.pallas_call(
        functools.partial(kernel, sizes),
        out_shape=pltpu.VMEM((NX * NY * ROWS, LANES), F32),
        in_specs=spaces,
        out_specs=pl.BlockSpec(memory_space=pltpu.VMEM),
        scratch_shapes=held,
        compiler_params=pltpu.CompilerParams(
            collective_id=0, has_side_effects=True, vmem_limit_bytes=60 * 1024 * 1024
        ),
        cost_estimate=pl.CostEstimate(flops=3_000_000_000, bytes_accessed=10_000_000, transcendentals=0),
        name="step",
    )(*operands)
    return pl.pallas_call(
        spread,
        out_shape=jax.ShapeDtypeStruct((NX, NY, SLAB), F32),
        in_specs=[pl.BlockSpec(memory_space=pltpu.VMEM)],
        out_specs=pl.BlockSpec(memory_space=pltpu.VMEM),
        name="spread",
    )(pltpu.with_memory_space_constraint(dense, pltpu.VMEM))


def solution(mesh):
    placed = (
        P("gx", "gy", "vert"),
        P("gx", "gy"),
        P("vert"),
        P("vert"),
        P(None, "vert"),
        P(),
        P(),
        P(),
    )
    sizes = (mesh.shape["gx"], mesh.shape["gy"])
    return jax.shard_map(
        functools.partial(on_device, sizes),
        mesh=mesh,
        in_specs=placed,
        out_specs=P("gx", "gy", "vert"),
        check_vma=False,
    )
```

```python
import functools

import jax
import jax.numpy as jnp
import ml_dtypes
import numpy as np
from jax import lax
from jax.experimental import pallas as pl
from jax.experimental.pallas import tpu as pltpu
from jax.sharding import PartitionSpec as P

MESH = pl.DeviceIdType.MESH
F32 = jnp.float32
BF16 = jnp.bfloat16

V = 24
PLANE = V * V
HALF = V // 2
RANK = 4
TABLES = 2 * RANK + 1
GROUPS = 4
NX, NY = 4, 2
SLAB = PLANE * V // GROUPS
LANES = 128
ROWS = SLAB // LANES
BLOCK = 56
EDGE = 32
PAIRS = 3
SOME = 16
CHUNKS = 2 * PLANE // LANES
W = 256
PACK = 5
GROUPED = 5 * LANES
SIGNS = ((1, 1), (1, -1), (-1, 1), (-1, -1))
COLLISION_STEP = 0.25
COURANT = 0.45


def split_constant(a):
    hi = a.astype(ml_dtypes.bfloat16)
    lo = (a - hi.astype(np.float64)).astype(ml_dtypes.bfloat16)
    return hi, lo


def chunked(a):
    pad = -a.shape[-1] % LANES
    a = np.pad(a, [(0, 0)] * (a.ndim - 1) + [(0, pad)])
    a = a.reshape(*a.shape[:-1], -1, LANES)
    return np.ascontiguousarray(np.moveaxis(a, -2, -3))


def stacked(a):
    hi, lo = split_constant(a)
    return chunked(np.concatenate([hi, hi, lo], axis=1))


@functools.cache
def constants():
    step = 2.0 * np.pi / V
    inner = [(a, b) for a in range(1, HALF) for b in range(1, HALF)]
    outer = [(a, b) for a in range(HALF + 1) for b in range(HALF + 1) if a % HALF == 0 or b % HALF == 0]
    points = np.array(inner + outer)
    count = len(points)
    qy, qz = points[:, 0], points[:, 1]
    natural = np.arange(PLANE)
    ny, nz = natural // V, natural % V
    trig = (np.cos, np.sin)
    classes = ((0, 0), (0, 1), (1, 0), (1, 1))

    def grid(rows_y, rows_z, cy, cz):
        by = trig[cy](step * (rows_y[:, None] * qy[None, :] % V))
        bz = trig[cz](step * (rows_z[:, None] * qz[None, :] % V))
        return by * bz

    plane_forward = np.zeros((PLANE, 4 * W))
    plane_inverse = np.zeros((4, W, W))
    weight = np.where(qy % HALF == 0, 0.5, 1.0) * np.where(qz % HALF == 0, 0.5, 1.0) / PLANE
    for c, (cy, cz) in enumerate(classes):
        plane_forward[:, c * W : c * W + count] = grid(ny, nz, cy, cz)
        plane_inverse[c, :count, :count] = weight[:, None] * grid(qy, qz, cy, cz)

    place = np.zeros((GROUPED, 4 * W))
    unplace = np.zeros((4 * W, PLANE))
    seen = set()
    for s, (sy, sz) in enumerate(SIGNS):
        for q in range(count):
            y, z = sy * qy[q] % V, sz * qz[q] % V
            place[(y // PACK) * LANES + (y % PACK) * V + z, s * W + q] = 1.0
            if (y, z) not in seen:
                seen.add((y, z))
                unplace[s * W + q, y * V + z] = 1.0

    row_of = np.zeros((2, V), dtype=int)
    for jx in range(V):
        pair, odd = jx // 2, jx % 2
        u, q = pair // PAIRS, pair % PAIRS
        for cell in range(2):
            row_of[cell, jx] = odd * V + 2 * PAIRS * u + PAIRS * cell + q
    k = np.arange(V)
    theta = step * (k[:, None] * k[None, :] % V)
    cos, sin = np.cos(theta), np.sin(theta)
    x_forward = np.zeros((2 * V, 2 * V))
    x_forward[:V, row_of[0]] = cos
    x_forward[:V, row_of[1]] = sin
    x_forward[V:, row_of[0]] = -sin
    x_forward[V:, row_of[1]] = cos
    real = np.concatenate([cos, -sin], axis=1)
    imag = np.concatenate([sin, cos], axis=1)
    x_inverse, x_slab = [], [[] for _ in range(GROUPS)]
    for first, second in ((real, imag), (-imag, real), (-imag, real), (-real, -imag)):
        m = np.zeros((2 * V, 2 * V))
        m[row_of[0]] = first
        m[row_of[1]] = second
        m = m / (2 * V)
        x_inverse.append(stacked(m))
        for u in range(GROUPS):
            own = np.zeros((SOME, 2 * V))
            own[:6], own[6:12] = m[6 * u : 6 * u + 6], m[V + 6 * u : V + 6 * u + 6]
            x_slab[u].append(stacked(own))

    reverse = np.zeros((32, 2 * V))
    for r in range(V):
        reverse[r, (V - r) % V] = 1.0
        reverse[r, V + (V - r) % V] = 1.0

    velocity = np.arange(PLANE * V)
    courant_x = COURANT * np.abs(2 * (velocity // PLANE) - (V - 1)).astype(np.float32) / (V - 1)
    courant_y = COURANT * np.abs(2 * (velocity // V % V) - (V - 1)).astype(np.float32) / (V - 1)
    courants = np.zeros((GROUPS, 2, EDGE, LANES), np.float32)
    courants[:, 0, :ROWS] = courant_x.reshape(GROUPS, ROWS, LANES)
    courants[:, 1, :ROWS] = courant_y.reshape(GROUPS, ROWS, LANES)

    return {
        "x_forward": stacked(x_forward),
        "x_inverse": np.stack(x_inverse),
        "x_slab": np.stack([np.stack(a) for a in x_slab]),
        "plane_forward": chunked(np.stack(split_constant(plane_forward))),
        "plane_inverse": chunked(np.stack(split_constant(plane_inverse))),
        "place": chunked(place.astype(ml_dtypes.bfloat16)),
        "unplace": chunked(unplace.astype(ml_dtypes.bfloat16)),
        "reverse": reverse.astype(ml_dtypes.bfloat16),
        "courants": courants,
    }


NAMES = ("x_forward", "x_inverse", "plane_forward", "plane_inverse", "place", "unplace", "reverse", "x_slab", "courants")


def halves(a):
    hi = a.astype(BF16)
    lo = (a - hi.astype(F32)).astype(BF16)
    return hi, lo


def wide(ref, start, count, width=None):
    a = jnp.concatenate([ref[start + i] for i in range(count)], axis=1)
    return a if width is None else a[:, :width]


def dot(a, b):
    return jnp.dot(a, b, preferred_element_type=F32)


def quadrants(a, b, c, d):
    p, m = a + b, a - b
    q, r = c + d, c - d
    return p + q, m + r, p - q, m - r


def kernel(
    sizes,
    dist_hbm, kinds_hbm, wall_hbm, inflow_hbm, side_hbm, left_hbm, right_hbm, loss_hbm,
    xf_hbm, xi_hbm, pf_hbm, pi_hbm, place_hbm, unplace_hbm, reverse_hbm, xs_hbm, courants_hbm,
    out_ref,
    dist, dense, kinds, wall, inflow, side, raw, xf, xi, pf, pi, place, unplace, reverse, xs, courants,
    sides, packed, quads, table, send, recv, field, shaped_hi, shaped_lo, planes, collided, back, own, from_y, from_x, edge, far_raw, far_done,
    local_sem, send1, recv1, send_own, recv_own, send_y, recv_y, send_x, recv_x, send_raw, recv_raw, ready,
):
    n_gx, n_gy = sizes
    gx, gy, me = lax.axis_index("gx"), lax.axis_index("gy"), lax.axis_index("vert")
    my_y, my_h = lax.rem(me, 2), me // 2
    step_y, step_x = 2 * my_y - 1, 2 * my_h - 1
    to_y, to_x = gy + step_y, gx + step_x
    has_y = jnp.logical_and(to_y >= 0, to_y < n_gy)
    core = lax.rem(gx, 2)
    early = lax.rem(gx // 2, 2) == 0
    near_x, far_x = gx + 1 - 2 * core, gx - 1 + 2 * core
    has_far = jnp.logical_and(far_x >= 0, far_x < n_gx)
    sends_far = my_h == core
    early_far = jnp.logical_and(has_far, early)
    late_far = jnp.logical_and(has_far, jnp.logical_not(early))

    barrier = pltpu.get_barrier_semaphore()

    def greet(x, y, v):
        pl.semaphore_signal(barrier, inc=1, device_id=(x, y, v), device_id_type=MESH)

    @pl.when(early_far)
    def _():
        for v in range(GROUPS):
            greet(far_x, gy, v)

    for d in range(1, GROUPS):
        greet(gx, gy, lax.rem(me + d, GROUPS))
    for step in (-1, 1):
        @pl.when(jnp.logical_and(gy + step >= 0, gy + step < n_gy))
        def _(step=step):
            for h in range(2):
                greet(gx, gy + step, 2 * h + (1 if step < 0 else 0))

    for y in range(2):
        greet(near_x, gy, y + 2 * core)

    at_gain = RANK * V * PLANE // V
    pulls = [
        (dist_hbm, dist), (wall_hbm, wall), (inflow_hbm, inflow),
        (left_hbm, raw.at[pl.ds(0, at_gain)]), (right_hbm, raw.at[pl.ds(at_gain, at_gain)]),
        (loss_hbm, raw.at[pl.ds(2 * at_gain, PLANE)]), (place_hbm, place), (reverse_hbm, reverse),
        (xf_hbm, xf), (pf_hbm, pf), (xi_hbm, xi), (pi_hbm, pi), (unplace_hbm, unplace), (side_hbm, side),
        (courants_hbm.at[me], courants), (xs_hbm.at[me], xs), (kinds_hbm, kinds),
    ]
    pulls = [pltpu.make_async_copy(a, b, local_sem.at[i]) for i, (a, b) in enumerate(pulls)]
    for i in (0, 16, 1, 2, *range(3, 16)):
        pulls[i].start()

    @pl.when(jnp.logical_not(late_far))
    def _():
        from_x[core] = jnp.zeros((2, EDGE, LANES), F32)

    for k in range(2):
        @pl.when(gy == k * (n_gy - 1))
        def _(k=k):
            from_y[k] = jnp.zeros((2, BLOCK, LANES), F32)

    for i in (0, 1, 2, 16):
        pulls[i].wait()
    for x in range(NX):
        for r in range(ROWS):
            at = (x * ROWS + r) * NY
            dense[at : at + NY, :] = dist[x, :, r * LANES : (r + 1) * LANES]
    for v in range(GROUPS):
        y, h = v % 2, v // 2
        send[v, pl.ds(48, 8)] = jnp.zeros((8, LANES), F32)
        for cell in range(2):
            x = 3 * h + (1 - 2 * h) * cell
            kind = jnp.broadcast_to(kinds[y : y + 1, x : x + 1], (ROWS, LANES))
            own_state = dense[pl.ds(x * 2 * ROWS + y, ROWS, stride=2), :]
            state = jnp.where(kind == 1, wall[...], jnp.where(kind == 2, inflow[...], own_state))
            send[v, pl.ds(cell * ROWS, ROWS)] = state
    recv[me] = send[me]
    for y in range(NY):
        edge[pl.ds(y * ROWS, ROWS)] = send[2 * core + y, pl.ds(0, ROWS)]
    edge[pl.ds(2 * ROWS, BLOCK - 2 * ROWS)] = jnp.zeros((BLOCK - 2 * ROWS, LANES), F32)

    awaited = GROUPS - 1 + jnp.where(has_y, GROUPS, 0) + jnp.where(sends_far, 0, GROUPS)
    pl.semaphore_wait(barrier, awaited + jnp.where(late_far, GROUPS, 0))

    receiver = jnp.where(early, core, 1 - core)
    every = jnp.logical_or(gy == n_gy // 8, jnp.logical_and(gy < n_gy // 8, receiver == 1))

    def push_raw(d):
        return pltpu.make_async_remote_copy(
            src_ref=edge, dst_ref=far_raw.at[me], send_sem=send_raw.at[d], recv_sem=recv_raw.at[me],
            device_id=(far_x, gy, lax.rem(me + d, GROUPS)), device_id_type=MESH,
        )

    def at_others(wanted, act):
        @pl.when(wanted)
        def _():
            for d in range(1, GROUPS):
                act(d)

    shared = jnp.logical_not(every)

    @pl.when(late_far)
    def _():
        push_raw(0).start()
        at_others(every, lambda d: push_raw(d).start())

    first = []
    for d in range(1, GROUPS):
        to = lax.rem(me + d, GROUPS)
        first.append(
            pltpu.make_async_remote_copy(
                src_ref=send.at[to], dst_ref=recv.at[me], send_sem=send1.at[d], recv_sem=recv1.at[d],
                device_id=(gx, gy, to), device_id_type=MESH,
            )
        )
        first[-1].start()

    @pl.when(late_far)
    def _():
        for y in range(2):
            pl.semaphore_signal(
                ready, inc=1, device_id=(far_x, gy, y + 2 * (1 - core)), device_id_type=MESH
            )

    for i in range(3, 8):
        pulls[i].wait()
    packed[...] = jnp.zeros_like(packed)
    for ky in range(V):
        at = (ky // PACK) * LANES + (ky % PACK) * V
        packed[:, at : at + V] = raw[pl.ds(ky, TABLES * V, stride=V), :]
    hi, lo = halves(packed[...])
    both = jnp.concatenate([hi, lo], axis=0)
    for s in range(4):
        q = dot(both, wide(place, 2 * s, 2))
        quads[s] = q[: TABLES * V] + q[TABLES * V :]

    def symmetrise(t, _):
        at = pl.ds(pl.multiple_of(t * V, 8), V)
        for s in range(4):
            hi, lo = halves(quads[3 - s, at])
            mirrored = dot(reverse[...], jnp.concatenate([hi, lo], axis=0))[:V]
            table[s, at] = quads[s, at] + mirrored
        return 0

    lax.fori_loop(0, TABLES, symmetrise, 0)

    pulls[13].wait()
    for r in range(ROWS):
        for k in range(2):
            sides[k, r : r + 1, :] = side[k : k + 1, r * LANES : (r + 1) * LANES]

    for i in range(8, 13):
        pulls[i].wait()
    for d in range(1, GROUPS):
        first[d - 1].wait_recv()

    def gather_cells(blocks):
        for u in range(GROUPS):
            for c in range(CHUNKS):
                field[6 * u : 6 * u + 6, c * LANES : (c + 1) * LANES] = blocks[u, pl.ds(c, 6, stride=CHUNKS), :]
        return jnp.concatenate([field[:, :PLANE], field[:, PLANE:]], axis=0)

    def forward(cells):
        hi, lo = halves(cells)
        along_x = dot(wide(xf, 0, 2, 6 * V), jnp.concatenate([hi, lo, hi], axis=0))
        hi, lo = halves(along_x)
        both = jnp.concatenate([hi, lo], axis=0)
        parts = []
        for c in range(4):
            top = dot(both, wide(pf.at[0], 2 * c, 2))
            parts.append(top[: 2 * V] + top[2 * V :] + dot(hi, wide(pf.at[1], 2 * c, 2)))
        cc, cs, sc, ss = parts
        swapped = lambda a: jnp.concatenate([a[V:], -a[:V]], axis=0)
        return quadrants(cc, swapped(cs), swapped(sc), -ss)

    def collide(cells, spectrum, along_x, rows):
        for t in range(TABLES):
            at = slice(t * V, (t + 1) * V)
            a = []
            for s in range(4):
                m = table[s, at]
                a.append(jnp.concatenate([spectrum[s][:V] * m, spectrum[s][V:] * m], axis=0))
            for c, b in enumerate(quadrants_to_classes(*a)):
                hi, lo = halves(b)
                z = dot(wide(along_x.at[c], 0, 2, 6 * V), jnp.concatenate([hi, lo, hi], axis=0))
                hi, lo = halves(z)
                shaped_hi[c, t * rows : (t + 1) * rows] = hi
                shaped_lo[c, t * rows : (t + 1) * rows] = lo
        used = slice(0, TABLES * rows)
        for c in range(4):
            top, low = wide(pi.at[0, c], 0, 2), wide(pi.at[1, c], 0, 2)
            hi, lo = shaped_hi[c, used], shaped_lo[c, used]
            planes[c, used] = dot(hi, top) + dot(lo, top) + dot(hi, low)

        def fields(t):
            return quadrants(*(planes[c, t * rows : (t + 1) * rows] for c in range(4)))

        gain = [0.0] * 4
        for r in range(RANK):
            gain = [g + a * b for g, a, b in zip(gain, fields(r), fields(RANK + r))]
        rates = jnp.concatenate(
            [jnp.concatenate(list(gain), axis=1), jnp.concatenate(list(fields(2 * RANK)), axis=1)], axis=0
        )
        hi, lo = halves(rates)
        rates = dot(jnp.concatenate([hi, lo], axis=0), wide(unplace, 0, 5, PLANE))
        rates = rates[: 2 * rows] + rates[2 * rows :]
        return cells + COLLISION_STEP * (rates[:rows] - cells * rates[rows:])

    cells = gather_cells(recv)
    result = collide(cells, forward(cells), xi, 2 * V)
    collided[:, :PLANE] = result[:V]
    collided[:, PLANE:] = result[V:]
    for u in range(GROUPS):
        back[u, pl.ds(48, 8)] = jnp.zeros((8, LANES), F32)
        for c in range(CHUNKS):
            back[u, pl.ds(c, 6, stride=CHUNKS), :] = collided[6 * u : 6 * u + 6, c * LANES : (c + 1) * LANES]

    def push_x(u):
        return pltpu.make_async_remote_copy(
            src_ref=back.at[u, pl.ds(0, EDGE)], dst_ref=from_x.at[1 - my_h, my_y],
            send_sem=send_x.at[u], recv_sem=recv_x.at[1 - my_h, my_y],
            device_id=(to_x, gy, u), device_id_type=MESH,
        )

    def push_y(u):
        return pltpu.make_async_remote_copy(
            src_ref=back.at[u], dst_ref=from_y.at[1 - my_y, my_h],
            send_sem=send_y.at[u], recv_sem=recv_y.at[1 - my_y, my_h],
            device_id=(gx, to_y, u), device_id_type=MESH,
        )

    def push_own(d):
        to = lax.rem(me + d, GROUPS)
        return pltpu.make_async_remote_copy(
            src_ref=back.at[to], dst_ref=own.at[me], send_sem=send_own.at[d], recv_sem=recv_own.at[d],
            device_id=(gx, gy, to), device_id_type=MESH,
        )

    @pl.when(jnp.logical_not(sends_far))
    def _():
        for u in range(GROUPS):
            push_x(u).start()

    @pl.when(has_y)
    def _():
        for u in range(GROUPS):
            push_y(u).start()

    for d in range(1, GROUPS):
        push_own(d).start()
    own[me] = back[me]

    def push_far():
        pl.semaphore_wait(ready, GROUPS)
        for u in range(GROUPS):
            push_x(u).start()

    @pl.when(jnp.logical_and(early_far, sends_far))
    def _():
        push_far()

    def share_raw(d):
        return pltpu.make_async_remote_copy(
            src_ref=far_raw.at[me], dst_ref=far_raw.at[me], send_sem=send_raw.at[d], recv_sem=recv_raw.at[me],
            device_id=(gx, gy, lax.rem(me + d, GROUPS)), device_id_type=MESH,
        )

    @pl.when(early_far)
    def _():
        push_raw(0).wait_recv()
        at_others(shared, lambda d: share_raw(d).start())

    pulls[14].wait()
    for d in range(1, GROUPS):
        push_own(d).wait_recv()
    for step in (-1, 1):
        k = 0 if step < 0 else 1

        @pl.when(jnp.logical_and(gy + step >= 0, gy + step < n_gy))
        def _(k=k):
            for h in range(2):
                pltpu.make_async_remote_copy(
                    src_ref=back.at[0], dst_ref=from_y.at[k, h], send_sem=send_y.at[0], recv_sem=recv_y.at[k, h],
                    device_id=(gx, to_y, me), device_id_type=MESH,
                ).wait_recv()

    def wait_x(k):
        for y in range(2):
            pltpu.make_async_remote_copy(
                src_ref=back.at[0, pl.ds(0, EDGE)], dst_ref=from_x.at[k, y], send_sem=send_x.at[0],
                recv_sem=recv_x.at[k, y], device_id=(near_x, gy, me), device_id_type=MESH,
            ).wait_recv()

    wait_x(1 - core)

    @pl.when(late_far)
    def _():
        wait_x(core)

    def at_cell(ref, x):
        cell = (0, 1, 1, 0)[x]
        return ref[pl.ds(cell * ROWS, ROWS), :]

    courant_x, courant_y = courants[0, pl.ds(0, ROWS)], courants[1, pl.ds(0, ROWS)]
    higher_x, higher_y = sides[0] == 1, sides[1] == 1
    centre = {(x, y): at_cell(own.at[y + 2 * (x // 2)], x) for x in range(NX) for y in range(NY)}
    for x in range(NX):
        for y in range(NY):
            here = centre[x, y]
            below_x = centre[x - 1, y] if x > 0 else from_x[0, y, pl.ds(0, ROWS)]
            above_x = centre[x + 1, y] if x < NX - 1 else from_x[1, y, pl.ds(0, ROWS)]
            below_y = centre[x, 0] if y > 0 else at_cell(from_y.at[0, x // 2], x)
            above_y = centre[x, 1] if y < 1 else at_cell(from_y.at[1, x // 2], x)
            up_x = jnp.where(higher_x, below_x, above_x)
            up_y = jnp.where(higher_y, below_y, above_y)
            out_ref[pl.ds(x * 2 * ROWS + y, ROWS, stride=2), :] = (
                here - courant_x * (here - up_x) - courant_y * (here - up_y)
            )

    pulls[15].wait()

    @pl.when(early_far)
    def _():
        for d in range(1, GROUPS):
            peer = lax.rem(me + d, GROUPS)
            pltpu.make_async_remote_copy(
                src_ref=edge, dst_ref=far_raw.at[peer], send_sem=send_raw.at[d], recv_sem=recv_raw.at[peer],
                device_id=(gx, gy, peer), device_id_type=MESH,
            ).wait_recv()
        spectrum = forward(gather_cells(far_raw))
        for c in range(CHUNKS):
            collided[:6, c * LANES : (c + 1) * LANES] = far_raw[me, pl.ds(c, 6, stride=CHUNKS), :]
        far = jnp.concatenate([collided[:6, :PLANE], collided[:6, PLANE:], jnp.zeros((SOME - 12, PLANE), F32)], axis=0)
        far = collide(far, spectrum, xs, SOME)
        collided[:6, :PLANE] = far[:6]
        collided[:6, PLANE:] = far[6:12]
        for c in range(CHUNKS):
            far_done[pl.ds(c, 6, stride=CHUNKS), :] = collided[:6, c * LANES : (c + 1) * LANES]
        x = (NX - 1) * core
        for y in range(NY):
            at = pl.ds(x * NY * ROWS + y, ROWS, stride=NY)
            inward = courant_x * far_done[pl.ds(y * ROWS, ROWS)]
            out_ref[at, :] = out_ref[at, :] + jnp.where(sides[0] == 1 - core, inward, 0.0)

    for d in range(1, GROUPS):
        first[d - 1].wait_send()
        push_own(d).wait_send()

    @pl.when(has_y)
    def _():
        for u in range(GROUPS):
            push_y(u).wait_send()

    @pl.when(jnp.logical_or(jnp.logical_not(sends_far), early_far))
    def _():
        for u in range(GROUPS):
            push_x(u).wait_send()

    @pl.when(late_far)
    def _():
        push_raw(0).wait_send()
        at_others(every, lambda d: push_raw(d).wait_send())

    @pl.when(early_far)
    def _():
        at_others(shared, lambda d: share_raw(d).wait_send())


def spread(dense, out_ref):
    for x in range(NX):
        for r in range(ROWS):
            at = (x * ROWS + r) * NY
            out_ref[x, :, r * LANES : (r + 1) * LANES] = dense[at : at + NY, :]


def quadrants_to_classes(pp, pm, mp, mm):
    a, b = pp + pm, pp - pm
    c, d = mp + mm, mp - mm
    return a + c, b + d, a - c, b - d


def on_device(sizes, distribution, cell_types, wall_state, inflow_state, upwind_side, gain_left, gain_right, loss_table):
    tables = constants()
    tables = [jnp.asarray(tables[name]) for name in NAMES]
    operands = [
        distribution,
        cell_types.T,
        wall_state.reshape(ROWS, LANES),
        inflow_state.reshape(ROWS, LANES),
        upwind_side,
        gain_left.reshape(RANK * PLANE, V),
        gain_right.reshape(RANK * PLANE, V),
        loss_table.reshape(PLANE, V),
        *tables,
    ]
    spaces = [pl.BlockSpec(memory_space=pl.ANY)] * len(operands)
    dma = pltpu.SemaphoreType.DMA
    held = [
        pltpu.VMEM((NX, NY, SLAB), F32),
        pltpu.VMEM((NX * NY * ROWS, LANES), F32),
        pltpu.VMEM((NY, NX), jnp.int32),
        pltpu.VMEM((ROWS, LANES), F32),
        pltpu.VMEM((ROWS, LANES), F32),
        pltpu.VMEM((2, SLAB), jnp.int32),
        pltpu.VMEM((TABLES * PLANE, V), F32),
        *(pltpu.VMEM(t.shape, t.dtype) for t in tables[:-2]),
        *(pltpu.VMEM(t.shape[1:], t.dtype) for t in tables[-2:]),
        pltpu.VMEM((2, ROWS, LANES), jnp.int32),
        pltpu.VMEM((TABLES * V, GROUPED), F32),
        pltpu.VMEM((4, TABLES * V, W), F32),
        pltpu.VMEM((4, TABLES * V, W), F32),
        pltpu.VMEM((GROUPS, BLOCK, LANES), F32),
        pltpu.VMEM((GROUPS, BLOCK, LANES), F32),
        pltpu.VMEM((V, 2 * PLANE), F32),
        pltpu.VMEM((4, TABLES * 2 * V, W), BF16),
        pltpu.VMEM((4, TABLES * 2 * V, W), BF16),
        pltpu.VMEM((4, TABLES * 2 * V, W), F32),
        pltpu.VMEM((V, 2 * PLANE), F32),
        pltpu.VMEM((GROUPS, BLOCK, LANES), F32),
        pltpu.VMEM((GROUPS, BLOCK, LANES), F32),
        pltpu.VMEM((2, 2, BLOCK, LANES), F32),
        pltpu.VMEM((2, 2, EDGE, LANES), F32),
        pltpu.VMEM((BLOCK, LANES), F32),
        pltpu.VMEM((GROUPS, BLOCK, LANES), F32),
        pltpu.VMEM((BLOCK, LANES), F32),
        dma((17,)),
        dma((GROUPS,)), dma((GROUPS,)),
        dma((GROUPS,)), dma((GROUPS,)),
        dma((GROUPS,)), dma((2, 2)),
        dma((GROUPS,)), dma((2, 2)),
        dma((GROUPS,)), dma((GROUPS,)),
        pltpu.SemaphoreType.REGULAR,
    ]
    dense = pl.pallas_call(
        functools.partial(kernel, sizes),
        out_shape=pltpu.VMEM((NX * NY * ROWS, LANES), F32),
        in_specs=spaces,
        out_specs=pl.BlockSpec(memory_space=pltpu.VMEM),
        scratch_shapes=held,
        compiler_params=pltpu.CompilerParams(
            collective_id=0, has_side_effects=True, vmem_limit_bytes=60 * 1024 * 1024
        ),
        cost_estimate=pl.CostEstimate(flops=3_000_000_000, bytes_accessed=10_000_000, transcendentals=0),
        name="step",
    )(*operands)
    return pl.pallas_call(
        spread,
        out_shape=jax.ShapeDtypeStruct((NX, NY, SLAB), F32),
        in_specs=[pl.BlockSpec(memory_space=pltpu.VMEM)],
        out_specs=pl.BlockSpec(memory_space=pltpu.VMEM),
        name="spread",
    )(pltpu.with_memory_space_constraint(dense, pltpu.VMEM))


def solution(mesh):
    placed = (
        P("gx", "gy", "vert"),
        P("gx", "gy"),
        P("vert"),
        P("vert"),
        P(None, "vert"),
        P(),
        P(),
        P(),
    )
    sizes = (mesh.shape["gx"], mesh.shape["gy"])
    return jax.shard_map(
        functools.partial(on_device, sizes),
        mesh=mesh,
        in_specs=placed,
        out_specs=P("gx", "gy", "vert"),
        check_vma=False,
    )
```

```python
import functools

import jax
import jax.numpy as jnp
import ml_dtypes
import numpy as np
from jax import lax
from jax.experimental import pallas as pl
from jax.experimental.pallas import tpu as pltpu
from jax.sharding import PartitionSpec as P

MESH = pl.DeviceIdType.MESH
F32 = jnp.float32
BF16 = jnp.bfloat16

V = 24
PLANE = V * V
HALF = V // 2
RANK = 4
TABLES = 2 * RANK + 1
GROUPS = 4
NX, NY = 4, 2
SLAB = PLANE * V // GROUPS
LANES = 128
ROWS = SLAB // LANES
BLOCK = 56
EDGE = 32
PAIRS = 3
SOME = 16
CHUNKS = 2 * PLANE // LANES
W = 256
PACK = 5
GROUPED = 5 * LANES
SIGNS = ((1, 1), (1, -1), (-1, 1), (-1, -1))
OTHERS = (2, 1, 3)
COLLISION_STEP = 0.25
COURANT = 0.45


def split_constant(a):
    hi = a.astype(ml_dtypes.bfloat16)
    lo = (a - hi.astype(np.float64)).astype(ml_dtypes.bfloat16)
    return hi, lo


def chunked(a):
    pad = -a.shape[-1] % LANES
    a = np.pad(a, [(0, 0)] * (a.ndim - 1) + [(0, pad)])
    a = a.reshape(*a.shape[:-1], -1, LANES)
    return np.ascontiguousarray(np.moveaxis(a, -2, -3))


def stacked(a):
    hi, lo = split_constant(a)
    return chunked(np.concatenate([hi, hi, lo], axis=1))


@functools.cache
def constants():
    step = 2.0 * np.pi / V
    inner = [(a, b) for a in range(1, HALF) for b in range(1, HALF)]
    outer = [(a, b) for a in range(HALF + 1) for b in range(HALF + 1) if a % HALF == 0 or b % HALF == 0]
    points = np.array(inner + outer)
    count = len(points)
    qy, qz = points[:, 0], points[:, 1]
    natural = np.arange(PLANE)
    ny, nz = natural // V, natural % V
    trig = (np.cos, np.sin)
    classes = ((0, 0), (0, 1), (1, 0), (1, 1))

    def grid(rows_y, rows_z, cy, cz):
        by = trig[cy](step * (rows_y[:, None] * qy[None, :] % V))
        bz = trig[cz](step * (rows_z[:, None] * qz[None, :] % V))
        return by * bz

    plane_forward = np.zeros((PLANE, 4 * W))
    plane_inverse = np.zeros((4, W, W))
    weight = np.where(qy % HALF == 0, 0.5, 1.0) * np.where(qz % HALF == 0, 0.5, 1.0) / PLANE
    for c, (cy, cz) in enumerate(classes):
        plane_forward[:, c * W : c * W + count] = grid(ny, nz, cy, cz)
        plane_inverse[c, :count, :count] = weight[:, None] * grid(qy, qz, cy, cz)

    place = np.zeros((GROUPED, 4 * W))
    unplace = np.zeros((4 * W, PLANE))
    seen = set()
    for s, (sy, sz) in enumerate(SIGNS):
        for q in range(count):
            y, z = sy * qy[q] % V, sz * qz[q] % V
            place[(y // PACK) * LANES + (y % PACK) * V + z, s * W + q] = 1.0
            if (y, z) not in seen:
                seen.add((y, z))
                unplace[s * W + q, y * V + z] = 1.0

    row_of = np.zeros((2, V), dtype=int)
    for jx in range(V):
        pair, odd = jx // 2, jx % 2
        u, q = pair // PAIRS, pair % PAIRS
        for cell in range(2):
            row_of[cell, jx] = odd * V + 2 * PAIRS * u + PAIRS * cell + q
    k = np.arange(V)
    theta = step * (k[:, None] * k[None, :] % V)
    cos, sin = np.cos(theta), np.sin(theta)
    x_forward = np.zeros((2 * V, 2 * V))
    x_forward[:V, row_of[0]] = cos
    x_forward[:V, row_of[1]] = sin
    x_forward[V:, row_of[0]] = -sin
    x_forward[V:, row_of[1]] = cos
    real = np.concatenate([cos, -sin], axis=1)
    imag = np.concatenate([sin, cos], axis=1)
    x_inverse, x_slab = [], [[] for _ in range(GROUPS)]
    for first, second in ((real, imag), (-imag, real), (-imag, real), (-real, -imag)):
        m = np.zeros((2 * V, 2 * V))
        m[row_of[0]] = first
        m[row_of[1]] = second
        m = m / (2 * V)
        x_inverse.append(stacked(m))
        for u in range(GROUPS):
            own = np.zeros((SOME, 2 * V))
            own[:6], own[6:12] = m[6 * u : 6 * u + 6], m[V + 6 * u : V + 6 * u + 6]
            x_slab[u].append(stacked(own))

    reverse = np.zeros((32, 2 * V))
    for r in range(V):
        reverse[r, (V - r) % V] = 1.0
        reverse[r, V + (V - r) % V] = 1.0

    velocity = np.arange(PLANE * V)
    courant_x = COURANT * np.abs(2 * (velocity // PLANE) - (V - 1)).astype(np.float32) / (V - 1)
    courant_y = COURANT * np.abs(2 * (velocity // V % V) - (V - 1)).astype(np.float32) / (V - 1)
    courants = np.zeros((GROUPS, 2, EDGE, LANES), np.float32)
    courants[:, 0, :ROWS] = courant_x.reshape(GROUPS, ROWS, LANES)
    courants[:, 1, :ROWS] = courant_y.reshape(GROUPS, ROWS, LANES)

    return {
        "x_forward": stacked(x_forward),
        "x_inverse": np.stack(x_inverse),
        "x_slab": np.stack([np.stack(a) for a in x_slab]),
        "plane_forward": chunked(np.stack(split_constant(plane_forward))),
        "plane_inverse": chunked(np.stack(split_constant(plane_inverse))),
        "place": chunked(place.astype(ml_dtypes.bfloat16)),
        "unplace": chunked(unplace.astype(ml_dtypes.bfloat16)),
        "reverse": reverse.astype(ml_dtypes.bfloat16),
        "courants": courants,
    }


NAMES = ("x_forward", "x_inverse", "plane_forward", "plane_inverse", "place", "unplace", "reverse", "x_slab", "courants")


def halves(a):
    hi = a.astype(BF16)
    lo = (a - hi.astype(F32)).astype(BF16)
    return hi, lo


def wide(ref, start, count, width=None):
    a = jnp.concatenate([ref[start + i] for i in range(count)], axis=1)
    return a if width is None else a[:, :width]


def dot(a, b):
    return jnp.dot(a, b, preferred_element_type=F32)


def quadrants(a, b, c, d):
    p, m = a + b, a - b
    q, r = c + d, c - d
    return p + q, m + r, p - q, m - r


def kernel(
    sizes,
    dist_hbm, kinds_hbm, wall_hbm, inflow_hbm, side_hbm, left_hbm, right_hbm, loss_hbm,
    xf_hbm, xi_hbm, pf_hbm, pi_hbm, place_hbm, unplace_hbm, reverse_hbm, xs_hbm, courants_hbm,
    out_ref,
    dist, dense, kinds, wall, inflow, side, raw, xf, xi, pf, pi, place, unplace, reverse, xs, courants,
    sides, packed, quads, table, send, recv, field, shaped_hi, shaped_lo, planes, collided, back, own, from_y, from_x, edge, far_raw, far_done,
    local_sem, send1, recv1, send_own, recv_own, send_y, recv_y, send_x, recv_x, send_raw, recv_raw, ready,
):
    n_gx, n_gy = sizes
    gx, gy, me = lax.axis_index("gx"), lax.axis_index("gy"), lax.axis_index("vert")
    my_y, my_h = lax.rem(me, 2), me // 2
    step_y, step_x = 2 * my_y - 1, 2 * my_h - 1
    to_y, to_x = gy + step_y, gx + step_x
    has_y = jnp.logical_and(to_y >= 0, to_y < n_gy)
    core = lax.rem(gx, 2)
    early = lax.rem(gx // 2, 2) == 0
    near_x, far_x = gx + 1 - 2 * core, gx - 1 + 2 * core
    has_far = jnp.logical_and(far_x >= 0, far_x < n_gx)
    sends_far = my_h == core
    early_far = jnp.logical_and(has_far, early)
    late_far = jnp.logical_and(has_far, jnp.logical_not(early))

    barrier = pltpu.get_barrier_semaphore()

    def greet(x, y, v):
        pl.semaphore_signal(barrier, inc=1, device_id=(x, y, v), device_id_type=MESH)

    @pl.when(early_far)
    def _():
        for v in range(GROUPS):
            greet(far_x, gy, v)

    for d in OTHERS:
        greet(gx, gy, lax.rem(me + d, GROUPS))
    for step in (-1, 1):
        @pl.when(jnp.logical_and(gy + step >= 0, gy + step < n_gy))
        def _(step=step):
            for h in range(2):
                greet(gx, gy + step, 2 * h + (1 if step < 0 else 0))

    for y in range(2):
        greet(near_x, gy, y + 2 * core)

    at_gain = RANK * V * PLANE // V
    pulls = [
        (dist_hbm, dist), (wall_hbm, wall), (inflow_hbm, inflow),
        (left_hbm, raw.at[pl.ds(0, at_gain)]), (right_hbm, raw.at[pl.ds(at_gain, at_gain)]),
        (loss_hbm, raw.at[pl.ds(2 * at_gain, PLANE)]), (place_hbm, place), (reverse_hbm, reverse),
        (xf_hbm, xf), (pf_hbm, pf), (xi_hbm, xi), (pi_hbm, pi), (unplace_hbm, unplace), (side_hbm, side),
        (courants_hbm.at[me], courants), (xs_hbm.at[me], xs), (kinds_hbm, kinds),
    ]
    pulls = [pltpu.make_async_copy(a, b, local_sem.at[i]) for i, (a, b) in enumerate(pulls)]
    for i in (0, 16, 1, 2, *range(3, 16)):
        pulls[i].start()

    @pl.when(jnp.logical_not(late_far))
    def _():
        from_x[core] = jnp.zeros((2, EDGE, LANES), F32)

    for k in range(2):
        @pl.when(gy == k * (n_gy - 1))
        def _(k=k):
            from_y[k] = jnp.zeros((2, BLOCK, LANES), F32)

    for i in (0, 1, 2, 16):
        pulls[i].wait()
    for x in range(NX):
        for r in range(ROWS):
            at = (x * ROWS + r) * NY
            dense[at : at + NY, :] = dist[x, :, r * LANES : (r + 1) * LANES]
    for v in range(GROUPS):
        y, h = v % 2, v // 2
        send[v, pl.ds(48, 8)] = jnp.zeros((8, LANES), F32)
        for cell in range(2):
            x = 3 * h + (1 - 2 * h) * cell
            kind = jnp.broadcast_to(kinds[y : y + 1, x : x + 1], (ROWS, LANES))
            own_state = dense[pl.ds(x * 2 * ROWS + y, ROWS, stride=2), :]
            state = jnp.where(kind == 1, wall[...], jnp.where(kind == 2, inflow[...], own_state))
            send[v, pl.ds(cell * ROWS, ROWS)] = state
    recv[me] = send[me]
    for y in range(NY):
        edge[pl.ds(y * ROWS, ROWS)] = send[2 * core + y, pl.ds(0, ROWS)]
    edge[pl.ds(2 * ROWS, BLOCK - 2 * ROWS)] = jnp.zeros((BLOCK - 2 * ROWS, LANES), F32)

    awaited = GROUPS - 1 + jnp.where(has_y, GROUPS, 0) + jnp.where(sends_far, 0, GROUPS)
    pl.semaphore_wait(barrier, awaited + jnp.where(late_far, GROUPS, 0))

    receiver = jnp.where(early, core, 1 - core)
    every = jnp.logical_or(gy == n_gy // 8, jnp.logical_and(gy < n_gy // 8, receiver == 1))

    def push_raw(d):
        return pltpu.make_async_remote_copy(
            src_ref=edge, dst_ref=far_raw.at[me], send_sem=send_raw.at[d], recv_sem=recv_raw.at[me],
            device_id=(far_x, gy, lax.rem(me + d, GROUPS)), device_id_type=MESH,
        )

    def at_others(wanted, act):
        @pl.when(wanted)
        def _():
            for d in OTHERS:
                act(d)

    shared = jnp.logical_not(every)

    @pl.when(late_far)
    def _():
        push_raw(0).start()
        at_others(every, lambda d: push_raw(d).start())

    first = []
    for d in OTHERS:
        to = lax.rem(me + d, GROUPS)
        first.append(
            pltpu.make_async_remote_copy(
                src_ref=send.at[to], dst_ref=recv.at[me], send_sem=send1.at[d], recv_sem=recv1.at[d],
                device_id=(gx, gy, to), device_id_type=MESH,
            )
        )
        first[-1].start()

    @pl.when(late_far)
    def _():
        for y in range(2):
            pl.semaphore_signal(
                ready, inc=1, device_id=(far_x, gy, y + 2 * (1 - core)), device_id_type=MESH
            )

    for i in range(3, 8):
        pulls[i].wait()
    packed[...] = jnp.zeros_like(packed)
    for ky in range(V):
        at = (ky // PACK) * LANES + (ky % PACK) * V
        packed[:, at : at + V] = raw[pl.ds(ky, TABLES * V, stride=V), :]
    hi, lo = halves(packed[...])
    both = jnp.concatenate([hi, lo], axis=0)
    for s in range(4):
        q = dot(both, wide(place, 2 * s, 2))
        quads[s] = q[: TABLES * V] + q[TABLES * V :]

    def symmetrise(t, _):
        at = pl.ds(pl.multiple_of(t * V, 8), V)
        for s in range(4):
            hi, lo = halves(quads[3 - s, at])
            mirrored = dot(reverse[...], jnp.concatenate([hi, lo], axis=0))[:V]
            table[s, at] = quads[s, at] + mirrored
        return 0

    lax.fori_loop(0, TABLES, symmetrise, 0)

    pulls[13].wait()
    for r in range(ROWS):
        for k in range(2):
            sides[k, r : r + 1, :] = side[k : k + 1, r * LANES : (r + 1) * LANES]

    for i in range(8, 13):
        pulls[i].wait()
    for d in range(1, GROUPS):
        first[d - 1].wait_recv()

    def gather_cells(blocks):
        for u in range(GROUPS):
            for c in range(CHUNKS):
                field[6 * u : 6 * u + 6, c * LANES : (c + 1) * LANES] = blocks[u, pl.ds(c, 6, stride=CHUNKS), :]
        return jnp.concatenate([field[:, :PLANE], field[:, PLANE:]], axis=0)

    def forward(cells):
        hi, lo = halves(cells)
        along_x = dot(wide(xf, 0, 2, 6 * V), jnp.concatenate([hi, lo, hi], axis=0))
        hi, lo = halves(along_x)
        both = jnp.concatenate([hi, lo], axis=0)
        parts = []
        for c in range(4):
            top = dot(both, wide(pf.at[0], 2 * c, 2))
            parts.append(top[: 2 * V] + top[2 * V :] + dot(hi, wide(pf.at[1], 2 * c, 2)))
        cc, cs, sc, ss = parts
        swapped = lambda a: jnp.concatenate([a[V:], -a[:V]], axis=0)
        return quadrants(cc, swapped(cs), swapped(sc), -ss)

    def collide(cells, spectrum, along_x, rows):
        for t in range(TABLES):
            at = slice(t * V, (t + 1) * V)
            a = []
            for s in range(4):
                m = table[s, at]
                a.append(jnp.concatenate([spectrum[s][:V] * m, spectrum[s][V:] * m], axis=0))
            for c, b in enumerate(quadrants_to_classes(*a)):
                hi, lo = halves(b)
                z = dot(wide(along_x.at[c], 0, 2, 6 * V), jnp.concatenate([hi, lo, hi], axis=0))
                hi, lo = halves(z)
                shaped_hi[c, t * rows : (t + 1) * rows] = hi
                shaped_lo[c, t * rows : (t + 1) * rows] = lo
        used = slice(0, TABLES * rows)
        for c in range(4):
            top, low = wide(pi.at[0, c], 0, 2), wide(pi.at[1, c], 0, 2)
            hi, lo = shaped_hi[c, used], shaped_lo[c, used]
            planes[c, used] = dot(hi, top) + dot(lo, top) + dot(hi, low)

        def fields(t):
            return quadrants(*(planes[c, t * rows : (t + 1) * rows] for c in range(4)))

        gain = [0.0] * 4
        for r in range(RANK):
            gain = [g + a * b for g, a, b in zip(gain, fields(r), fields(RANK + r))]
        rates = jnp.concatenate(
            [jnp.concatenate(list(gain), axis=1), jnp.concatenate(list(fields(2 * RANK)), axis=1)], axis=0
        )
        hi, lo = halves(rates)
        rates = dot(jnp.concatenate([hi, lo], axis=0), wide(unplace, 0, 5, PLANE))
        rates = rates[: 2 * rows] + rates[2 * rows :]
        return cells + COLLISION_STEP * (rates[:rows] - cells * rates[rows:])

    cells = gather_cells(recv)
    result = collide(cells, forward(cells), xi, 2 * V)
    collided[:, :PLANE] = result[:V]
    collided[:, PLANE:] = result[V:]
    for u in range(GROUPS):
        back[u, pl.ds(48, 8)] = jnp.zeros((8, LANES), F32)
        for c in range(CHUNKS):
            back[u, pl.ds(c, 6, stride=CHUNKS), :] = collided[6 * u : 6 * u + 6, c * LANES : (c + 1) * LANES]

    def push_x(u):
        return pltpu.make_async_remote_copy(
            src_ref=back.at[u, pl.ds(0, EDGE)], dst_ref=from_x.at[1 - my_h, my_y],
            send_sem=send_x.at[u], recv_sem=recv_x.at[1 - my_h, my_y],
            device_id=(to_x, gy, u), device_id_type=MESH,
        )

    def push_y(u):
        return pltpu.make_async_remote_copy(
            src_ref=back.at[u], dst_ref=from_y.at[1 - my_y, my_h],
            send_sem=send_y.at[u], recv_sem=recv_y.at[1 - my_y, my_h],
            device_id=(gx, to_y, u), device_id_type=MESH,
        )

    def push_own(d):
        to = lax.rem(me + d, GROUPS)
        return pltpu.make_async_remote_copy(
            src_ref=back.at[to], dst_ref=own.at[me], send_sem=send_own.at[d], recv_sem=recv_own.at[d],
            device_id=(gx, gy, to), device_id_type=MESH,
        )

    @pl.when(jnp.logical_not(sends_far))
    def _():
        for u in range(GROUPS):
            push_x(u).start()

    @pl.when(has_y)
    def _():
        for u in range(GROUPS):
            push_y(u).start()

    for d in OTHERS:
        push_own(d).start()
    own[me] = back[me]

    def push_far():
        pl.semaphore_wait(ready, GROUPS)
        for u in range(GROUPS):
            push_x(u).start()

    @pl.when(jnp.logical_and(early_far, sends_far))
    def _():
        push_far()

    def share_raw(d):
        return pltpu.make_async_remote_copy(
            src_ref=far_raw.at[me], dst_ref=far_raw.at[me], send_sem=send_raw.at[d], recv_sem=recv_raw.at[me],
            device_id=(gx, gy, lax.rem(me + d, GROUPS)), device_id_type=MESH,
        )

    @pl.when(early_far)
    def _():
        push_raw(0).wait_recv()
        at_others(shared, lambda d: share_raw(d).start())

    pulls[14].wait()
    for d in range(1, GROUPS):
        push_own(d).wait_recv()
    for step in (-1, 1):
        k = 0 if step < 0 else 1

        @pl.when(jnp.logical_and(gy + step >= 0, gy + step < n_gy))
        def _(k=k):
            for h in range(2):
                pltpu.make_async_remote_copy(
                    src_ref=back.at[0], dst_ref=from_y.at[k, h], send_sem=send_y.at[0], recv_sem=recv_y.at[k, h],
                    device_id=(gx, to_y, me), device_id_type=MESH,
                ).wait_recv()

    def wait_x(k):
        for y in range(2):
            pltpu.make_async_remote_copy(
                src_ref=back.at[0, pl.ds(0, EDGE)], dst_ref=from_x.at[k, y], send_sem=send_x.at[0],
                recv_sem=recv_x.at[k, y], device_id=(near_x, gy, me), device_id_type=MESH,
            ).wait_recv()

    wait_x(1 - core)

    @pl.when(late_far)
    def _():
        wait_x(core)

    def at_cell(ref, x):
        cell = (0, 1, 1, 0)[x]
        return ref[pl.ds(cell * ROWS, ROWS), :]

    courant_x, courant_y = courants[0, pl.ds(0, ROWS)], courants[1, pl.ds(0, ROWS)]
    higher_x, higher_y = sides[0] == 1, sides[1] == 1
    centre = {(x, y): at_cell(own.at[y + 2 * (x // 2)], x) for x in range(NX) for y in range(NY)}
    for x in range(NX):
        for y in range(NY):
            here = centre[x, y]
            below_x = centre[x - 1, y] if x > 0 else from_x[0, y, pl.ds(0, ROWS)]
            above_x = centre[x + 1, y] if x < NX - 1 else from_x[1, y, pl.ds(0, ROWS)]
            below_y = centre[x, 0] if y > 0 else at_cell(from_y.at[0, x // 2], x)
            above_y = centre[x, 1] if y < 1 else at_cell(from_y.at[1, x // 2], x)
            up_x = jnp.where(higher_x, below_x, above_x)
            up_y = jnp.where(higher_y, below_y, above_y)
            out_ref[pl.ds(x * 2 * ROWS + y, ROWS, stride=2), :] = (
                here - courant_x * (here - up_x) - courant_y * (here - up_y)
            )

    for d in range(1, GROUPS):
        first[d - 1].wait_send()
        push_own(d).wait_send()

    @pl.when(has_y)
    def _():
        for u in range(GROUPS):
            push_y(u).wait_send()

    @pl.when(jnp.logical_or(jnp.logical_not(sends_far), early_far))
    def _():
        for u in range(GROUPS):
            push_x(u).wait_send()

    @pl.when(late_far)
    def _():
        push_raw(0).wait_send()
        at_others(every, lambda d: push_raw(d).wait_send())

    pulls[15].wait()

    @pl.when(early_far)
    def _():
        for d in range(1, GROUPS):
            peer = lax.rem(me + d, GROUPS)
            pltpu.make_async_remote_copy(
                src_ref=edge, dst_ref=far_raw.at[peer], send_sem=send_raw.at[d], recv_sem=recv_raw.at[peer],
                device_id=(gx, gy, peer), device_id_type=MESH,
            ).wait_recv()
        at_others(shared, lambda d: share_raw(d).wait_send())
        spectrum = forward(gather_cells(far_raw))
        for c in range(CHUNKS):
            collided[:6, c * LANES : (c + 1) * LANES] = far_raw[me, pl.ds(c, 6, stride=CHUNKS), :]
        far = jnp.concatenate([collided[:6, :PLANE], collided[:6, PLANE:], jnp.zeros((SOME - 12, PLANE), F32)], axis=0)
        far = collide(far, spectrum, xs, SOME)
        collided[:6, :PLANE] = far[:6]
        collided[:6, PLANE:] = far[6:12]
        for c in range(CHUNKS):
            far_done[pl.ds(c, 6, stride=CHUNKS), :] = collided[:6, c * LANES : (c + 1) * LANES]
        x = (NX - 1) * core
        for y in range(NY):
            at = pl.ds(x * NY * ROWS + y, ROWS, stride=NY)
            inward = courant_x * far_done[pl.ds(y * ROWS, ROWS)]
            out_ref[at, :] = out_ref[at, :] + jnp.where(sides[0] == 1 - core, inward, 0.0)


def spread(dense, out_ref):
    for x in range(NX):
        for r in range(ROWS):
            at = (x * ROWS + r) * NY
            out_ref[x, :, r * LANES : (r + 1) * LANES] = dense[at : at + NY, :]


def quadrants_to_classes(pp, pm, mp, mm):
    a, b = pp + pm, pp - pm
    c, d = mp + mm, mp - mm
    return a + c, b + d, a - c, b - d


def on_device(sizes, distribution, cell_types, wall_state, inflow_state, upwind_side, gain_left, gain_right, loss_table):
    tables = constants()
    tables = [jnp.asarray(tables[name]) for name in NAMES]
    operands = [
        distribution,
        cell_types.T,
        wall_state.reshape(ROWS, LANES),
        inflow_state.reshape(ROWS, LANES),
        upwind_side,
        gain_left.reshape(RANK * PLANE, V),
        gain_right.reshape(RANK * PLANE, V),
        loss_table.reshape(PLANE, V),
        *tables,
    ]
    spaces = [pl.BlockSpec(memory_space=pl.ANY)] * len(operands)
    dma = pltpu.SemaphoreType.DMA
    held = [
        pltpu.VMEM((NX, NY, SLAB), F32),
        pltpu.VMEM((NX * NY * ROWS, LANES), F32),
        pltpu.VMEM((NY, NX), jnp.int32),
        pltpu.VMEM((ROWS, LANES), F32),
        pltpu.VMEM((ROWS, LANES), F32),
        pltpu.VMEM((2, SLAB), jnp.int32),
        pltpu.VMEM((TABLES * PLANE, V), F32),
        *(pltpu.VMEM(t.shape, t.dtype) for t in tables[:-2]),
        *(pltpu.VMEM(t.shape[1:], t.dtype) for t in tables[-2:]),
        pltpu.VMEM((2, ROWS, LANES), jnp.int32),
        pltpu.VMEM((TABLES * V, GROUPED), F32),
        pltpu.VMEM((4, TABLES * V, W), F32),
        pltpu.VMEM((4, TABLES * V, W), F32),
        pltpu.VMEM((GROUPS, BLOCK, LANES), F32),
        pltpu.VMEM((GROUPS, BLOCK, LANES), F32),
        pltpu.VMEM((V, 2 * PLANE), F32),
        pltpu.VMEM((4, TABLES * 2 * V, W), BF16),
        pltpu.VMEM((4, TABLES * 2 * V, W), BF16),
        pltpu.VMEM((4, TABLES * 2 * V, W), F32),
        pltpu.VMEM((V, 2 * PLANE), F32),
        pltpu.VMEM((GROUPS, BLOCK, LANES), F32),
        pltpu.VMEM((GROUPS, BLOCK, LANES), F32),
        pltpu.VMEM((2, 2, BLOCK, LANES), F32),
        pltpu.VMEM((2, 2, EDGE, LANES), F32),
        pltpu.VMEM((BLOCK, LANES), F32),
        pltpu.VMEM((GROUPS, BLOCK, LANES), F32),
        pltpu.VMEM((BLOCK, LANES), F32),
        dma((17,)),
        dma((GROUPS,)), dma((GROUPS,)),
        dma((GROUPS,)), dma((GROUPS,)),
        dma((GROUPS,)), dma((2, 2)),
        dma((GROUPS,)), dma((2, 2)),
        dma((GROUPS,)), dma((GROUPS,)),
        pltpu.SemaphoreType.REGULAR,
    ]
    dense = pl.pallas_call(
        functools.partial(kernel, sizes),
        out_shape=pltpu.VMEM((NX * NY * ROWS, LANES), F32),
        in_specs=spaces,
        out_specs=pl.BlockSpec(memory_space=pltpu.VMEM),
        scratch_shapes=held,
        compiler_params=pltpu.CompilerParams(
            collective_id=0, has_side_effects=True, vmem_limit_bytes=60 * 1024 * 1024
        ),
        cost_estimate=pl.CostEstimate(flops=3_000_000_000, bytes_accessed=10_000_000, transcendentals=0),
        name="step",
    )(*operands)
    return pl.pallas_call(
        spread,
        out_shape=jax.ShapeDtypeStruct((NX, NY, SLAB), F32),
        in_specs=[pl.BlockSpec(memory_space=pltpu.VMEM)],
        out_specs=pl.BlockSpec(memory_space=pltpu.VMEM),
        name="spread",
    )(pltpu.with_memory_space_constraint(dense, pltpu.VMEM))


def solution(mesh):
    placed = (
        P("gx", "gy", "vert"),
        P("gx", "gy"),
        P("vert"),
        P("vert"),
        P(None, "vert"),
        P(),
        P(),
        P(),
    )
    sizes = (mesh.shape["gx"], mesh.shape["gy"])
    return jax.shard_map(
        functools.partial(on_device, sizes),
        mesh=mesh,
        in_specs=placed,
        out_specs=P("gx", "gy", "vert"),
        check_vma=False,
    )
```

```python
import functools

import jax
import jax.numpy as jnp
import ml_dtypes
import numpy as np
from jax import lax
from jax.experimental import pallas as pl
from jax.experimental.pallas import tpu as pltpu
from jax.sharding import PartitionSpec as P

MESH = pl.DeviceIdType.MESH
F32 = jnp.float32
BF16 = jnp.bfloat16

V = 24
PLANE = V * V
HALF = V // 2
RANK = 4
TABLES = 2 * RANK + 1
GROUPS = 4
NX, NY = 4, 2
SLAB = PLANE * V // GROUPS
LANES = 128
ROWS = SLAB // LANES
BLOCK = 56
EDGE = 32
PAIRS = 3
SOME = 16
CHUNKS = 2 * PLANE // LANES
W = 256
PACK = 5
GROUPED = 5 * LANES
SIGNS = ((1, 1), (1, -1), (-1, 1), (-1, -1))
OTHERS = (2, 1, 3)
COLLISION_STEP = 0.25
COURANT = 0.45


def split_constant(a):
    hi = a.astype(ml_dtypes.bfloat16)
    lo = (a - hi.astype(np.float64)).astype(ml_dtypes.bfloat16)
    return hi, lo


def chunked(a):
    pad = -a.shape[-1] % LANES
    a = np.pad(a, [(0, 0)] * (a.ndim - 1) + [(0, pad)])
    a = a.reshape(*a.shape[:-1], -1, LANES)
    return np.ascontiguousarray(np.moveaxis(a, -2, -3))


def stacked(a):
    hi, lo = split_constant(a)
    return chunked(np.concatenate([hi, hi, lo], axis=1))


@functools.cache
def constants():
    step = 2.0 * np.pi / V
    inner = [(a, b) for a in range(1, HALF) for b in range(1, HALF)]
    outer = [(a, b) for a in range(HALF + 1) for b in range(HALF + 1) if a % HALF == 0 or b % HALF == 0]
    points = np.array(inner + outer)
    count = len(points)
    qy, qz = points[:, 0], points[:, 1]
    natural = np.arange(PLANE)
    ny, nz = natural // V, natural % V
    trig = (np.cos, np.sin)
    classes = ((0, 0), (0, 1), (1, 0), (1, 1))

    def grid(rows_y, rows_z, cy, cz):
        by = trig[cy](step * (rows_y[:, None] * qy[None, :] % V))
        bz = trig[cz](step * (rows_z[:, None] * qz[None, :] % V))
        return by * bz

    plane_forward = np.zeros((PLANE, 4 * W))
    plane_inverse = np.zeros((4, W, W))
    weight = np.where(qy % HALF == 0, 0.5, 1.0) * np.where(qz % HALF == 0, 0.5, 1.0) / PLANE
    for c, (cy, cz) in enumerate(classes):
        plane_forward[:, c * W : c * W + count] = grid(ny, nz, cy, cz)
        plane_inverse[c, :count, :count] = weight[:, None] * grid(qy, qz, cy, cz)

    place = np.zeros((GROUPED, 4 * W))
    unplace = np.zeros((4 * W, PLANE))
    seen = set()
    for s, (sy, sz) in enumerate(SIGNS):
        for q in range(count):
            y, z = sy * qy[q] % V, sz * qz[q] % V
            place[(y // PACK) * LANES + (y % PACK) * V + z, s * W + q] = 1.0
            if (y, z) not in seen:
                seen.add((y, z))
                unplace[s * W + q, y * V + z] = 1.0

    row_of = np.zeros((2, V), dtype=int)
    for jx in range(V):
        pair, odd = jx // 2, jx % 2
        u, q = pair // PAIRS, pair % PAIRS
        for cell in range(2):
            row_of[cell, jx] = odd * V + 2 * PAIRS * u + PAIRS * cell + q
    k = np.arange(V)
    theta = step * (k[:, None] * k[None, :] % V)
    cos, sin = np.cos(theta), np.sin(theta)
    x_forward = np.zeros((2 * V, 2 * V))
    x_forward[:V, row_of[0]] = cos
    x_forward[:V, row_of[1]] = sin
    x_forward[V:, row_of[0]] = -sin
    x_forward[V:, row_of[1]] = cos
    real = np.concatenate([cos, -sin], axis=1)
    imag = np.concatenate([sin, cos], axis=1)
    x_inverse, x_slab = [], [[] for _ in range(GROUPS)]
    for first, second in ((real, imag), (-imag, real), (-imag, real), (-real, -imag)):
        m = np.zeros((2 * V, 2 * V))
        m[row_of[0]] = first
        m[row_of[1]] = second
        m = m / (2 * V)
        x_inverse.append(stacked(m))
        for u in range(GROUPS):
            own = np.zeros((SOME, 2 * V))
            own[:6], own[6:12] = m[6 * u : 6 * u + 6], m[V + 6 * u : V + 6 * u + 6]
            x_slab[u].append(stacked(own))

    reverse = np.zeros((32, 2 * V))
    for r in range(V):
        reverse[r, (V - r) % V] = 1.0
        reverse[r, V + (V - r) % V] = 1.0

    velocity = np.arange(PLANE * V)
    courant_x = COURANT * np.abs(2 * (velocity // PLANE) - (V - 1)).astype(np.float32) / (V - 1)
    courant_y = COURANT * np.abs(2 * (velocity // V % V) - (V - 1)).astype(np.float32) / (V - 1)
    courants = np.zeros((GROUPS, 2, EDGE, LANES), np.float32)
    courants[:, 0, :ROWS] = courant_x.reshape(GROUPS, ROWS, LANES)
    courants[:, 1, :ROWS] = courant_y.reshape(GROUPS, ROWS, LANES)

    return {
        "x_forward": stacked(x_forward),
        "x_inverse": np.stack(x_inverse),
        "x_slab": np.stack([np.stack(a) for a in x_slab]),
        "plane_forward": chunked(np.stack(split_constant(plane_forward))),
        "plane_inverse": chunked(np.stack(split_constant(plane_inverse))),
        "place": chunked(place.astype(ml_dtypes.bfloat16)),
        "unplace": chunked(unplace.astype(ml_dtypes.bfloat16)),
        "reverse": reverse.astype(ml_dtypes.bfloat16),
        "courants": courants,
    }


NAMES = ("x_forward", "x_inverse", "plane_forward", "plane_inverse", "place", "unplace", "reverse", "x_slab", "courants")


def halves(a):
    hi = a.astype(BF16)
    lo = (a - hi.astype(F32)).astype(BF16)
    return hi, lo


def wide(ref, start, count, width=None):
    a = jnp.concatenate([ref[start + i] for i in range(count)], axis=1)
    return a if width is None else a[:, :width]


def dot(a, b):
    return jnp.dot(a, b, preferred_element_type=F32)


def quadrants(a, b, c, d):
    p, m = a + b, a - b
    q, r = c + d, c - d
    return p + q, m + r, p - q, m - r


def kernel(
    sizes,
    dist_hbm, kinds_hbm, wall_hbm, inflow_hbm, side_hbm, left_hbm, right_hbm, loss_hbm,
    xf_hbm, xi_hbm, pf_hbm, pi_hbm, place_hbm, unplace_hbm, reverse_hbm, xs_hbm, courants_hbm,
    out_ref,
    dist, dense, kinds, wall, inflow, side, raw, xf, xi, pf, pi, place, unplace, reverse, xs, courants,
    sides, packed, quads, table, send, recv, field, shaped_hi, shaped_lo, planes, collided, back, own, from_y, from_x, edge, far_raw, far_done,
    local_sem, send1, recv1, send_own, recv_own, send_y, recv_y, send_x, recv_x, send_raw, recv_raw, ready,
):
    n_gx, n_gy = sizes
    gx, gy, me = lax.axis_index("gx"), lax.axis_index("gy"), lax.axis_index("vert")
    my_y, my_h = lax.rem(me, 2), me // 2
    step_y, step_x = 2 * my_y - 1, 2 * my_h - 1
    to_y, to_x = gy + step_y, gx + step_x
    has_y = jnp.logical_and(to_y >= 0, to_y < n_gy)
    core = lax.rem(gx, 2)
    early = lax.rem(gx // 2, 2) == 0
    near_x, far_x = gx + 1 - 2 * core, gx - 1 + 2 * core
    has_far = jnp.logical_and(far_x >= 0, far_x < n_gx)
    sends_far = my_h == core
    early_far = jnp.logical_and(has_far, early)
    late_far = jnp.logical_and(has_far, jnp.logical_not(early))

    barrier = pltpu.get_barrier_semaphore()

    def greet(x, y, v):
        pl.semaphore_signal(barrier, inc=1, device_id=(x, y, v), device_id_type=MESH)

    @pl.when(early_far)
    def _():
        for v in range(GROUPS):
            greet(far_x, gy, v)

    for d in OTHERS:
        greet(gx, gy, lax.rem(me + d, GROUPS))
    for step in (-1, 1):
        @pl.when(jnp.logical_and(gy + step >= 0, gy + step < n_gy))
        def _(step=step):
            for h in range(2):
                greet(gx, gy + step, 2 * h + (1 if step < 0 else 0))

    for y in range(2):
        greet(near_x, gy, y + 2 * core)

    at_gain = RANK * V * PLANE // V
    pulls = [
        (dist_hbm, dist), (wall_hbm, wall), (inflow_hbm, inflow),
        (left_hbm, raw.at[pl.ds(0, at_gain)]), (right_hbm, raw.at[pl.ds(at_gain, at_gain)]),
        (loss_hbm, raw.at[pl.ds(2 * at_gain, PLANE)]), (place_hbm, place), (reverse_hbm, reverse),
        (xf_hbm, xf), (pf_hbm, pf), (xi_hbm, xi), (pi_hbm, pi), (unplace_hbm, unplace), (side_hbm, side),
        (courants_hbm.at[me], courants), (xs_hbm.at[me], xs), (kinds_hbm, kinds),
    ]
    pulls = [pltpu.make_async_copy(a, b, local_sem.at[i]) for i, (a, b) in enumerate(pulls)]
    for i in (0, 16, 1, 2, *range(3, 16)):
        pulls[i].start()

    @pl.when(jnp.logical_not(late_far))
    def _():
        from_x[core] = jnp.zeros((2, EDGE, LANES), F32)

    for k in range(2):
        @pl.when(gy == k * (n_gy - 1))
        def _(k=k):
            from_y[k] = jnp.zeros((2, BLOCK, LANES), F32)

    for i in (0, 1, 2, 16):
        pulls[i].wait()
    for x in range(NX):
        for r in range(ROWS):
            at = (x * ROWS + r) * NY
            dense[at : at + NY, :] = dist[x, :, r * LANES : (r + 1) * LANES]
    for v in range(GROUPS):
        y, h = v % 2, v // 2
        send[v, pl.ds(48, 8)] = jnp.zeros((8, LANES), F32)
        for cell in range(2):
            x = 3 * h + (1 - 2 * h) * cell
            kind = jnp.broadcast_to(kinds[y : y + 1, x : x + 1], (ROWS, LANES))
            own_state = dense[pl.ds(x * 2 * ROWS + y, ROWS, stride=2), :]
            state = jnp.where(kind == 1, wall[...], jnp.where(kind == 2, inflow[...], own_state))
            send[v, pl.ds(cell * ROWS, ROWS)] = state
    recv[me] = send[me]
    for y in range(NY):
        edge[pl.ds(y * ROWS, ROWS)] = send[2 * core + y, pl.ds(0, ROWS)]
    edge[pl.ds(2 * ROWS, BLOCK - 2 * ROWS)] = jnp.zeros((BLOCK - 2 * ROWS, LANES), F32)

    awaited = GROUPS - 1 + jnp.where(has_y, GROUPS, 0) + jnp.where(sends_far, 0, GROUPS)
    pl.semaphore_wait(barrier, awaited + jnp.where(late_far, GROUPS, 0))

    receiver = jnp.where(early, core, 1 - core)
    every = jnp.logical_or(gy == n_gy // 8, jnp.logical_and(gy < n_gy // 8, receiver == 1))

    def push_raw(d):
        return pltpu.make_async_remote_copy(
            src_ref=edge, dst_ref=far_raw.at[me], send_sem=send_raw.at[d], recv_sem=recv_raw.at[me],
            device_id=(far_x, gy, lax.rem(me + d, GROUPS)), device_id_type=MESH,
        )

    def at_others(wanted, act):
        @pl.when(wanted)
        def _():
            for d in OTHERS:
                act(d)

    shared = jnp.logical_not(every)

    @pl.when(late_far)
    def _():
        push_raw(0).start()
        at_others(every, lambda d: push_raw(d).start())

    first = []
    for d in OTHERS:
        to = lax.rem(me + d, GROUPS)
        first.append(
            pltpu.make_async_remote_copy(
                src_ref=send.at[to], dst_ref=recv.at[me], send_sem=send1.at[d], recv_sem=recv1.at[d],
                device_id=(gx, gy, to), device_id_type=MESH,
            )
        )
        first[-1].start()

    @pl.when(late_far)
    def _():
        for y in range(2):
            pl.semaphore_signal(
                ready, inc=1, device_id=(far_x, gy, y + 2 * (1 - core)), device_id_type=MESH
            )

    for i in range(3, 8):
        pulls[i].wait()
    packed[...] = jnp.zeros_like(packed)
    for ky in range(V):
        at = (ky // PACK) * LANES + (ky % PACK) * V
        packed[:, at : at + V] = raw[pl.ds(ky, TABLES * V, stride=V), :]
    hi, lo = halves(packed[...])
    both = jnp.concatenate([hi, lo], axis=0)
    for s in range(4):
        q = dot(both, wide(place, 2 * s, 2))
        quads[s] = q[: TABLES * V] + q[TABLES * V :]

    def symmetrise(t, _):
        at = pl.ds(pl.multiple_of(t * V, 8), V)
        for s in range(4):
            hi, lo = halves(quads[3 - s, at])
            mirrored = dot(reverse[...], jnp.concatenate([hi, lo], axis=0))[:V]
            table[s, at] = quads[s, at] + mirrored
        return 0

    lax.fori_loop(0, TABLES, symmetrise, 0)

    pulls[13].wait()
    for r in range(ROWS):
        for k in range(2):
            sides[k, r : r + 1, :] = side[k : k + 1, r * LANES : (r + 1) * LANES]

    for i in range(8, 13):
        pulls[i].wait()
    for d in range(1, GROUPS):
        first[d - 1].wait_recv()

    def gather_cells(blocks):
        for u in range(GROUPS):
            for c in range(CHUNKS):
                field[6 * u : 6 * u + 6, c * LANES : (c + 1) * LANES] = blocks[u, pl.ds(c, 6, stride=CHUNKS), :]
        return jnp.concatenate([field[:, :PLANE], field[:, PLANE:]], axis=0)

    def forward(cells):
        hi, lo = halves(cells)
        along_x = dot(wide(xf, 0, 2, 6 * V), jnp.concatenate([hi, lo, hi], axis=0))
        hi, lo = halves(along_x)
        both = jnp.concatenate([hi, lo], axis=0)
        parts = []
        for c in range(4):
            top = dot(both, wide(pf.at[0], 2 * c, 2))
            parts.append(top[: 2 * V] + top[2 * V :] + dot(hi, wide(pf.at[1], 2 * c, 2)))
        cc, cs, sc, ss = parts
        swapped = lambda a: jnp.concatenate([a[V:], -a[:V]], axis=0)
        return quadrants(cc, swapped(cs), swapped(sc), -ss)

    def collide(cells, spectrum, along_x, rows):
        lanes = (W, W, W, LANES)
        for t in range(TABLES):
            at = slice(t * V, (t + 1) * V)
            a = []
            for s in range(4):
                m = table[s, at]
                a.append(jnp.concatenate([spectrum[s][:V] * m, spectrum[s][V:] * m], axis=0))
            for c, b in enumerate(quadrants_to_classes(*a)):
                hi, lo = halves(b[:, : lanes[c]])
                z = dot(wide(along_x.at[c], 0, 2, 6 * V), jnp.concatenate([hi, lo, hi], axis=0))
                hi, lo = halves(z)
                shaped_hi[c, t * rows : (t + 1) * rows, : lanes[c]] = hi
                shaped_lo[c, t * rows : (t + 1) * rows, : lanes[c]] = lo
        used = slice(0, TABLES * rows)
        for c in range(4):
            n = lanes[c]
            top, low = (wide(pi.at[k, c, :, pl.ds(0, n)], 0, n // LANES) for k in range(2))
            hi, lo = shaped_hi[c, used, :n], shaped_lo[c, used, :n]
            planes[c, used, :n] = dot(hi, top) + dot(lo, top) + dot(hi, low)

        def fields(t):
            at = slice(t * rows, (t + 1) * rows)
            parts = [planes[c, at, : lanes[c]] for c in range(4)]
            parts[3] = jnp.concatenate([parts[3], jnp.zeros((rows, W - LANES), F32)], axis=1)
            return quadrants(*parts)

        gain = [0.0] * 4
        for r in range(RANK):
            gain = [g + a * b for g, a, b in zip(gain, fields(r), fields(RANK + r))]
        rates = jnp.concatenate(
            [jnp.concatenate(list(gain), axis=1), jnp.concatenate(list(fields(2 * RANK)), axis=1)], axis=0
        )
        hi, lo = halves(rates)
        rates = dot(jnp.concatenate([hi, lo], axis=0), wide(unplace, 0, 5, PLANE))
        rates = rates[: 2 * rows] + rates[2 * rows :]
        return cells + COLLISION_STEP * (rates[:rows] - cells * rates[rows:])

    cells = gather_cells(recv)
    result = collide(cells, forward(cells), xi, 2 * V)
    collided[:, :PLANE] = result[:V]
    collided[:, PLANE:] = result[V:]
    for u in range(GROUPS):
        back[u, pl.ds(48, 8)] = jnp.zeros((8, LANES), F32)
        for c in range(CHUNKS):
            back[u, pl.ds(c, 6, stride=CHUNKS), :] = collided[6 * u : 6 * u + 6, c * LANES : (c + 1) * LANES]

    def push_x(u):
        return pltpu.make_async_remote_copy(
            src_ref=back.at[u, pl.ds(0, EDGE)], dst_ref=from_x.at[1 - my_h, my_y],
            send_sem=send_x.at[u], recv_sem=recv_x.at[1 - my_h, my_y],
            device_id=(to_x, gy, u), device_id_type=MESH,
        )

    def push_y(u):
        return pltpu.make_async_remote_copy(
            src_ref=back.at[u], dst_ref=from_y.at[1 - my_y, my_h],
            send_sem=send_y.at[u], recv_sem=recv_y.at[1 - my_y, my_h],
            device_id=(gx, to_y, u), device_id_type=MESH,
        )

    def push_own(d):
        to = lax.rem(me + d, GROUPS)
        return pltpu.make_async_remote_copy(
            src_ref=back.at[to], dst_ref=own.at[me], send_sem=send_own.at[d], recv_sem=recv_own.at[d],
            device_id=(gx, gy, to), device_id_type=MESH,
        )

    @pl.when(jnp.logical_not(sends_far))
    def _():
        for u in range(GROUPS):
            push_x(u).start()

    @pl.when(has_y)
    def _():
        for u in range(GROUPS):
            push_y(u).start()

    for d in OTHERS:
        push_own(d).start()
    own[me] = back[me]

    def push_far():
        pl.semaphore_wait(ready, GROUPS)
        for u in range(GROUPS):
            push_x(u).start()

    @pl.when(jnp.logical_and(early_far, sends_far))
    def _():
        push_far()

    def share_raw(d):
        return pltpu.make_async_remote_copy(
            src_ref=far_raw.at[me], dst_ref=far_raw.at[me], send_sem=send_raw.at[d], recv_sem=recv_raw.at[me],
            device_id=(gx, gy, lax.rem(me + d, GROUPS)), device_id_type=MESH,
        )

    @pl.when(early_far)
    def _():
        push_raw(0).wait_recv()
        at_others(shared, lambda d: share_raw(d).start())

    pulls[14].wait()
    for d in range(1, GROUPS):
        push_own(d).wait_recv()
    for step in (-1, 1):
        k = 0 if step < 0 else 1

        @pl.when(jnp.logical_and(gy + step >= 0, gy + step < n_gy))
        def _(k=k):
            for h in range(2):
                pltpu.make_async_remote_copy(
                    src_ref=back.at[0], dst_ref=from_y.at[k, h], send_sem=send_y.at[0], recv_sem=recv_y.at[k, h],
                    device_id=(gx, to_y, me), device_id_type=MESH,
                ).wait_recv()

    def wait_x(k):
        for y in range(2):
            pltpu.make_async_remote_copy(
                src_ref=back.at[0, pl.ds(0, EDGE)], dst_ref=from_x.at[k, y], send_sem=send_x.at[0],
                recv_sem=recv_x.at[k, y], device_id=(near_x, gy, me), device_id_type=MESH,
            ).wait_recv()

    wait_x(1 - core)

    @pl.when(late_far)
    def _():
        wait_x(core)

    def at_cell(ref, x):
        cell = (0, 1, 1, 0)[x]
        return ref[pl.ds(cell * ROWS, ROWS), :]

    courant_x, courant_y = courants[0, pl.ds(0, ROWS)], courants[1, pl.ds(0, ROWS)]
    higher_x, higher_y = sides[0] == 1, sides[1] == 1
    centre = {(x, y): at_cell(own.at[y + 2 * (x // 2)], x) for x in range(NX) for y in range(NY)}
    for x in range(NX):
        for y in range(NY):
            here = centre[x, y]
            below_x = centre[x - 1, y] if x > 0 else from_x[0, y, pl.ds(0, ROWS)]
            above_x = centre[x + 1, y] if x < NX - 1 else from_x[1, y, pl.ds(0, ROWS)]
            below_y = centre[x, 0] if y > 0 else at_cell(from_y.at[0, x // 2], x)
            above_y = centre[x, 1] if y < 1 else at_cell(from_y.at[1, x // 2], x)
            up_x = jnp.where(higher_x, below_x, above_x)
            up_y = jnp.where(higher_y, below_y, above_y)
            out_ref[pl.ds(x * 2 * ROWS + y, ROWS, stride=2), :] = (
                here - courant_x * (here - up_x) - courant_y * (here - up_y)
            )

    for d in range(1, GROUPS):
        first[d - 1].wait_send()
        push_own(d).wait_send()

    @pl.when(has_y)
    def _():
        for u in range(GROUPS):
            push_y(u).wait_send()

    @pl.when(jnp.logical_or(jnp.logical_not(sends_far), early_far))
    def _():
        for u in range(GROUPS):
            push_x(u).wait_send()

    @pl.when(late_far)
    def _():
        push_raw(0).wait_send()
        at_others(every, lambda d: push_raw(d).wait_send())

    pulls[15].wait()

    @pl.when(early_far)
    def _():
        for d in range(1, GROUPS):
            peer = lax.rem(me + d, GROUPS)
            pltpu.make_async_remote_copy(
                src_ref=edge, dst_ref=far_raw.at[peer], send_sem=send_raw.at[d], recv_sem=recv_raw.at[peer],
                device_id=(gx, gy, peer), device_id_type=MESH,
            ).wait_recv()
        at_others(shared, lambda d: share_raw(d).wait_send())
        spectrum = forward(gather_cells(far_raw))
        for c in range(CHUNKS):
            collided[:6, c * LANES : (c + 1) * LANES] = far_raw[me, pl.ds(c, 6, stride=CHUNKS), :]
        far = jnp.concatenate([collided[:6, :PLANE], collided[:6, PLANE:], jnp.zeros((SOME - 12, PLANE), F32)], axis=0)
        far = collide(far, spectrum, xs, SOME)
        collided[:6, :PLANE] = far[:6]
        collided[:6, PLANE:] = far[6:12]
        for c in range(CHUNKS):
            far_done[pl.ds(c, 6, stride=CHUNKS), :] = collided[:6, c * LANES : (c + 1) * LANES]
        x = (NX - 1) * core
        for y in range(NY):
            at = pl.ds(x * NY * ROWS + y, ROWS, stride=NY)
            inward = courant_x * far_done[pl.ds(y * ROWS, ROWS)]
            out_ref[at, :] = out_ref[at, :] + jnp.where(sides[0] == 1 - core, inward, 0.0)


def spread(dense, out_ref):
    for x in range(NX):
        for r in range(ROWS):
            at = (x * ROWS + r) * NY
            out_ref[x, :, r * LANES : (r + 1) * LANES] = dense[at : at + NY, :]


def quadrants_to_classes(pp, pm, mp, mm):
    a, b = pp + pm, pp - pm
    c, d = mp + mm, mp - mm
    return a + c, b + d, a - c, b - d


def on_device(sizes, distribution, cell_types, wall_state, inflow_state, upwind_side, gain_left, gain_right, loss_table):
    tables = constants()
    tables = [jnp.asarray(tables[name]) for name in NAMES]
    operands = [
        distribution,
        cell_types.T,
        wall_state.reshape(ROWS, LANES),
        inflow_state.reshape(ROWS, LANES),
        upwind_side,
        gain_left.reshape(RANK * PLANE, V),
        gain_right.reshape(RANK * PLANE, V),
        loss_table.reshape(PLANE, V),
        *tables,
    ]
    spaces = [pl.BlockSpec(memory_space=pl.ANY)] * len(operands)
    dma = pltpu.SemaphoreType.DMA
    held = [
        pltpu.VMEM((NX, NY, SLAB), F32),
        pltpu.VMEM((NX * NY * ROWS, LANES), F32),
        pltpu.VMEM((NY, NX), jnp.int32),
        pltpu.VMEM((ROWS, LANES), F32),
        pltpu.VMEM((ROWS, LANES), F32),
        pltpu.VMEM((2, SLAB), jnp.int32),
        pltpu.VMEM((TABLES * PLANE, V), F32),
        *(pltpu.VMEM(t.shape, t.dtype) for t in tables[:-2]),
        *(pltpu.VMEM(t.shape[1:], t.dtype) for t in tables[-2:]),
        pltpu.VMEM((2, ROWS, LANES), jnp.int32),
        pltpu.VMEM((TABLES * V, GROUPED), F32),
        pltpu.VMEM((4, TABLES * V, W), F32),
        pltpu.VMEM((4, TABLES * V, W), F32),
        pltpu.VMEM((GROUPS, BLOCK, LANES), F32),
        pltpu.VMEM((GROUPS, BLOCK, LANES), F32),
        pltpu.VMEM((V, 2 * PLANE), F32),
        pltpu.VMEM((4, TABLES * 2 * V, W), BF16),
        pltpu.VMEM((4, TABLES * 2 * V, W), BF16),
        pltpu.VMEM((4, TABLES * 2 * V, W), F32),
        pltpu.VMEM((V, 2 * PLANE), F32),
        pltpu.VMEM((GROUPS, BLOCK, LANES), F32),
        pltpu.VMEM((GROUPS, BLOCK, LANES), F32),
        pltpu.VMEM((2, 2, BLOCK, LANES), F32),
        pltpu.VMEM((2, 2, EDGE, LANES), F32),
        pltpu.VMEM((BLOCK, LANES), F32),
        pltpu.VMEM((GROUPS, BLOCK, LANES), F32),
        pltpu.VMEM((BLOCK, LANES), F32),
        dma((17,)),
        dma((GROUPS,)), dma((GROUPS,)),
        dma((GROUPS,)), dma((GROUPS,)),
        dma((GROUPS,)), dma((2, 2)),
        dma((GROUPS,)), dma((2, 2)),
        dma((GROUPS,)), dma((GROUPS,)),
        pltpu.SemaphoreType.REGULAR,
    ]
    dense = pl.pallas_call(
        functools.partial(kernel, sizes),
        out_shape=pltpu.VMEM((NX * NY * ROWS, LANES), F32),
        in_specs=spaces,
        out_specs=pl.BlockSpec(memory_space=pltpu.VMEM),
        scratch_shapes=held,
        compiler_params=pltpu.CompilerParams(
            collective_id=0, has_side_effects=True, vmem_limit_bytes=60 * 1024 * 1024
        ),
        cost_estimate=pl.CostEstimate(flops=3_000_000_000, bytes_accessed=10_000_000, transcendentals=0),
        name="step",
    )(*operands)
    return pl.pallas_call(
        spread,
        out_shape=jax.ShapeDtypeStruct((NX, NY, SLAB), F32),
        in_specs=[pl.BlockSpec(memory_space=pltpu.VMEM)],
        out_specs=pl.BlockSpec(memory_space=pltpu.VMEM),
        name="spread",
    )(pltpu.with_memory_space_constraint(dense, pltpu.VMEM))


def solution(mesh):
    placed = (
        P("gx", "gy", "vert"),
        P("gx", "gy"),
        P("vert"),
        P("vert"),
        P(None, "vert"),
        P(),
        P(),
        P(),
    )
    sizes = (mesh.shape["gx"], mesh.shape["gy"])
    return jax.shard_map(
        functools.partial(on_device, sizes),
        mesh=mesh,
        in_specs=placed,
        out_specs=P("gx", "gy", "vert"),
        check_vma=False,
    )
```

```python
import functools

import jax
import jax.numpy as jnp
import ml_dtypes
import numpy as np
from jax import lax
from jax.experimental import pallas as pl
from jax.experimental.pallas import tpu as pltpu
from jax.sharding import PartitionSpec as P

MESH = pl.DeviceIdType.MESH
F32 = jnp.float32
BF16 = jnp.bfloat16

V = 24
PLANE = V * V
HALF = V // 2
RANK = 4
TABLES = 2 * RANK + 1
GROUPS = 4
NX, NY = 4, 2
SLAB = PLANE * V // GROUPS
LANES = 128
ROWS = SLAB // LANES
BLOCK = 56
EDGE = 32
PAIRS = 3
SOME = 16
CHUNKS = 2 * PLANE // LANES
W = 256
PACK = 5
GROUPED = 5 * LANES
SIGNS = ((1, 1), (1, -1), (-1, 1), (-1, -1))
OTHERS = (2, 1, 3)
COLLISION_STEP = 0.25
COURANT = 0.45


def split_constant(a):
    hi = a.astype(ml_dtypes.bfloat16)
    lo = (a - hi.astype(np.float64)).astype(ml_dtypes.bfloat16)
    return hi, lo


def chunked(a):
    pad = -a.shape[-1] % LANES
    a = np.pad(a, [(0, 0)] * (a.ndim - 1) + [(0, pad)])
    a = a.reshape(*a.shape[:-1], -1, LANES)
    return np.ascontiguousarray(np.moveaxis(a, -2, -3))


def stacked(a):
    hi, lo = split_constant(a)
    return chunked(np.concatenate([hi, hi, lo], axis=1))


@functools.cache
def constants():
    step = 2.0 * np.pi / V
    inner = [(a, b) for a in range(1, HALF) for b in range(1, HALF)]
    outer = [(a, b) for a in range(HALF + 1) for b in range(HALF + 1) if a % HALF == 0 or b % HALF == 0]
    points = np.array(inner + outer)
    count = len(points)
    qy, qz = points[:, 0], points[:, 1]
    natural = np.arange(PLANE)
    ny, nz = natural // V, natural % V
    trig = (np.cos, np.sin)
    classes = ((0, 0), (0, 1), (1, 0), (1, 1))

    def grid(rows_y, rows_z, cy, cz):
        by = trig[cy](step * (rows_y[:, None] * qy[None, :] % V))
        bz = trig[cz](step * (rows_z[:, None] * qz[None, :] % V))
        return by * bz

    plane_forward = np.zeros((PLANE, 4 * W))
    plane_inverse = np.zeros((4, W, W))
    weight = np.where(qy % HALF == 0, 0.5, 1.0) * np.where(qz % HALF == 0, 0.5, 1.0) / PLANE
    for c, (cy, cz) in enumerate(classes):
        plane_forward[:, c * W : c * W + count] = grid(ny, nz, cy, cz)
        plane_inverse[c, :count, :count] = weight[:, None] * grid(qy, qz, cy, cz)

    place = np.zeros((GROUPED, 4 * W))
    unplace = np.zeros((4 * W, PLANE))
    seen = set()
    for s, (sy, sz) in enumerate(SIGNS):
        for q in range(count):
            y, z = sy * qy[q] % V, sz * qz[q] % V
            place[(y // PACK) * LANES + (y % PACK) * V + z, s * W + q] = 1.0
            if (y, z) not in seen:
                seen.add((y, z))
                unplace[s * W + q, y * V + z] = 1.0

    row_of = np.zeros((2, V), dtype=int)
    for jx in range(V):
        pair, odd = jx // 2, jx % 2
        u, q = pair // PAIRS, pair % PAIRS
        for cell in range(2):
            row_of[cell, jx] = odd * V + 2 * PAIRS * u + PAIRS * cell + q
    k = np.arange(V)
    theta = step * (k[:, None] * k[None, :] % V)
    cos, sin = np.cos(theta), np.sin(theta)
    x_forward = np.zeros((2 * V, 2 * V))
    x_forward[:V, row_of[0]] = cos
    x_forward[:V, row_of[1]] = sin
    x_forward[V:, row_of[0]] = -sin
    x_forward[V:, row_of[1]] = cos
    real = np.concatenate([cos, -sin], axis=1)
    imag = np.concatenate([sin, cos], axis=1)
    x_inverse, x_slab = [], [[] for _ in range(GROUPS)]
    for first, second in ((real, imag), (-imag, real), (-imag, real), (-real, -imag)):
        m = np.zeros((2 * V, 2 * V))
        m[row_of[0]] = first
        m[row_of[1]] = second
        m = m / (2 * V)
        x_inverse.append(stacked(m))
        for u in range(GROUPS):
            own = np.zeros((SOME, 2 * V))
            own[:6], own[6:12] = m[6 * u : 6 * u + 6], m[V + 6 * u : V + 6 * u + 6]
            x_slab[u].append(stacked(own))

    reverse = np.zeros((32, 2 * V))
    for r in range(V):
        reverse[r, (V - r) % V] = 1.0
        reverse[r, V + (V - r) % V] = 1.0

    velocity = np.arange(PLANE * V)
    courant_x = COURANT * np.abs(2 * (velocity // PLANE) - (V - 1)).astype(np.float32) / (V - 1)
    courant_y = COURANT * np.abs(2 * (velocity // V % V) - (V - 1)).astype(np.float32) / (V - 1)
    courants = np.zeros((GROUPS, 2, EDGE, LANES), np.float32)
    courants[:, 0, :ROWS] = courant_x.reshape(GROUPS, ROWS, LANES)
    courants[:, 1, :ROWS] = courant_y.reshape(GROUPS, ROWS, LANES)

    return {
        "x_forward": stacked(x_forward),
        "x_inverse": np.stack(x_inverse),
        "x_slab": np.stack([np.stack(a) for a in x_slab]),
        "plane_forward": chunked(np.stack(split_constant(plane_forward))),
        "plane_inverse": chunked(np.stack(split_constant(plane_inverse))),
        "place": chunked(place.astype(ml_dtypes.bfloat16)),
        "unplace": chunked(unplace.astype(ml_dtypes.bfloat16)),
        "reverse": reverse.astype(ml_dtypes.bfloat16),
        "courants": courants,
    }


NAMES = ("x_forward", "x_inverse", "plane_forward", "plane_inverse", "place", "unplace", "reverse", "x_slab", "courants")


def halves(a):
    hi = a.astype(BF16)
    lo = (a - hi.astype(F32)).astype(BF16)
    return hi, lo


def wide(ref, start, count, width=None):
    a = jnp.concatenate([ref[start + i] for i in range(count)], axis=1)
    return a if width is None else a[:, :width]


def dot(a, b):
    return jnp.dot(a, b, preferred_element_type=F32)


def quadrants(a, b, c, d):
    p, m = a + b, a - b
    q, r = c + d, c - d
    return p + q, m + r, p - q, m - r


def kernel(
    sizes,
    dist_hbm, kinds_hbm, wall_hbm, inflow_hbm, side_hbm, left_hbm, right_hbm, loss_hbm,
    xf_hbm, xi_hbm, pf_hbm, pi_hbm, place_hbm, unplace_hbm, reverse_hbm, xs_hbm, courants_hbm,
    out_ref,
    dist, dense, kinds, wall, inflow, side, raw, xf, xi, pf, pi, place, unplace, reverse, xs, courants,
    sides, packed, quads, table, send, recv, field, shaped_hi, shaped_lo, planes, collided, back, own, from_y, from_x, edge, far_raw, far_done,
    local_sem, send1, recv1, send_own, recv_own, send_y, recv_y, send_x, recv_x, send_raw, recv_raw, ready,
):
    n_gx, n_gy = sizes
    gx, gy, me = lax.axis_index("gx"), lax.axis_index("gy"), lax.axis_index("vert")
    my_y, my_h = lax.rem(me, 2), me // 2
    step_y, step_x = 2 * my_y - 1, 2 * my_h - 1
    to_y, to_x = gy + step_y, gx + step_x
    has_y = jnp.logical_and(to_y >= 0, to_y < n_gy)
    core = lax.rem(gx, 2)
    early = lax.rem(gx // 2, 2) == 0
    near_x, far_x = gx + 1 - 2 * core, gx - 1 + 2 * core
    has_far = jnp.logical_and(far_x >= 0, far_x < n_gx)
    sends_far = my_h == core
    early_far = jnp.logical_and(has_far, early)
    late_far = jnp.logical_and(has_far, jnp.logical_not(early))

    barrier = pltpu.get_barrier_semaphore()

    def greet(x, y, v):
        pl.semaphore_signal(barrier, inc=1, device_id=(x, y, v), device_id_type=MESH)

    @pl.when(early_far)
    def _():
        for v in range(GROUPS):
            greet(far_x, gy, v)

    for step in (-1, 1):
        @pl.when(jnp.logical_and(gy + step >= 0, gy + step < n_gy))
        def _(step=step):
            for h in range(2):
                greet(gx, gy + step, 2 * h + (1 if step < 0 else 0))

    for y in range(2):
        greet(near_x, gy, y + 2 * core)
    for d in OTHERS:
        greet(gx, gy, lax.rem(me + d, GROUPS))

    at_gain = RANK * V * PLANE // V
    pulls = [
        (dist_hbm, dist), (wall_hbm, wall), (inflow_hbm, inflow),
        (left_hbm, raw.at[pl.ds(0, at_gain)]), (right_hbm, raw.at[pl.ds(at_gain, at_gain)]),
        (loss_hbm, raw.at[pl.ds(2 * at_gain, PLANE)]), (place_hbm, place), (reverse_hbm, reverse),
        (xf_hbm, xf), (pf_hbm, pf), (xi_hbm, xi), (pi_hbm, pi), (unplace_hbm, unplace), (side_hbm, side),
        (courants_hbm.at[me], courants), (xs_hbm.at[me], xs), (kinds_hbm, kinds),
    ]
    pulls = [pltpu.make_async_copy(a, b, local_sem.at[i]) for i, (a, b) in enumerate(pulls)]
    for i in (0, 16, 1, 2, *range(3, 16)):
        pulls[i].start()

    @pl.when(jnp.logical_not(late_far))
    def _():
        from_x[core] = jnp.zeros((2, EDGE, LANES), F32)

    for k in range(2):
        @pl.when(gy == k * (n_gy - 1))
        def _(k=k):
            from_y[k] = jnp.zeros((2, BLOCK, LANES), F32)

    for i in (0, 1, 2, 16):
        pulls[i].wait()
    for x in range(NX):
        for r in range(ROWS):
            at = (x * ROWS + r) * NY
            dense[at : at + NY, :] = dist[x, :, r * LANES : (r + 1) * LANES]
    for v in range(GROUPS):
        y, h = v % 2, v // 2
        send[v, pl.ds(48, 8)] = jnp.zeros((8, LANES), F32)
        for cell in range(2):
            x = 3 * h + (1 - 2 * h) * cell
            kind = jnp.broadcast_to(kinds[y : y + 1, x : x + 1], (ROWS, LANES))
            own_state = dense[pl.ds(x * 2 * ROWS + y, ROWS, stride=2), :]
            state = jnp.where(kind == 1, wall[...], jnp.where(kind == 2, inflow[...], own_state))
            send[v, pl.ds(cell * ROWS, ROWS)] = state
    recv[me] = send[me]
    for y in range(NY):
        edge[pl.ds(y * ROWS, ROWS)] = send[2 * core + y, pl.ds(0, ROWS)]
    edge[pl.ds(2 * ROWS, BLOCK - 2 * ROWS)] = jnp.zeros((BLOCK - 2 * ROWS, LANES), F32)

    awaited = GROUPS - 1 + jnp.where(has_y, GROUPS, 0) + jnp.where(sends_far, 0, GROUPS)
    pl.semaphore_wait(barrier, awaited + jnp.where(late_far, GROUPS, 0))

    receiver = jnp.where(early, core, 1 - core)
    every = jnp.logical_or(gy == n_gy // 8, jnp.logical_and(gy < n_gy // 8, receiver == 1))

    def push_raw(d):
        return pltpu.make_async_remote_copy(
            src_ref=edge, dst_ref=far_raw.at[me], send_sem=send_raw.at[d], recv_sem=recv_raw.at[me],
            device_id=(far_x, gy, lax.rem(me + d, GROUPS)), device_id_type=MESH,
        )

    def at_others(wanted, act):
        @pl.when(wanted)
        def _():
            for d in OTHERS:
                act(d)

    shared = jnp.logical_not(every)

    @pl.when(late_far)
    def _():
        push_raw(0).start()
        at_others(every, lambda d: push_raw(d).start())

    first = []
    for d in OTHERS:
        to = lax.rem(me + d, GROUPS)
        first.append(
            pltpu.make_async_remote_copy(
                src_ref=send.at[to], dst_ref=recv.at[me], send_sem=send1.at[d], recv_sem=recv1.at[d],
                device_id=(gx, gy, to), device_id_type=MESH,
            )
        )
        first[-1].start()

    @pl.when(late_far)
    def _():
        for y in range(2):
            pl.semaphore_signal(
                ready, inc=1, device_id=(far_x, gy, y + 2 * (1 - core)), device_id_type=MESH
            )

    for i in range(3, 8):
        pulls[i].wait()
    packed[...] = jnp.zeros_like(packed)
    for ky in range(V):
        at = (ky // PACK) * LANES + (ky % PACK) * V
        packed[:, at : at + V] = raw[pl.ds(ky, TABLES * V, stride=V), :]
    hi, lo = halves(packed[...])
    both = jnp.concatenate([hi, lo], axis=0)
    for s in range(4):
        q = dot(both, wide(place, 2 * s, 2))
        quads[s] = q[: TABLES * V] + q[TABLES * V :]

    def symmetrise(t, _):
        at = pl.ds(pl.multiple_of(t * V, 8), V)
        for s in range(4):
            hi, lo = halves(quads[3 - s, at])
            mirrored = dot(reverse[...], jnp.concatenate([hi, lo], axis=0))[:V]
            table[s, at] = quads[s, at] + mirrored
        return 0

    lax.fori_loop(0, TABLES, symmetrise, 0)

    pulls[13].wait()
    for r in range(ROWS):
        for k in range(2):
            sides[k, r : r + 1, :] = side[k : k + 1, r * LANES : (r + 1) * LANES]

    for i in range(8, 13):
        pulls[i].wait()
    for d in range(1, GROUPS):
        first[d - 1].wait_recv()

    def gather_cells(blocks):
        for u in range(GROUPS):
            for c in range(CHUNKS):
                field[6 * u : 6 * u + 6, c * LANES : (c + 1) * LANES] = blocks[u, pl.ds(c, 6, stride=CHUNKS), :]
        return jnp.concatenate([field[:, :PLANE], field[:, PLANE:]], axis=0)

    def forward(cells):
        hi, lo = halves(cells)
        along_x = dot(wide(xf, 0, 2, 6 * V), jnp.concatenate([hi, lo, hi], axis=0))
        hi, lo = halves(along_x)
        both = jnp.concatenate([hi, lo], axis=0)
        parts = []
        for c in range(4):
            top = dot(both, wide(pf.at[0], 2 * c, 2))
            parts.append(top[: 2 * V] + top[2 * V :] + dot(hi, wide(pf.at[1], 2 * c, 2)))
        cc, cs, sc, ss = parts
        swapped = lambda a: jnp.concatenate([a[V:], -a[:V]], axis=0)
        return quadrants(cc, swapped(cs), swapped(sc), -ss)

    def collide(cells, spectrum, along_x, rows):
        lanes = (W, W, W, LANES)
        for t in range(TABLES):
            at = slice(t * V, (t + 1) * V)
            a = []
            for s in range(4):
                m = table[s, at]
                a.append(jnp.concatenate([spectrum[s][:V] * m, spectrum[s][V:] * m], axis=0))
            for c, b in enumerate(quadrants_to_classes(*a)):
                hi, lo = halves(b[:, : lanes[c]])
                z = dot(wide(along_x.at[c], 0, 2, 6 * V), jnp.concatenate([hi, lo, hi], axis=0))
                hi, lo = halves(z)
                shaped_hi[c, t * rows : (t + 1) * rows, : lanes[c]] = hi
                shaped_lo[c, t * rows : (t + 1) * rows, : lanes[c]] = lo
        used = slice(0, TABLES * rows)
        for c in range(4):
            n = lanes[c]
            top, low = (wide(pi.at[k, c, :, pl.ds(0, n)], 0, n // LANES) for k in range(2))
            hi, lo = shaped_hi[c, used, :n], shaped_lo[c, used, :n]
            planes[c, used, :n] = dot(hi, top) + dot(lo, top) + dot(hi, low)

        def fields(t):
            at = slice(t * rows, (t + 1) * rows)
            parts = [planes[c, at, : lanes[c]] for c in range(4)]
            parts[3] = jnp.concatenate([parts[3], jnp.zeros((rows, W - LANES), F32)], axis=1)
            return quadrants(*parts)

        gain = [0.0] * 4
        for r in range(RANK):
            gain = [g + a * b for g, a, b in zip(gain, fields(r), fields(RANK + r))]
        rates = jnp.concatenate(
            [jnp.concatenate(list(gain), axis=1), jnp.concatenate(list(fields(2 * RANK)), axis=1)], axis=0
        )
        hi, lo = halves(rates)
        rates = dot(jnp.concatenate([hi, lo], axis=0), wide(unplace, 0, 5, PLANE))
        rates = rates[: 2 * rows] + rates[2 * rows :]
        return cells + COLLISION_STEP * (rates[:rows] - cells * rates[rows:])

    cells = gather_cells(recv)
    result = collide(cells, forward(cells), xi, 2 * V)
    collided[:, :PLANE] = result[:V]
    collided[:, PLANE:] = result[V:]
    for u in range(GROUPS):
        back[u, pl.ds(48, 8)] = jnp.zeros((8, LANES), F32)
        for c in range(CHUNKS):
            back[u, pl.ds(c, 6, stride=CHUNKS), :] = collided[6 * u : 6 * u + 6, c * LANES : (c + 1) * LANES]

    def push_x(u):
        return pltpu.make_async_remote_copy(
            src_ref=back.at[u, pl.ds(0, EDGE)], dst_ref=from_x.at[1 - my_h, my_y],
            send_sem=send_x.at[u], recv_sem=recv_x.at[1 - my_h, my_y],
            device_id=(to_x, gy, u), device_id_type=MESH,
        )

    def push_y(u):
        return pltpu.make_async_remote_copy(
            src_ref=back.at[u], dst_ref=from_y.at[1 - my_y, my_h],
            send_sem=send_y.at[u], recv_sem=recv_y.at[1 - my_y, my_h],
            device_id=(gx, to_y, u), device_id_type=MESH,
        )

    def push_own(d):
        to = lax.rem(me + d, GROUPS)
        return pltpu.make_async_remote_copy(
            src_ref=back.at[to], dst_ref=own.at[me], send_sem=send_own.at[d], recv_sem=recv_own.at[d],
            device_id=(gx, gy, to), device_id_type=MESH,
        )

    @pl.when(jnp.logical_not(sends_far))
    def _():
        for u in range(GROUPS):
            push_x(u).start()

    @pl.when(has_y)
    def _():
        for u in range(GROUPS):
            push_y(u).start()

    for d in OTHERS:
        push_own(d).start()
    own[me] = back[me]

    def push_far():
        pl.semaphore_wait(ready, GROUPS)
        for u in range(GROUPS):
            push_x(u).start()

    @pl.when(jnp.logical_and(early_far, sends_far))
    def _():
        push_far()

    def share_raw(d):
        return pltpu.make_async_remote_copy(
            src_ref=far_raw.at[me], dst_ref=far_raw.at[me], send_sem=send_raw.at[d], recv_sem=recv_raw.at[me],
            device_id=(gx, gy, lax.rem(me + d, GROUPS)), device_id_type=MESH,
        )

    @pl.when(early_far)
    def _():
        push_raw(0).wait_recv()
        at_others(shared, lambda d: share_raw(d).start())

    pulls[14].wait()
    for d in range(1, GROUPS):
        push_own(d).wait_recv()
    for step in (-1, 1):
        k = 0 if step < 0 else 1

        @pl.when(jnp.logical_and(gy + step >= 0, gy + step < n_gy))
        def _(k=k):
            for h in range(2):
                pltpu.make_async_remote_copy(
                    src_ref=back.at[0], dst_ref=from_y.at[k, h], send_sem=send_y.at[0], recv_sem=recv_y.at[k, h],
                    device_id=(gx, to_y, me), device_id_type=MESH,
                ).wait_recv()

    def wait_x(k):
        for y in range(2):
            pltpu.make_async_remote_copy(
                src_ref=back.at[0, pl.ds(0, EDGE)], dst_ref=from_x.at[k, y], send_sem=send_x.at[0],
                recv_sem=recv_x.at[k, y], device_id=(near_x, gy, me), device_id_type=MESH,
            ).wait_recv()

    wait_x(1 - core)

    @pl.when(late_far)
    def _():
        wait_x(core)

    def at_cell(ref, x):
        cell = (0, 1, 1, 0)[x]
        return ref[pl.ds(cell * ROWS, ROWS), :]

    courant_x, courant_y = courants[0, pl.ds(0, ROWS)], courants[1, pl.ds(0, ROWS)]
    higher_x, higher_y = sides[0] == 1, sides[1] == 1
    centre = {(x, y): at_cell(own.at[y + 2 * (x // 2)], x) for x in range(NX) for y in range(NY)}
    for x in range(NX):
        for y in range(NY):
            here = centre[x, y]
            below_x = centre[x - 1, y] if x > 0 else from_x[0, y, pl.ds(0, ROWS)]
            above_x = centre[x + 1, y] if x < NX - 1 else from_x[1, y, pl.ds(0, ROWS)]
            below_y = centre[x, 0] if y > 0 else at_cell(from_y.at[0, x // 2], x)
            above_y = centre[x, 1] if y < 1 else at_cell(from_y.at[1, x // 2], x)
            up_x = jnp.where(higher_x, below_x, above_x)
            up_y = jnp.where(higher_y, below_y, above_y)
            out_ref[pl.ds(x * 2 * ROWS + y, ROWS, stride=2), :] = (
                here - courant_x * (here - up_x) - courant_y * (here - up_y)
            )

    for d in range(1, GROUPS):
        first[d - 1].wait_send()
        push_own(d).wait_send()

    @pl.when(has_y)
    def _():
        for u in range(GROUPS):
            push_y(u).wait_send()

    @pl.when(jnp.logical_or(jnp.logical_not(sends_far), early_far))
    def _():
        for u in range(GROUPS):
            push_x(u).wait_send()

    @pl.when(late_far)
    def _():
        push_raw(0).wait_send()
        at_others(every, lambda d: push_raw(d).wait_send())

    pulls[15].wait()

    @pl.when(early_far)
    def _():
        for d in range(1, GROUPS):
            peer = lax.rem(me + d, GROUPS)
            pltpu.make_async_remote_copy(
                src_ref=edge, dst_ref=far_raw.at[peer], send_sem=send_raw.at[d], recv_sem=recv_raw.at[peer],
                device_id=(gx, gy, peer), device_id_type=MESH,
            ).wait_recv()
        at_others(shared, lambda d: share_raw(d).wait_send())
        spectrum = forward(gather_cells(far_raw))
        for c in range(CHUNKS):
            collided[:6, c * LANES : (c + 1) * LANES] = far_raw[me, pl.ds(c, 6, stride=CHUNKS), :]
        far = jnp.concatenate([collided[:6, :PLANE], collided[:6, PLANE:], jnp.zeros((SOME - 12, PLANE), F32)], axis=0)
        far = collide(far, spectrum, xs, SOME)
        collided[:6, :PLANE] = far[:6]
        collided[:6, PLANE:] = far[6:12]
        for c in range(CHUNKS):
            far_done[pl.ds(c, 6, stride=CHUNKS), :] = collided[:6, c * LANES : (c + 1) * LANES]
        x = (NX - 1) * core
        for y in range(NY):
            at = pl.ds(x * NY * ROWS + y, ROWS, stride=NY)
            inward = courant_x * far_done[pl.ds(y * ROWS, ROWS)]
            out_ref[at, :] = out_ref[at, :] + jnp.where(sides[0] == 1 - core, inward, 0.0)


def spread(dense, out_ref):
    for x in range(NX):
        for r in range(ROWS):
            at = (x * ROWS + r) * NY
            out_ref[x, :, r * LANES : (r + 1) * LANES] = dense[at : at + NY, :]


def quadrants_to_classes(pp, pm, mp, mm):
    a, b = pp + pm, pp - pm
    c, d = mp + mm, mp - mm
    return a + c, b + d, a - c, b - d


def on_device(sizes, distribution, cell_types, wall_state, inflow_state, upwind_side, gain_left, gain_right, loss_table):
    tables = constants()
    tables = [jnp.asarray(tables[name]) for name in NAMES]
    operands = [
        distribution,
        cell_types.T,
        wall_state.reshape(ROWS, LANES),
        inflow_state.reshape(ROWS, LANES),
        upwind_side,
        gain_left.reshape(RANK * PLANE, V),
        gain_right.reshape(RANK * PLANE, V),
        loss_table.reshape(PLANE, V),
        *tables,
    ]
    spaces = [pl.BlockSpec(memory_space=pl.ANY)] * len(operands)
    dma = pltpu.SemaphoreType.DMA
    held = [
        pltpu.VMEM((NX, NY, SLAB), F32),
        pltpu.VMEM((NX * NY * ROWS, LANES), F32),
        pltpu.VMEM((NY, NX), jnp.int32),
        pltpu.VMEM((ROWS, LANES), F32),
        pltpu.VMEM((ROWS, LANES), F32),
        pltpu.VMEM((2, SLAB), jnp.int32),
        pltpu.VMEM((TABLES * PLANE, V), F32),
        *(pltpu.VMEM(t.shape, t.dtype) for t in tables[:-2]),
        *(pltpu.VMEM(t.shape[1:], t.dtype) for t in tables[-2:]),
        pltpu.VMEM((2, ROWS, LANES), jnp.int32),
        pltpu.VMEM((TABLES * V, GROUPED), F32),
        pltpu.VMEM((4, TABLES * V, W), F32),
        pltpu.VMEM((4, TABLES * V, W), F32),
        pltpu.VMEM((GROUPS, BLOCK, LANES), F32),
        pltpu.VMEM((GROUPS, BLOCK, LANES), F32),
        pltpu.VMEM((V, 2 * PLANE), F32),
        pltpu.VMEM((4, TABLES * 2 * V, W), BF16),
        pltpu.VMEM((4, TABLES * 2 * V, W), BF16),
        pltpu.VMEM((4, TABLES * 2 * V, W), F32),
        pltpu.VMEM((V, 2 * PLANE), F32),
        pltpu.VMEM((GROUPS, BLOCK, LANES), F32),
        pltpu.VMEM((GROUPS, BLOCK, LANES), F32),
        pltpu.VMEM((2, 2, BLOCK, LANES), F32),
        pltpu.VMEM((2, 2, EDGE, LANES), F32),
        pltpu.VMEM((BLOCK, LANES), F32),
        pltpu.VMEM((GROUPS, BLOCK, LANES), F32),
        pltpu.VMEM((BLOCK, LANES), F32),
        dma((17,)),
        dma((GROUPS,)), dma((GROUPS,)),
        dma((GROUPS,)), dma((GROUPS,)),
        dma((GROUPS,)), dma((2, 2)),
        dma((GROUPS,)), dma((2, 2)),
        dma((GROUPS,)), dma((GROUPS,)),
        pltpu.SemaphoreType.REGULAR,
    ]
    dense = pl.pallas_call(
        functools.partial(kernel, sizes),
        out_shape=pltpu.VMEM((NX * NY * ROWS, LANES), F32),
        in_specs=spaces,
        out_specs=pl.BlockSpec(memory_space=pltpu.VMEM),
        scratch_shapes=held,
        compiler_params=pltpu.CompilerParams(
            collective_id=0, has_side_effects=True, vmem_limit_bytes=60 * 1024 * 1024
        ),
        cost_estimate=pl.CostEstimate(flops=3_000_000_000, bytes_accessed=10_000_000, transcendentals=0),
        name="step",
    )(*operands)
    return pl.pallas_call(
        spread,
        out_shape=jax.ShapeDtypeStruct((NX, NY, SLAB), F32),
        in_specs=[pl.BlockSpec(memory_space=pltpu.VMEM)],
        out_specs=pl.BlockSpec(memory_space=pltpu.VMEM),
        name="spread",
    )(pltpu.with_memory_space_constraint(dense, pltpu.VMEM))


def solution(mesh):
    placed = (
        P("gx", "gy", "vert"),
        P("gx", "gy"),
        P("vert"),
        P("vert"),
        P(None, "vert"),
        P(),
        P(),
        P(),
    )
    sizes = (mesh.shape["gx"], mesh.shape["gy"])
    return jax.shard_map(
        functools.partial(on_device, sizes),
        mesh=mesh,
        in_specs=placed,
        out_specs=P("gx", "gy", "vert"),
        check_vma=False,
    )
```
